32 devices in a mesh: dp: 8 (over y, x, core), tensor: 4 (over z).
Axes of the slice: x: 2, y: 2, z: 4, core: 2. Of those that a mesh axis runs over, the one named last changes fastest.
Arguments:
- inputs: bfloat16 [16384, 1024], P('dp'), may hold values from -6 to 6
- cotangent: bfloat16 [16384, 1024], P(('dp', 'tensor')), may hold values from -6 to 6
- lengths: int32 [16], P('dp'), may hold values from 256 to 1024, as said below
- query_weight: bfloat16 [1024, 1024], P(None, 'tensor'), may hold values from -0.1875 to 0.1875
- key_weight: bfloat16 [1024, 1024], P(None, 'tensor'), may hold values from -0.1875 to 0.1875
- value_weight: bfloat16 [1024, 1024], P(None, 'tensor'), may hold values from -0.1875 to 0.1875
- query_bias: float32 [1024], P('tensor'), may hold values from -3 to 3
- value_bias: float32 [1024], P('tensor'), may hold values from -3 to 3
- out_weight: bfloat16 [1024, 1024], P('tensor'), may hold values from -1 to 1
- out_bias: float32 [1024], replicated, may hold values from -3 to 3
- norm1_gain: float32 [1024], replicated, may hold values from 0.5 to 1.5
- norm1_bias: float32 [1024], replicated, may hold values from -2 to 2
- up_weight: bfloat16 [1024, 4096], P(None, 'tensor'), may hold values from -0.1875 to 0.1875
- up_bias: float32 [4096], P('tensor'), may hold values from -3 to 3
- down_weight: bfloat16 [4096, 1024], P('tensor'), may hold values from -0.09375 to 0.09375
- down_bias: float32 [1024], replicated, may hold values from -3 to 3
- norm2_gain: float32 [1024], replicated, may hold values from 0.5 to 1.5
- norm2_bias: float32 [1024], replicated, may hold values from -2 to 2
Outputs:
- outputs: bfloat16 [16384, 1024], P(('dp', 'tensor'))
- input_grad: float32 [16384, 1024], P(('dp', 'tensor'))
- query_weight_grad: float32 [1024, 1024], P(None, 'tensor')
- key_weight_grad: float32 [1024, 1024], P(None, 'tensor')
- value_weight_grad: float32 [1024, 1024], P(None, 'tensor')
- query_bias_grad: float32 [1024], P('tensor')
- value_bias_grad: float32 [1024], P('tensor')
- out_weight_grad: float32 [1024, 1024], P('tensor')
- out_bias_grad: float32 [1024], replicated
- norm1_gain_grad: float32 [1024], replicated
- norm1_bias_grad: float32 [1024], replicated
- up_weight_grad: float32 [1024, 4096], P(None, 'tensor')
- up_bias_grad: float32 [4096], P('tensor')
- down_weight_grad: float32 [4096, 1024], P('tensor')
- down_bias_grad: float32 [1024], replicated
- norm2_gain_grad: float32 [1024], replicated
- norm2_bias_grad: float32 [1024], replicated
The draws below stay inside these ranges and needn't reach their ends.
Inputs may be any that keep to these rules, and one draw needn't show every extreme that they name: `lengths`: among the 2 sequences of each index of dp one has length 1024.
All inputs are finite; a program needn't handle non-finite values.
Results may differ from the reference program's by a relative error of at most 0.023.
Values may be sent and summed in bfloat16 or wider, within the bound.
A program may use at most 128 MiB of HBM per device.

```python
import jax
import jax.numpy as jnp
from jax import lax

D = 1024
HEADS = 16
HD = 64
FF = 4096
LEN = 1024
SEQ_DEV = 2
SEQS = 16
TOKENS = 16384
N_TENSOR = 4


def draw_lengths(key, part):
    base = jax.random.randint(key, (SEQS,), LEN // 4, LEN + 1)
    chosen = jax.random.randint(jax.random.fold_in(key, 7), (SEQS // SEQ_DEV, 1), 0, SEQ_DEV)
    full = (jnp.arange(SEQ_DEV)[None, :] == chosen).reshape(SEQS)
    return jnp.where(full, LEN, base).astype(jnp.int32)


def shard_levels(key, extent, split, least, top_value):
    factor_of = 1.0
    for dim, shards_of in split:
        steps = jax.random.uniform(jax.random.fold_in(jax.random.fold_in(key, 6), dim), (shards_of,), jnp.float32, least / len(split), top_value / len(split))
        factor_of = factor_of * jnp.repeat(jnp.exp(steps), extent[dim] // shards_of).reshape((-1,) + (1,) * (len(extent) - 1 - dim))
    return factor_of


def normal_values(rng, extent, scale, most, split=(), held_as=jnp.bfloat16):
    level = shard_levels(rng, extent, split, -0.22, 0.18) if split else 1.0
    result = jax.random.normal(rng, extent, jnp.float32) * scale * level
    return jnp.minimum(jnp.maximum(result, -most), most).astype(held_as)


def setup_inputs(seed: int = 0) -> dict:
    streams_of = jax.random.split(jax.random.key(seed), 19)
    inputs = normal_values(streams_of[0], (TOKENS, D), 1.0, 6.0, ((0, 8),))
    cotangent = normal_values(streams_of[1], (TOKENS, D), 1.0, 6.0, ((0, 32),))
    lengths = draw_lengths(jax.random.fold_in(streams_of[18], 71), 0)
    query_weight = normal_values(streams_of[3], (D, D), D ** -0.5, 0.1875, ((1, 4),))
    key_weight = normal_values(streams_of[4], (D, D), D ** -0.5, 0.1875, ((1, 4),))
    value_weight = normal_values(streams_of[5], (D, D), D ** -0.5, 0.1875, ((1, 4),))
    query_bias = normal_values(streams_of[6], (D,), 0.5, 3.0, ((0, 4),), jnp.float32)
    value_bias = normal_values(streams_of[7], (D,), 0.5, 3.0, ((0, 4),), jnp.float32)
    out_weight = normal_values(streams_of[8], (D, D), (D // 32) ** -0.5, 1.0, ((0, 4),))
    out_bias = normal_values(streams_of[9], (D,), 0.5, 3.0, (), jnp.float32)
    norm1_gain = jnp.clip(1.0 + 0.1 * jax.random.normal(streams_of[10], (D,), jnp.float32), 0.5, 1.5)
    norm1_bias = normal_values(streams_of[11], (D,), 0.3, 2.0, (), jnp.float32)
    up_weight = normal_values(streams_of[12], (D, FF), D ** -0.5, 0.1875, ((1, 4),))
    up_bias = normal_values(streams_of[13], (FF,), 0.5, 3.0, ((0, 4),), jnp.float32)
    down_weight = normal_values(streams_of[14], (FF, D), FF ** -0.5, 0.09375, ((0, 4),))
    down_bias = normal_values(streams_of[15], (D,), 0.5, 3.0, (), jnp.float32)
    norm2_gain = jnp.clip(1.0 + 0.1 * jax.random.normal(streams_of[16], (D,), jnp.float32), 0.5, 1.5)
    norm2_bias = normal_values(streams_of[17], (D,), 0.3, 2.0, (), jnp.float32)
    return dict(inputs=inputs, cotangent=cotangent, lengths=lengths, query_weight=query_weight, key_weight=key_weight, value_weight=value_weight, query_bias=query_bias, value_bias=value_bias, out_weight=out_weight, out_bias=out_bias, norm1_gain=norm1_gain, norm1_bias=norm1_bias, up_weight=up_weight, up_bias=up_bias, down_weight=down_weight, down_bias=down_bias, norm2_gain=norm2_gain, norm2_bias=norm2_bias)


@jax.custom_vjp
def low(v):
    return lax.optimization_barrier(v.astype(jnp.bfloat16)).astype(jnp.float32)

@jax.custom_vjp
def low_back(v):
    return v

def low_keep(v):
    return (low(v), None)

def low_pass(kept, grad):
    return (grad,)

def back_keep(v):
    return (v, None)

def back_low(kept, grad):
    return (low(grad),)
low.defvjp(low_keep, low_pass)
low_back.defvjp(back_keep, back_low)

def matmul(left, right):
    return jnp.dot(left, right, precision=lax.Precision.HIGHEST)

def grouped_product(left, right):
    inner = left.shape[1]
    left_groups = left.reshape(left.shape[0], N_TENSOR, inner // N_TENSOR)
    right_groups = right.reshape(N_TENSOR, inner // N_TENSOR, right.shape[1])
    partials = low(jnp.einsum('rgi,gio->rgo', left_groups, right_groups, precision=lax.Precision.HIGHEST))
    return lax.optimization_barrier(jnp.sum(partials, axis=1))

def layer_norm(values, gain, bias):
    center = values - lax.optimization_barrier(jnp.mean(values, axis=-1, keepdims=True))
    spread = lax.optimization_barrier(jnp.mean(center * center, axis=-1, keepdims=True))
    return center * lax.rsqrt(spread + 1e-05) * gain + bias

def encoder_layer(seq_inputs, params, length):
    query_weight, key_weight, value_weight, query_bias, value_bias, out_weight, out_bias, norm1_gain, norm1_bias, up_weight, up_bias, down_weight, down_bias, norm2_gain, norm2_bias = params
    queries = low(low_back(matmul(seq_inputs, query_weight) + query_bias)).reshape(LEN, HEADS, HD)
    keys = low(low_back(matmul(seq_inputs, key_weight))).reshape(LEN, HEADS, HD)
    values = low(low_back(matmul(seq_inputs, value_weight) + value_bias)).reshape(LEN, HEADS, HD)
    raw = low_back(jnp.einsum('qhd,khd->hqk', queries, keys, precision=lax.Precision.HIGHEST))
    scores = raw * HD ** (-0.5)
    key_valid = jnp.arange(LEN) < length
    scores = jnp.where(key_valid[None, None, :], scores, -1e+30)
    row_max = lax.optimization_barrier(jnp.max(scores, axis=-1, keepdims=True))
    exponent = jnp.exp(scores - row_max)
    probs = exponent / lax.optimization_barrier(jnp.sum(exponent, axis=-1, keepdims=True))
    attended = jnp.einsum('hqk,khd->qhd', low(probs), values, precision=lax.Precision.HIGHEST).reshape(LEN, D)
    attended = low(low_back(attended))
    first = seq_inputs + low_back(grouped_product(attended, out_weight)) + out_bias
    normed1 = layer_norm(first, norm1_gain, norm1_bias)
    hidden = low(normed1)
    upper = low_back(matmul(hidden, up_weight) + up_bias)
    active = low(jax.nn.gelu(upper, approximate=False))
    second = normed1 + low_back(grouped_product(active, down_weight)) + down_bias
    return layer_norm(second, norm2_gain, norm2_bias)

def reference(inputs, cotangent, lengths, query_weight, key_weight, value_weight, query_bias, value_bias, out_weight, out_bias, norm1_gain, norm1_bias, up_weight, up_bias, down_weight, down_bias, norm2_gain, norm2_bias):
    params = tuple((p.astype(jnp.float32) for p in (query_weight, key_weight, value_weight, query_bias, value_bias, out_weight, out_bias, norm1_gain, norm1_bias, up_weight, up_bias, down_weight, down_bias, norm2_gain, norm2_bias)))
    seq_all = inputs.astype(jnp.float32).reshape(SEQS, LEN, D)
    cot_all = cotangent.astype(jnp.float32).reshape(SEQS, LEN, D)

    def step(totals, sequence_item):
        seq_inputs, seq_cot, length = sequence_item
        row_valid = (jnp.arange(LEN) < length).astype(jnp.float32)
        seq_out, pull = jax.vjp(lambda xv, pv: encoder_layer(xv, pv, length), seq_inputs, params)
        seq_dx, grads = pull(seq_cot * row_valid[:, None])
        totals = jax.tree.map(lambda a, b: a + b, totals, grads)
        return (totals, (seq_out, seq_dx))
    zeros = jax.tree.map(jnp.zeros_like, params)
    totals, (seq_outs, seq_dxs) = lax.scan(step, zeros, (seq_all, cot_all, lengths.astype(jnp.int32)))
    return (seq_outs.reshape(TOKENS, D).astype(jnp.bfloat16), seq_dxs.reshape(TOKENS, D), totals[0], totals[1], totals[2], totals[3], totals[4], totals[5], totals[6], totals[7], totals[8], totals[9], totals[10], totals[11], totals[12], totals[13], totals[14])
```

```python
import functools

import jax
import jax.numpy as jnp
from jax import lax
from jax.experimental import pallas as pl
from jax.experimental.pallas import tpu as pltpu
from jax.sharding import PartitionSpec as P

HD = 64
LEN = 1024
PAIR = 2 * HD
F32 = jnp.float32
BF = jnp.bfloat16
NN = (((1,), (0,)), ((), ()))
NT = (((1,), (1,)), ((), ()))
TN = (((0,), (0,)), ((), ()))


def product(left, right, dims=NN):
    return lax.dot_general(left, right, dims, preferred_element_type=F32)


def attend_forward_kernel(
    block,
    len_ref,
    x_ref,
    wq_ref,
    wk_ref,
    wv_ref,
    bq_ref,
    bv_ref,
    q_ref,
    k_ref,
    v_ref,
    o_ref,
    lse_ref,
):
    rows, width = q_ref.shape
    proj_rows = 256

    def project(index, carry):
        at = pl.ds(pl.multiple_of(index * proj_rows, proj_rows), proj_rows)
        x = x_ref[at, :]
        queries = (product(x, wq_ref[...]) + bq_ref[...]).astype(BF)
        q_ref[at, :] = (queries.astype(F32) * HD ** (-0.5)).astype(BF)
        k_ref[at, :] = product(x, wk_ref[...]).astype(BF)
        v_ref[at, :] = (product(x, wv_ref[...]) + bv_ref[...]).astype(BF)
        return carry

    lax.fori_loop(0, rows // proj_rows, project, 0)
    blocks_per_seq = LEN // block

    def attend(index, carry):
        seq = index // blocks_per_seq
        keys_at = pl.ds(pl.multiple_of(seq * LEN, LEN), LEN)
        rows_at = pl.ds(pl.multiple_of(index * block, block), block)
        length = len_ref[seq]
        key_slot = lax.broadcasted_iota(jnp.int32, (LEN, block), 0)
        lane = lax.broadcasted_iota(jnp.int32, (block, PAIR), 1)
        for pair in range(width // PAIR):
            cols = slice(pair * PAIR, (pair + 1) * PAIR)
            keys, values, queries = k_ref[keys_at, cols], v_ref[keys_at, cols], q_ref[rows_at, cols]
            parts = []
            for head in range(2):
                own = jnp.where((lane >= HD) == (head == 1), queries, jnp.zeros_like(queries))
                scores = jnp.where(key_slot < length, product(keys, own, NT), -1e30)
                top = jnp.max(scores, axis=0, keepdims=True)
                exponent = jnp.exp(scores - top)
                total = jnp.sum(exponent, axis=0, keepdims=True)
                mixed = product(values, exponent.astype(BF), TN)
                parts.append(mixed[head * HD : (head + 1) * HD] * (1.0 / total))
                lse_ref[pl.ds(pair * 2 + head, 1), rows_at] = top + jnp.log(total)
            o_ref[rows_at, cols] = jnp.concatenate(parts, axis=0).T.astype(BF)
        return carry

    lax.fori_loop(0, rows // block, attend, 0)


def attend_forward(lengths, x, wq, wk, wv, bq, bv, block):
    rows, width = x.shape[0], wq.shape[1]
    vmem = pl.BlockSpec(memory_space=pltpu.VMEM)
    out = jax.ShapeDtypeStruct((rows, width), BF)
    return pl.pallas_call(
        functools.partial(attend_forward_kernel, block),
        in_specs=[pl.BlockSpec(memory_space=pltpu.SMEM)] + [vmem] * 6,
        out_specs=[vmem] * 5,
        out_shape=[out, out, out, out, jax.ShapeDtypeStruct((8, rows), F32)],
        compiler_params=pltpu.CompilerParams(vmem_limit_bytes=56 << 20),
        cost_estimate=pl.CostEstimate(
            flops=20 * 10**9, bytes_accessed=12 << 20, transcendentals=8 << 20
        ),
        name="attend_forward",
    )(lengths, x, wq, wk, wv, bq.reshape(1, -1), bv.reshape(1, -1))


def attend_backward_kernel(
    block,
    len_ref,
    q_ref,
    k_ref,
    v_ref,
    o_ref,
    do_ref,
    lse_ref,
    dq_ref,
    dk_ref,
    dv_ref,
    key_sum,
    value_sum,
):
    rows, width = q_ref.shape
    blocks_per_seq = LEN // block

    def back(index, carry):
        seq = index // blocks_per_seq
        keys_at = pl.ds(pl.multiple_of(seq * LEN, LEN), LEN)
        rows_at = pl.ds(pl.multiple_of(index * block, block), block)
        length = len_ref[seq]
        key_slot = lax.broadcasted_iota(jnp.int32, (LEN, block), 0)
        lane = lax.broadcasted_iota(jnp.int32, (block, PAIR), 1)
        starts = lax.rem(index, blocks_per_seq) == 0
        for pair in range(width // PAIR):
            cols = slice(pair * PAIR, (pair + 1) * PAIR)
            keys, values, queries = k_ref[keys_at, cols], v_ref[keys_at, cols], q_ref[rows_at, cols]
            d_out = do_ref[rows_at, cols]
            inner_all = (d_out.astype(F32) * o_ref[rows_at, cols].astype(F32)).T
            value_part, key_part, query_parts = None, None, []
            for head in range(2):
                mine = (lane >= HD) == (head == 1)
                own_q = jnp.where(mine, queries, jnp.zeros_like(queries))
                own_d = jnp.where(mine, d_out, jnp.zeros_like(d_out))
                inner = jnp.sum(inner_all[head * HD : (head + 1) * HD], axis=0, keepdims=True)
                scores = jnp.where(key_slot < length, product(keys, own_q, NT), -1e30)
                probs = jnp.exp(scores - lse_ref[pl.ds(pair * 2 + head, 1), rows_at])
                d_probs = product(values, own_d, NT)
                d_scores = (probs * (d_probs - inner) * HD ** (-0.5)).astype(BF)
                d_values = product(probs.astype(BF), own_d)
                d_keys = product(d_scores, own_q)
                value_part = d_values if head == 0 else value_part + d_values
                key_part = d_keys if head == 0 else key_part + d_keys
                query_parts.append(product(keys, d_scores, TN)[head * HD : (head + 1) * HD])
            key_part = key_part * HD**0.5
            dq_ref[rows_at, cols] = jnp.concatenate(query_parts, axis=0).T.astype(BF)

            @pl.when(starts)
            def _():
                key_sum[:, cols] = key_part
                value_sum[:, cols] = value_part

            @pl.when(jnp.logical_not(starts))
            def _():
                key_sum[:, cols] += key_part
                value_sum[:, cols] += value_part

        @pl.when(lax.rem(index, blocks_per_seq) == blocks_per_seq - 1)
        def _():
            dk_ref[keys_at, :] = key_sum[...].astype(BF)
            dv_ref[keys_at, :] = value_sum[...].astype(BF)

        return carry

    lax.fori_loop(0, rows // block, back, 0)


def attend_backward(lengths, q, k, v, o, d_out, lse, block):
    vmem = pl.BlockSpec(memory_space=pltpu.VMEM)
    out = jax.ShapeDtypeStruct(q.shape, BF)
    return pl.pallas_call(
        functools.partial(attend_backward_kernel, block),
        in_specs=[pl.BlockSpec(memory_space=pltpu.SMEM)] + [vmem] * 6,
        out_specs=[vmem] * 3,
        out_shape=[out] * 3,
        scratch_shapes=[pltpu.VMEM((LEN, q.shape[1]), F32)] * 2,
        compiler_params=pltpu.CompilerParams(vmem_limit_bytes=56 << 20),
        cost_estimate=pl.CostEstimate(
            flops=24 * 10**9, bytes_accessed=12 << 20, transcendentals=8 << 20
        ),
        name="attend_backward",
    )(lengths, q, k, v, o, d_out, lse)


def norm_forward(values, gain, bias):
    center = values - jnp.mean(values, axis=-1, keepdims=True)
    inverse = lax.rsqrt(jnp.mean(center * center, axis=-1, keepdims=True) + 1e-05)
    normal = center * inverse
    return (normal * gain + bias, normal, inverse)


def norm_backward(grad, normal, inverse, gain):
    scaled = grad * gain
    first_mean = jnp.mean(scaled, axis=-1, keepdims=True)
    second_mean = jnp.mean(scaled * normal, axis=-1, keepdims=True)
    return (
        inverse * (scaled - first_mean - normal * second_mean),
        jnp.sum(grad * normal, 0),
        jnp.sum(grad, 0),
    )


def exact_gelu(values):
    return jax.nn.gelu(values, approximate=False)


GROUP = 8


def dp_groups():
    size = lax.axis_size("dp")
    return [list(range(first, first + GROUP)) for first in range(0, size, GROUP)]


def gather_weights(packed):
    rows = packed.shape[0]
    own = lax.rem(lax.axis_index("dp"), GROUP)
    piece = lax.dynamic_slice_in_dim(packed, own * (rows // GROUP), rows // GROUP, 0)
    along = lax.all_gather(piece, "tensor", axis=0, tiled=False)
    full = lax.all_gather(along, "dp", axis=1, tiled=False, axis_index_groups=dp_groups())
    return full.reshape(along.shape[0], rows, packed.shape[1])


def reduce_grads(packed):
    tensor_size, rows, cols = packed.shape
    part = lax.psum_scatter(
        packed.reshape(tensor_size, GROUP, rows // GROUP, cols),
        "dp",
        scatter_dimension=1,
        axis_index_groups=dp_groups(),
        tiled=False,
    )
    part = lax.psum_scatter(part, "tensor", scatter_dimension=0, tiled=False)
    full = lax.all_gather(part, "dp", axis=0, tiled=True, axis_index_groups=dp_groups()).astype(F32)
    if lax.axis_size("dp") > GROUP:
        full = lax.psum(
            full,
            "dp",
            axis_index_groups=[
                list(range(first, lax.axis_size("dp"), GROUP)) for first in range(GROUP)
            ],
        )
    return full


def on_device(
    inputs,
    cotangent,
    lengths,
    query_weight,
    key_weight,
    value_weight,
    query_bias,
    value_bias,
    out_weight,
    out_bias,
    norm1_gain,
    norm1_bias,
    up_weight,
    up_bias,
    down_weight,
    down_bias,
    norm2_gain,
    norm2_bias,
):
    tensor_size = lax.axis_size("tensor")
    tensor_pos = lax.axis_index("tensor")
    row_count, model = inputs.shape
    share_rows = row_count // tensor_size
    first_share = tensor_pos * share_rows
    width = out_weight.shape[0]
    hidden_width = down_weight.shape[0]

    packed = jnp.concatenate([out_weight, up_weight, down_weight], axis=0)
    full = gather_weights(packed)
    out_full = full[:, :width].reshape(tensor_size * width, model)
    up_full = full[:, width : width + model]
    down_full = full[:, width + model :]

    queries, keys, values, attended, log_total = attend_forward(
        lengths, inputs, query_weight, key_weight, value_weight, query_bias, value_bias, 512
    )

    def to_rows(split_heads):
        moved = lax.all_to_all(
            split_heads.reshape(tensor_size, share_rows, -1), "tensor", 0, 0, tiled=False
        )
        return moved.transpose(1, 0, 2).reshape(share_rows, -1)

    def to_heads(split_rows):
        moved = split_rows.reshape(share_rows, tensor_size, -1).transpose(1, 0, 2)
        return lax.all_to_all(moved, "tensor", 0, 0, tiled=False).reshape(row_count, -1)

    attended_rows = to_rows(attended)
    input_share = lax.dynamic_slice_in_dim(inputs, first_share, share_rows, 0).astype(F32)
    first = input_share + product(attended_rows, out_full) + out_bias
    normed1, normal1, inverse1 = norm_forward(first, norm1_gain, norm1_bias)
    hidden_low = normed1.astype(BF)
    up_bias_full = lax.all_gather(up_bias, "tensor", axis=0, tiled=False)
    uppers, actives, mlp = [], [], 0.0
    for part in range(tensor_size):
        upper = product(hidden_low, up_full[part]) + up_bias_full[part]
        active = exact_gelu(upper).astype(BF)
        mlp = mlp + product(active, down_full[part])
        uppers.append(upper)
        actives.append(active)
    second = normed1 + mlp + down_bias
    outputs, normal2, inverse2 = norm_forward(second, norm2_gain, norm2_bias)
    row_index = first_share + jnp.arange(share_rows)
    row_length = jnp.sum(
        jnp.where(
            (row_index // LEN)[:, None] == jnp.arange(lengths.shape[0])[None, :],
            lengths[None, :],
            0,
        ),
        1,
    )
    row_valid = (row_index % LEN < row_length).astype(F32)
    grad_out = cotangent.astype(F32) * row_valid[:, None]
    d_second, norm2_gain_part, norm2_bias_part = norm_backward(
        grad_out, normal2, inverse2, norm2_gain
    )
    down_bias_part = jnp.sum(d_second, 0)
    d_second_low = d_second.astype(BF)
    d_normed1 = d_second
    up_grads, down_grads, up_bias_parts = [], [], []
    for part in range(tensor_size):
        down_grads.append(product(actives[part], d_second_low, TN).astype(BF))
        d_active = product(d_second_low, down_full[part], NT)
        d_upper = jax.vjp(exact_gelu, uppers[part])[1](d_active)[0].astype(BF)
        up_grads.append(product(hidden_low, d_upper, TN).astype(BF))
        up_bias_parts.append(jnp.sum(d_upper.astype(F32), 0))
        d_normed1 = d_normed1 + product(d_upper, up_full[part], NT)
    d_first, norm1_gain_part, norm1_bias_part = norm_backward(
        d_normed1, normal1, inverse1, norm1_gain
    )
    out_bias_part = jnp.sum(d_first, 0)
    d_first_low = d_first.astype(BF)
    out_grad = product(attended_rows, d_first_low, TN).astype(BF).reshape(tensor_size, width, model)
    d_attended = to_heads(product(d_first_low, out_full, NT).astype(BF))
    reduced = reduce_grads(
        jnp.concatenate([out_grad, jnp.stack(up_grads), jnp.stack(down_grads)], axis=1)
    )
    d_queries, d_keys, d_values = attend_backward(
        lengths, queries, keys, values, attended, d_attended, log_total, 512
    )
    total = product(d_queries, query_weight, NT)
    total = total + product(d_keys, key_weight, NT) + product(d_values, value_weight, NT)
    input_grad = (
        lax.psum_scatter(total.astype(BF), "tensor", scatter_dimension=0, tiled=True).astype(F32)
        + d_first
    )
    (
        query_weight_grad,
        key_weight_grad,
        value_weight_grad,
        query_bias_grad,
        value_bias_grad,
    ) = lax.psum(
        (
            product(inputs, d_queries, TN),
            product(inputs, d_keys, TN),
            product(inputs, d_values, TN),
            jnp.sum(d_queries.astype(F32), 0),
            jnp.sum(d_values.astype(F32), 0),
        ),
        "dp",
    )
    small = lax.psum(
        jnp.stack(
            [
                norm1_gain_part,
                norm1_bias_part,
                norm2_gain_part,
                norm2_bias_part,
                out_bias_part,
                down_bias_part,
                *up_bias_parts,
            ]
        ),
        ("dp", "tensor"),
    )
    up_bias_grad = lax.dynamic_index_in_dim(small[6:], tensor_pos, 0, keepdims=False)
    return (
        outputs.astype(BF),
        input_grad,
        query_weight_grad,
        key_weight_grad,
        value_weight_grad,
        query_bias_grad,
        value_bias_grad,
        reduced[:width],
        small[4],
        small[0],
        small[1],
        reduced[width : width + model],
        up_bias_grad,
        reduced[width + model :],
        small[5],
        small[2],
        small[3],
    )


def solution(mesh):
    rows = P(("dp", "tensor"), None)
    by_col = P(None, "tensor")
    by_row = P("tensor", None)
    split = P("tensor")
    whole = P()
    return jax.shard_map(
        on_device,
        mesh=mesh,
        in_specs=(
            P("dp", None),
            rows,
            P("dp"),
            by_col,
            by_col,
            by_col,
            split,
            split,
            by_row,
            whole,
            whole,
            whole,
            by_col,
            split,
            by_row,
            whole,
            whole,
            whole,
        ),
        out_specs=(
            rows,
            rows,
            by_col,
            by_col,
            by_col,
            split,
            split,
            by_row,
            whole,
            whole,
            whole,
            by_col,
            split,
            by_row,
            whole,
            whole,
            whole,
        ),
        check_vma=False,
    )
```

```python
import functools

import jax
import jax.numpy as jnp
from jax import lax
from jax.experimental import pallas as pl
from jax.experimental.pallas import tpu as pltpu
from jax.sharding import PartitionSpec as P

HD = 64
LEN = 1024
PAIR = 2 * HD
GROUP = 8
F32 = jnp.float32
BF = jnp.bfloat16
NN = (((1,), (0,)), ((), ()))
NT = (((1,), (1,)), ((), ()))
TN = (((0,), (0,)), ((), ()))
MESH = pl.DeviceIdType.MESH
VMEM_LIMIT = 60 << 20


def product(left, right, dims=NN):
    return lax.dot_general(left, right, dims, preferred_element_type=F32)


def flip(index, bit):
    return index + bit * (1 - 2 * lax.rem(lax.div(index, bit), 2))


def mix(index, step):
    low = lax.rem(index + step, 2)
    high = lax.rem(lax.div(index, 2) + lax.div(step, 2), 2)
    return 2 * high + low


class Place:
    def __init__(self):
        self.dp = lax.axis_index("dp")
        self.t = lax.axis_index("tensor")
        self.e = lax.rem(self.dp, GROUP)
        self.core = lax.rem(self.e, 2)
        self.quad = lax.div(self.e, 2)
        self.to_core = (flip(self.dp, 1), self.t)
        self.to_x = (flip(self.dp, 2), self.t)
        self.to_y = (flip(self.dp, 4), self.t)
        self.quad_x = flip(self.quad, 1)
        self.quad_y = flip(self.quad, 2)
        self.quad_xy = flip(self.quad_x, 2)

    def to_z(self, step):
        return (self.dp, mix(self.t, jnp.int32(step)))

    def greet(self):
        barrier = pltpu.get_barrier_semaphore()
        peers = [self.to_core, self.to_x, self.to_y, self.to_z(1), self.to_z(2), self.to_z(3)]
        for peer in peers:
            pl.semaphore_signal(barrier, inc=1, device_id=peer, device_id_type=MESH)
        pl.semaphore_wait(barrier, len(peers))


def remote(src, dst, send, recv, index, device):
    return pltpu.make_async_remote_copy(
        src_ref=src,
        dst_ref=dst,
        send_sem=send.at[index],
        recv_sem=recv.at[index],
        device_id=device,
        device_id_type=MESH,
    )


class Spread:
    def __init__(self, place, full, sems, index):
        self.p = place
        self.full = full
        self.sems = sems
        self.index = index

    def block(self, step):
        return mix(self.p.t, jnp.int32(step)) if step else self.p.t

    def slot(self, step):
        return self.index * 4 + step

    def x_copy(self, step):
        p = self.p
        ref = self.full.at[self.block(step), p.quad, p.core]
        return remote(ref, ref, self.sems[0], self.sems[1], self.slot(step), p.to_x)

    def y_copy(self, step):
        p = self.p
        ref = self.full.at[self.block(step), p.quad, p.core]
        return remote(ref, ref, self.sems[2], self.sems[3], self.slot(step), p.to_y)

    def half_copies(self, step):
        p = self.p
        half = self.full.shape[3] // 2
        first = self.full.at[self.block(step), p.quad_x, p.core, pl.ds(0, half)]
        second = self.full.at[self.block(step), p.quad_y, p.core, pl.ds(half, half)]
        return (
            remote(first, first, self.sems[4], self.sems[5], self.slot(step), p.to_y),
            remote(second, second, self.sems[6], self.sems[7], self.slot(step), p.to_x),
        )

    def core_copy(self, step):
        p = self.p
        ref = self.full.at[self.block(step), :, p.core]
        return remote(ref, ref, self.sems[8], self.sems[9], self.slot(step), p.to_core)

    def first(self, step):
        self.x_copy(step).start()
        self.y_copy(step).start()

    def second(self, step):
        self.x_copy(step).wait_recv()
        self.y_copy(step).wait_recv()
        for copy in self.half_copies(step):
            copy.start()

    def third(self, step):
        for copy in self.half_copies(step):
            copy.wait_recv()
        self.core_copy(step).start()

    def arrived(self, step):
        self.core_copy(step).wait_recv()

    def finish(self, step):
        self.x_copy(step).wait_send()
        self.y_copy(step).wait_send()
        for copy in self.half_copies(step):
            copy.wait_send()
        self.core_copy(step).wait_send()

    @staticmethod
    def scratch(count):
        return [pltpu.SemaphoreType.DMA((4 * count,))] * 10


def norm_center(values):
    center = values - jnp.mean(values, axis=-1, keepdims=True)
    inverse = lax.rsqrt(jnp.mean(center * center, axis=-1, keepdims=True) + 1e-05)
    return center * inverse, inverse


def norm_back(grad, normal, inverse, gain):
    scaled = grad * gain
    first_mean = jnp.mean(scaled, axis=-1, keepdims=True)
    second_mean = jnp.mean(scaled * normal, axis=-1, keepdims=True)
    return inverse * (scaled - first_mean - normal * second_mean)


def forward_kernel(
    len_ref,
    x_hbm,
    cot_ref,
    vec_ref,
    small_ref,
    wq_hbm,
    wk_hbm,
    wv_hbm,
    wo_hbm,
    wu_hbm,
    wd_hbm,
    qkv_full,
    out_full,
    up_full,
    down_full,
    q_hbm,
    k_hbm,
    v_hbm,
    o_hbm,
    act_hbm,
    slope_hbm,
    outputs_ref,
    d_second_ref,
    normal1_ref,
    inverse1_ref,
    hidden_ref,
    lse_ref,
    sums_ref,
    x_seq,
    small_all,
    w_qkv,
    w_out,
    w_up,
    w_down,
    q_s,
    k_s,
    v_s,
    o_s,
    act_s,
    slope_s,
    acc,
    z_send,
    z_recv,
    small_send,
    small_recv,
    local,
    load,
    save,
    *spread_sems,
):
    p = Place()
    rows, model = acc.shape
    width = q_s.shape[2]
    half_index = lax.rem(p.t, 2)
    seq = lax.div(p.t, 2)
    own_rows = pl.ds(pl.multiple_of(half_index * rows, rows), rows)
    fulls = [qkv_full, out_full, up_full, down_full]
    spreads = [Spread(p, full, spread_sems, i) for i, full in enumerate(fulls)]
    QKV, OUT, UP, DOWN = range(4)

    own = [(w_qkv.at[0], None), (w_out.at[0], wo_hbm), (w_up.at[0], wu_hbm), (w_down.at[0], wd_hbm)]
    x_load = pltpu.make_async_copy(
        x_hbm.at[pl.ds(pl.multiple_of(seq * LEN, LEN), LEN)], x_seq, local.at[0]
    )
    own_loads = [
        pltpu.make_async_copy(w, w_qkv.at[0, :, :, :, pl.ds(i * width, width)], local.at[1 + i])
        for i, w in enumerate((wq_hbm, wk_hbm, wv_hbm))
    ]
    x_load.start()
    for copy in own_loads:
        copy.start()
    out_loads = [pltpu.make_async_copy(wo_hbm, w_out.at[0], local.at[4])]
    up_load = pltpu.make_async_copy(wu_hbm, w_up.at[0], local.at[5])
    down_load = pltpu.make_async_copy(wd_hbm, w_down.at[0], local.at[6])
    own_saves = [
        pltpu.make_async_copy(w_qkv.at[0], qkv_full.at[p.t], local.at[7]),
        pltpu.make_async_copy(wo_hbm, out_full.at[p.t], local.at[8]),
        pltpu.make_async_copy(wu_hbm, up_full.at[p.t], local.at[9]),
        pltpu.make_async_copy(wd_hbm, down_full.at[p.t], local.at[10]),
    ]

    p.greet()

    def z_copies(array, step):
        slot = array * 4 + step
        if array == QKV:
            return [
                remote(
                    w.at[p.quad, p.core],
                    qkv_full.at[p.t, p.quad, p.core, :, pl.ds(i * width, width)],
                    z_send,
                    z_recv,
                    slot if i == 0 else 16 + 4 * (i - 1) + step,
                    p.to_z(step),
                )
                for i, w in enumerate((wq_hbm, wk_hbm, wv_hbm))
            ]
        w = (None, wo_hbm, wu_hbm, wd_hbm)[array]
        return [
            remote(
                w.at[p.quad, p.core],
                fulls[array].at[p.t, p.quad, p.core],
                z_send,
                z_recv,
                slot,
                p.to_z(step),
            )
        ]

    def small_copy(step):
        return remote(
            small_ref, small_all.at[p.t], small_send, small_recv, step, p.to_z(step)
        )

    def z_start(array, step):
        for copy in z_copies(array, step):
            copy.start()

    def z_sent(array, step):
        for copy in z_copies(array, step):
            copy.wait_send()

    def z_first(array, step):
        for copy in z_copies(array, step):
            copy.wait_recv()
        spreads[array].first(step)

    small_all[p.t] = small_ref[...]
    for step in (1, 2, 3):
        small_copy(step).start()
    for step in (1, 2, 3):
        z_start(QKV, step)
    for step in (1, 2, 3):
        z_start(OUT, step)

    def load_copy(array, step, slot):
        vmem = (w_qkv, w_out, w_up, w_down)[array]
        return pltpu.make_async_copy(
            fulls[array].at[mix(p.t, jnp.int32(step))], vmem.at[slot], load.at[array * 4 + step]
        )

    def attend(step):
        group = mix(p.t, step)
        slot = lax.rem(step, 2)
        weights = w_qkv[slot].reshape(model, 3 * width)
        bias = small_all[group, 0:1]
        x_own = x_seq[own_rows, :]
        queries = (product(x_own, weights[:, :width]) + bias[:, :width]).astype(BF)
        q_s[step] = (queries.astype(F32) * HD ** (-0.5)).astype(BF)
        k_s[step] = product(x_seq[...], weights[:, width : 2 * width]).astype(BF)
        v_s[step] = (
            product(x_seq[...], weights[:, 2 * width :]) + bias[:, width : 2 * width]
        ).astype(BF)
        length = len_ref[seq]
        key_slot = lax.broadcasted_iota(jnp.int32, (LEN, rows), 0)
        lane = lax.broadcasted_iota(jnp.int32, (rows, PAIR), 1)
        for pair in range(width // PAIR):
            cols = slice(pair * PAIR, (pair + 1) * PAIR)
            keys, values, q_pair = k_s[step, :, cols], v_s[step, :, cols], q_s[step, :, cols]
            parts = []
            for head in range(2):
                mine = jnp.where((lane >= HD) == (head == 1), q_pair, jnp.zeros_like(q_pair))
                scores = jnp.where(key_slot < length, product(keys, mine, NT), -1e30)
                top = jnp.max(scores, axis=0, keepdims=True)
                exponent = jnp.exp(scores - top)
                total = jnp.sum(exponent, axis=0, keepdims=True)
                mixed = product(values, exponent.astype(BF), TN)
                parts.append(mixed[head * HD : (head + 1) * HD] * (1.0 / total))
                lse_ref[group, pl.ds(pair * 2 + head, 1), :] = top + jnp.log(total)
            o_s[step, :, cols] = jnp.concatenate(parts, axis=0).T.astype(BF)

    def attend_saves(step):
        group = mix(p.t, jnp.int32(step))
        pairs = ((q_s, q_hbm), (k_s, k_hbm), (v_s, v_hbm), (o_s, o_hbm))
        return [
            pltpu.make_async_copy(vmem.at[step], hbm.at[group], save.at[4 * step + i])
            for i, (vmem, hbm) in enumerate(pairs)
        ]

    def on(step, at, action):
        @pl.when(step == at)
        def _():
            action()

    x_load.wait()
    for copy in own_loads:
        copy.wait()
    for copy in own_saves:
        copy.start()
    out_loads[0].start()
    up_load.start()
    down_load.start()
    for step in (1, 2, 3):
        small_copy(step).wait_recv()

    def after_first():
        z_first(QKV, 1)
        z_start(UP, 1)
        spreads[QKV].second(1)
        spreads[QKV].third(1)
        spreads[QKV].arrived(1)
        load_copy(QKV, 1, 1).start()
        for step in (2, 3):
            z_first(QKV, step)
        load_copy(QKV, 1, 1).wait()

    def after_second():
        for step in (2, 3):
            z_start(UP, step)
        own_saves[0].wait()
        for step in (2, 3):
            spreads[QKV].second(step)
        for step in (1, 2, 3):
            z_first(OUT, step)
        for step in (2, 3):
            spreads[QKV].third(step)
        spreads[QKV].arrived(2)
        load_copy(QKV, 2, 0).start()
        z_first(UP, 1)
        load_copy(QKV, 2, 0).wait()

    def after_third():
        spreads[QKV].arrived(3)
        load_copy(QKV, 3, 1).start()
        for step in (1, 2, 3):
            spreads[OUT].second(step)
        spreads[UP].second(1)
        for step in (2, 3):
            z_first(UP, step)
        z_start(DOWN, 1)
        z_start(DOWN, 2)
        for step in (1, 2, 3):
            spreads[OUT].third(step)
        spreads[UP].third(1)
        load_copy(QKV, 3, 1).wait()

    def after_fourth():
        for step in (1, 2, 3):
            spreads[OUT].arrived(step)
            load_copy(OUT, step, step).start()
        spreads[UP].arrived(1)
        load_copy(UP, 1, 1).start()
        for step in (2, 3):
            spreads[UP].second(step)
        z_start(DOWN, 3)

    def attend_step(step, carry):
        attend(step)
        for i in range(4):
            on(step, i, lambda i=i: [copy.start() for copy in attend_saves(i)])
        on(step, 0, after_first)
        on(step, 1, after_second)
        on(step, 2, after_third)
        on(step, 3, after_fourth)
        return carry

    lax.fori_loop(0, 4, attend_step, 0)

    out_loads[0].wait()
    for step in (1, 2, 3):
        load_copy(OUT, step, step).wait()
    total = x_seq[own_rows, :].astype(F32) + vec_ref[0:1]
    for step in range(4):
        total = total + product(o_s[step], w_out[step].reshape(width, model))
    normal1, inverse1 = norm_center(total)
    normal1_ref[...] = normal1
    inverse1_ref[...] = jnp.broadcast_to(inverse1, inverse1_ref.shape)
    normed1 = normal1 * vec_ref[1:2] + vec_ref[2:3]
    hidden_ref[...] = normed1.astype(BF)
    acc[...] = normed1 + vec_ref[3:4]
    for step in (2, 3):
        spreads[UP].third(step)
    z_first(DOWN, 1)

    def mlp_saves(step):
        part = mix(p.t, jnp.int32(step))
        return [
            pltpu.make_async_copy(act_s.at[step], act_hbm.at[part], save.at[16 + 2 * step]),
            pltpu.make_async_copy(slope_s.at[step], slope_hbm.at[part], save.at[17 + 2 * step]),
        ]

    def up_step(step, carry):
        slot = lax.rem(step, 2)
        on(step, 0, up_load.wait)
        on(step, 1, load_copy(UP, 1, 1).wait)
        on(step, 2, load_copy(UP, 2, 0).wait)
        on(step, 3, load_copy(UP, 3, 1).wait)
        weights = w_up[slot].reshape(model, model)
        upper = product(hidden_ref[...], weights) + small_all[mix(p.t, step), 1:2]
        cdf = 0.5 * (1.0 + lax.erf(upper * 0.7071067811865476))
        act_s[step] = (upper * cdf).astype(BF)
        density = jnp.exp(-0.5 * upper * upper) * 0.3989422804014327
        slope_s[step] = (cdf + upper * density).astype(BF)
        for i in range(4):
            on(step, i, lambda i=i: [copy.start() for copy in mlp_saves(i)])

        def zero():
            spreads[UP].arrived(2)
            load_copy(UP, 2, 0).start()
            spreads[UP].arrived(3)
            spreads[DOWN].second(1)
            z_first(DOWN, 2)

        def one():
            load_copy(UP, 3, 1).start()
            spreads[DOWN].third(1)
            z_first(DOWN, 3)
            spreads[DOWN].second(2)

        def two():
            spreads[DOWN].arrived(1)
            load_copy(DOWN, 1, 1).start()
            spreads[DOWN].third(2)

        def three():
            spreads[DOWN].second(3)

        on(step, 0, zero)
        on(step, 1, one)
        on(step, 2, two)
        on(step, 3, three)
        return carry

    lax.fori_loop(0, 4, up_step, 0)

    def down_step(step, carry):
        slot = lax.rem(step, 2)
        on(step, 0, down_load.wait)
        on(step, 1, load_copy(DOWN, 1, 1).wait)
        on(step, 2, load_copy(DOWN, 2, 0).wait)
        on(step, 3, load_copy(DOWN, 3, 1).wait)
        acc[...] += product(act_s[step], w_down[slot].reshape(model, model))

        def zero():
            spreads[DOWN].arrived(2)
            load_copy(DOWN, 2, 0).start()

        def one():
            spreads[DOWN].third(3)
            spreads[DOWN].arrived(3)
            load_copy(DOWN, 3, 1).start()

        on(step, 0, zero)
        on(step, 1, one)
        return carry

    lax.fori_loop(0, 4, down_step, 0)

    normal2, inverse2 = norm_center(acc[...])
    outputs_ref[...] = (normal2 * vec_ref[4:5] + vec_ref[5:6]).astype(BF)
    slot_index = half_index * rows + lax.broadcasted_iota(jnp.int32, (rows, 1), 0)
    grad_out = jnp.where(slot_index < len_ref[seq], cot_ref[...].astype(F32), 0.0)
    d_second = norm_back(grad_out, normal2, inverse2, vec_ref[4:5])
    d_second_ref[...] = d_second
    sums_ref[0:1] = jnp.sum(grad_out * normal2, axis=0, keepdims=True)
    sums_ref[1:2] = jnp.sum(grad_out, axis=0, keepdims=True)
    sums_ref[2:3] = jnp.sum(d_second, axis=0, keepdims=True)
    sums_ref[3:8] = jnp.zeros((5, model), F32)

    for copy in own_saves[1:]:
        copy.wait()
    for step in range(4):
        for copy in attend_saves(step) + mlp_saves(step):
            copy.wait()
    for step in (1, 2, 3):
        small_copy(step).wait_send()
        for array in range(4):
            z_sent(array, step)
            spreads[array].finish(step)


def run_forward(lengths, x, cot, vec, small, wq, wk, wv, wo, wu, wd):
    tensor_size = lax.axis_size("tensor")
    model = x.shape[1]
    rows = x.shape[0] // tensor_size
    width = wo.shape[0]
    pieces = lambda w: w.reshape(4, 2, w.shape[0] // GROUP, w.shape[1])
    anyw = pl.BlockSpec(memory_space=pl.ANY)
    vmem = pl.BlockSpec(memory_space=pltpu.VMEM)
    smem = pl.BlockSpec(memory_space=pltpu.SMEM)
    T = tensor_size
    out = lambda shape, dtype=BF: jax.ShapeDtypeStruct(shape, dtype)
    outs = [
        (out((T, 4, 2, model // GROUP, 3 * width)), anyw),
        (out((T, 4, 2, width // GROUP, model)), anyw),
        (out((T, 4, 2, model // GROUP, wu.shape[1])), anyw),
        (out((T, 4, 2, wd.shape[0] // GROUP, model)), anyw),
        (out((T, rows, width)), anyw),
        (out((T, LEN, width)), anyw),
        (out((T, LEN, width)), anyw),
        (out((T, rows, width)), anyw),
        (out((T, rows, wu.shape[1])), anyw),
        (out((T, rows, wu.shape[1])), anyw),
        (out((rows, model)), vmem),
        (out((rows, model), F32), vmem),
        (out((rows, model), F32), vmem),
        (out((rows, 128), F32), vmem),
        (out((rows, model)), vmem),
        (out((T, 8, rows), F32), vmem),
        (out((8, model), F32), vmem),
    ]
    scratch = [
        pltpu.VMEM((LEN, model), BF),
        pltpu.VMEM((T, 8, model), F32),
        pltpu.VMEM((2, 4, 2, model // GROUP, 3 * width), BF),
        pltpu.VMEM((T, 4, 2, width // GROUP, model), BF),
        pltpu.VMEM((2, 4, 2, model // GROUP, wu.shape[1]), BF),
        pltpu.VMEM((2, 4, 2, wd.shape[0] // GROUP, model), BF),
        pltpu.VMEM((T, rows, width), BF),
        pltpu.VMEM((T, LEN, width), BF),
        pltpu.VMEM((T, LEN, width), BF),
        pltpu.VMEM((T, rows, width), BF),
        pltpu.VMEM((T, rows, wu.shape[1]), BF),
        pltpu.VMEM((T, rows, wu.shape[1]), BF),
        pltpu.VMEM((rows, model), F32),
        pltpu.SemaphoreType.DMA((24,)),
        pltpu.SemaphoreType.DMA((24,)),
        pltpu.SemaphoreType.DMA((4,)),
        pltpu.SemaphoreType.DMA((4,)),
        pltpu.SemaphoreType.DMA((11,)),
        pltpu.SemaphoreType.DMA((16,)),
        pltpu.SemaphoreType.DMA((24,)),
        *Spread.scratch(4),
    ]
    return pl.pallas_call(
        forward_kernel,
        in_specs=[smem, anyw, vmem, vmem, vmem] + [anyw] * 6,
        out_specs=[spec for _, spec in outs],
        out_shape=[shape for shape, _ in outs],
        scratch_shapes=scratch,
        compiler_params=pltpu.CompilerParams(
            collective_id=0, has_side_effects=True, vmem_limit_bytes=VMEM_LIMIT
        ),
        cost_estimate=pl.CostEstimate(
            flops=40 * 10**9, bytes_accessed=60 << 20, transcendentals=16 << 20
        ),
        name="forward",
    )(
        lengths,
        x,
        cot,
        vec,
        small,
        pieces(wq),
        pieces(wk),
        pieces(wv),
        pieces(wo),
        pieces(wu),
        pieces(wd),
    )


def attend_back(q_ref, k_ref, v_ref, o_ref, d_ref, lse_ref, dq_ref, dk_ref, dv_ref, length):
    rows, width = q_ref.shape
    key_slot = lax.broadcasted_iota(jnp.int32, (LEN, rows), 0)
    lane = lax.broadcasted_iota(jnp.int32, (rows, PAIR), 1)
    for pair in range(width // PAIR):
        cols = slice(pair * PAIR, (pair + 1) * PAIR)
        keys, values, queries = k_ref[:, cols], v_ref[:, cols], q_ref[:, cols]
        d_out = d_ref[:, cols]
        inner_all = (d_out.astype(F32) * o_ref[:, cols].astype(F32)).T
        value_part, key_part, query_parts = None, None, []
        for head in range(2):
            mine = (lane >= HD) == (head == 1)
            own_q = jnp.where(mine, queries, jnp.zeros_like(queries))
            own_d = jnp.where(mine, d_out, jnp.zeros_like(d_out))
            inner = jnp.sum(inner_all[head * HD : (head + 1) * HD], axis=0, keepdims=True)
            scores = jnp.where(key_slot < length, product(keys, own_q, NT), -1e30)
            probs = jnp.exp(scores - lse_ref[pl.ds(pair * 2 + head, 1), :])
            d_probs = product(values, own_d, NT)
            d_scores = (probs * (d_probs - inner) * HD ** (-0.5)).astype(BF)
            d_values = product(probs.astype(BF), own_d)
            d_keys = product(d_scores, own_q)
            value_part = d_values if head == 0 else value_part + d_values
            key_part = d_keys if head == 0 else key_part + d_keys
            query_parts.append(product(keys, d_scores, TN)[head * HD : (head + 1) * HD])
        dk_ref[:, cols] = key_part * HD**0.5
        dv_ref[:, cols] = value_part
        dq_ref[:, cols] = jnp.concatenate(query_parts, axis=0).T.astype(BF)


def attend_back_kernel(len_ref, q_ref, k_ref, v_ref, o_ref, d_ref, lse_ref, dq_ref, dk_ref, dv_ref):
    seq = lax.div(lax.axis_index("tensor"), 2)
    attend_back(
        *(r.at[0] for r in (q_ref, k_ref, v_ref, o_ref, d_ref, lse_ref, dq_ref, dk_ref, dv_ref)),
        len_ref[seq],
    )


def run_attend_back(lengths, q, k, v, o, d, lse):
    spec = lambda a: pl.BlockSpec((1,) + a.shape[1:], lambda i: (i, 0, 0))
    return pl.pallas_call(
        attend_back_kernel,
        grid=(q.shape[0],),
        in_specs=[pl.BlockSpec(memory_space=pltpu.SMEM)] + [spec(a) for a in (q, k, v, o, d, lse)],
        out_specs=[spec(q), spec(k), spec(v)],
        out_shape=[
            jax.ShapeDtypeStruct(q.shape, BF),
            jax.ShapeDtypeStruct(k.shape, F32),
            jax.ShapeDtypeStruct(v.shape, F32),
        ],
        compiler_params=pltpu.CompilerParams(vmem_limit_bytes=VMEM_LIMIT),
        name="attend_back",
    )(lengths, q, k, v, o, d, lse)


def dp_groups():
    size = lax.axis_size("dp")
    return [list(range(first, first + GROUP)) for first in range(0, size, GROUP)]


def reduce_grads(packed):
    tensor_size, rows, cols = packed.shape
    part = lax.psum_scatter(
        packed.reshape(tensor_size, GROUP, rows // GROUP, cols),
        "dp",
        scatter_dimension=1,
        axis_index_groups=dp_groups(),
        tiled=False,
    )
    part = lax.psum_scatter(part, "tensor", scatter_dimension=0, tiled=False)
    full = lax.all_gather(part, "dp", axis=0, tiled=True, axis_index_groups=dp_groups()).astype(F32)
    if lax.axis_size("dp") > GROUP:
        full = lax.psum(
            full,
            "dp",
            axis_index_groups=[
                list(range(first, lax.axis_size("dp"), GROUP)) for first in range(GROUP)
            ],
        )
    return full


def on_device(
    inputs,
    cotangent,
    lengths,
    query_weight,
    key_weight,
    value_weight,
    query_bias,
    value_bias,
    out_weight,
    out_bias,
    norm1_gain,
    norm1_bias,
    up_weight,
    up_bias,
    down_weight,
    down_bias,
    norm2_gain,
    norm2_bias,
):
    T = lax.axis_size("tensor")
    t = lax.axis_index("tensor")
    row_count, model = inputs.shape
    rows = row_count // T
    width = out_weight.shape[0]
    zero_row = jnp.zeros((model,), F32)
    vec = jnp.stack(
        [out_bias, norm1_gain, norm1_bias, down_bias, norm2_gain, norm2_bias, zero_row, zero_row]
    )
    small = jnp.stack(
        [jnp.concatenate([query_bias, value_bias, zero_row[2 * width :]]), up_bias] + [zero_row] * 6
    )
    (
        qkv_full,
        out_full,
        up_full,
        down_full,
        q,
        k,
        v,
        o,
        act,
        slope,
        outputs,
        d_second,
        normal1,
        inverse1,
        hidden,
        lse,
        sums,
    ) = run_forward(
        lengths,
        inputs,
        cotangent,
        vec,
        small,
        query_weight,
        key_weight,
        value_weight,
        out_weight,
        up_weight,
        down_weight,
    )
    qkv_full = qkv_full.reshape(T, model, 3 * width)
    out_full = out_full.reshape(T, width, model)
    up_full = up_full.reshape(T, model, -1)
    down_full = down_full.reshape(T, -1, model)
    inverse1 = inverse1[:, :1]
    d2 = d_second.astype(BF)
    d_normed1 = d_second
    up_grads, down_grads, up_bias_parts = [], [], []
    for f in range(T):
        down_grads.append(product(act[f], d2, TN).astype(BF))
        d_upper = (product(d2, down_full[f], NT) * slope[f].astype(F32)).astype(BF)
        up_grads.append(product(hidden, d_upper, TN).astype(BF))
        up_bias_parts.append(jnp.sum(d_upper.astype(F32), 0))
        d_normed1 = d_normed1 + product(d_upper, up_full[f], NT)
    d_first = norm_back(d_normed1, normal1, inverse1, norm1_gain)
    d1 = d_first.astype(BF)
    out_grads = [product(o[g], d1, TN).astype(BF) for g in range(T)]
    d_att = jnp.stack([product(d1, out_full[g], NT).astype(BF) for g in range(T)])
    dq, dk, dv = run_attend_back(lengths, q, k, v, o, d_att, lse)
    half = lax.rem(t, 2)
    both = jnp.stack([dk, dv]).reshape(2, T, 2, rows, width)
    mine = lax.dynamic_index_in_dim(both, half, 2, keepdims=False)
    other = lax.dynamic_index_in_dim(both, 1 - half, 2, keepdims=False).astype(BF)
    other = lax.ppermute(other, "tensor", [(i, i ^ 1) for i in range(T)])
    dk, dv = (mine + other.astype(F32)).astype(BF)
    own_x = lax.dynamic_slice_in_dim(inputs, t * rows, rows, 0)
    d_all = jnp.concatenate([dq, dk, dv], axis=2)
    input_grad = d_first
    qkv_grads = []
    for g in range(T):
        input_grad = input_grad + product(d_all[g], qkv_full[g], NT)
        qkv_grads.append(product(own_x, d_all[g], TN).astype(BF))
    qkv_red = reduce_grads(jnp.stack(qkv_grads).reshape(T, 3 * width, model)).reshape(model, 3 * width)
    out_red = reduce_grads(jnp.stack(out_grads))
    up_red = reduce_grads(jnp.stack(up_grads))
    down_red = reduce_grads(jnp.stack(down_grads))
    bias_rows = jnp.sum(d_all.astype(F32), 1)
    bias_rows = jnp.concatenate([bias_rows, jnp.zeros((T, model - 3 * width), F32)], axis=1)
    sums2 = jnp.stack(
        [
            jnp.sum(d_normed1 * normal1, 0),
            jnp.sum(d_normed1, 0),
            jnp.sum(d_first, 0),
        ]
    )
    total = lax.psum(
        jnp.concatenate([sums[:3], sums2, jnp.stack(up_bias_parts), bias_rows]), ("dp", "tensor")
    )
    up_bias_grad = lax.dynamic_index_in_dim(total[6 : 6 + T], t, 0, keepdims=False)
    qkv_bias = lax.dynamic_index_in_dim(total[6 + T :], t, 0, keepdims=False)
    return (
        outputs,
        input_grad,
        qkv_red[:, :width],
        qkv_red[:, width : 2 * width],
        qkv_red[:, 2 * width :],
        qkv_bias[:width],
        qkv_bias[2 * width : 3 * width],
        out_red,
        total[5],
        total[3],
        total[4],
        up_red,
        up_bias_grad,
        down_red,
        total[2],
        total[0],
        total[1],
    )


def solution(mesh):
    rows = P(("dp", "tensor"), None)
    by_col = P(None, "tensor")
    by_row = P("tensor", None)
    split = P("tensor")
    whole = P()
    return jax.shard_map(
        on_device,
        mesh=mesh,
        in_specs=(
            P("dp", None),
            rows,
            P("dp"),
            by_col,
            by_col,
            by_col,
            split,
            split,
            by_row,
            whole,
            whole,
            whole,
            by_col,
            split,
            by_row,
            whole,
            whole,
            whole,
        ),
        out_specs=(
            rows,
            rows,
            by_col,
            by_col,
            by_col,
            split,
            split,
            by_row,
            whole,
            whole,
            whole,
            by_col,
            split,
            by_row,
            whole,
            whole,
            whole,
        ),
        check_vma=False,
    )
```

```python
import functools

import jax
import jax.numpy as jnp
from jax import lax
from jax.experimental import pallas as pl
from jax.experimental.pallas import tpu as pltpu
from jax.sharding import PartitionSpec as P

HD = 64
LEN = 1024
PAIR = 2 * HD
GROUP = 8
F32 = jnp.float32
BF = jnp.bfloat16
NN = (((1,), (0,)), ((), ()))
NT = (((1,), (1,)), ((), ()))
TN = (((0,), (0,)), ((), ()))
MESH = pl.DeviceIdType.MESH
VMEM_LIMIT = 62 << 20


def product(left, right, dims=NN):
    return lax.dot_general(left, right, dims, preferred_element_type=F32)


def flip(index, bit):
    return index + bit * (1 - 2 * lax.rem(lax.div(index, bit), 2))


def mix(index, step):
    low = lax.rem(index + step, 2)
    high = lax.rem(lax.div(index, 2) + lax.div(step, 2), 2)
    return 2 * high + low


class Place:
    def __init__(self):
        self.dp = lax.axis_index("dp")
        self.t = lax.axis_index("tensor")
        self.e = lax.rem(self.dp, GROUP)
        self.core = lax.rem(self.e, 2)
        self.quad = lax.div(self.e, 2)
        self.to_core = (flip(self.dp, 1), self.t)
        self.to_x = (flip(self.dp, 2), self.t)
        self.to_y = (flip(self.dp, 4), self.t)
        self.quad_x = flip(self.quad, 1)
        self.quad_y = flip(self.quad, 2)
        self.quad_xy = flip(self.quad_x, 2)

    def to_z(self, step):
        return (self.dp, mix(self.t, jnp.int32(step)))

    def greet(self):
        barrier = pltpu.get_barrier_semaphore()
        peers = [self.to_core, self.to_x, self.to_y, self.to_z(1), self.to_z(2), self.to_z(3)]
        for peer in peers:
            pl.semaphore_signal(barrier, inc=1, device_id=peer, device_id_type=MESH)
        pl.semaphore_wait(barrier, len(peers))


def remote(src, dst, send, recv, index, device):
    return pltpu.make_async_remote_copy(
        src_ref=src,
        dst_ref=dst,
        send_sem=send.at[index],
        recv_sem=recv.at[index],
        device_id=device,
        device_id_type=MESH,
    )


class Spread:
    def __init__(self, place, full, sems, index):
        self.p = place
        self.full = full
        self.sems = sems
        self.index = index

    def block(self, step):
        return mix(self.p.t, jnp.int32(step)) if step else self.p.t

    def slot(self, step):
        return self.index * 4 + step

    def x_copy(self, step):
        p = self.p
        ref = self.full.at[self.block(step), p.quad, p.core]
        return remote(ref, ref, self.sems[0], self.sems[1], self.slot(step), p.to_x)

    def y_copy(self, step):
        p = self.p
        ref = self.full.at[self.block(step), p.quad, p.core]
        return remote(ref, ref, self.sems[2], self.sems[3], self.slot(step), p.to_y)

    def half_copies(self, step):
        p = self.p
        half = self.full.shape[3] // 2
        first = self.full.at[self.block(step), p.quad_x, p.core, pl.ds(0, half)]
        second = self.full.at[self.block(step), p.quad_y, p.core, pl.ds(half, half)]
        return (
            remote(first, first, self.sems[4], self.sems[5], self.slot(step), p.to_y),
            remote(second, second, self.sems[6], self.sems[7], self.slot(step), p.to_x),
        )

    def core_copy(self, step):
        p = self.p
        ref = self.full.at[self.block(step), :, p.core]
        return remote(ref, ref, self.sems[8], self.sems[9], self.slot(step), p.to_core)

    def first(self, step):
        self.x_copy(step).start()
        self.y_copy(step).start()

    def second(self, step):
        self.x_copy(step).wait_recv()
        self.y_copy(step).wait_recv()
        for copy in self.half_copies(step):
            copy.start()

    def third(self, step):
        for copy in self.half_copies(step):
            copy.wait_recv()
        self.core_copy(step).start()

    def arrived(self, step):
        self.core_copy(step).wait_recv()

    def finish(self, step):
        self.x_copy(step).wait_send()
        self.y_copy(step).wait_send()
        for copy in self.half_copies(step):
            copy.wait_send()
        self.core_copy(step).wait_send()

    @staticmethod
    def scratch(count):
        return [pltpu.SemaphoreType.DMA((4 * count,))] * 10


def norm_center(values):
    center = values - jnp.mean(values, axis=-1, keepdims=True)
    inverse = lax.rsqrt(jnp.mean(center * center, axis=-1, keepdims=True) + 1e-05)
    return center * inverse, inverse


def norm_back(grad, normal, inverse, gain):
    scaled = grad * gain
    first_mean = jnp.mean(scaled, axis=-1, keepdims=True)
    second_mean = jnp.mean(scaled * normal, axis=-1, keepdims=True)
    return inverse * (scaled - first_mean - normal * second_mean)


def forward_kernel(
    len_ref,
    x_hbm,
    cot_ref,
    vec_ref,
    small_ref,
    wq_hbm,
    wk_hbm,
    wv_hbm,
    wo_hbm,
    wu_hbm,
    wd_hbm,
    qkv_full,
    out_full,
    up_full,
    down_full,
    q_hbm,
    k_hbm,
    v_hbm,
    o_hbm,
    act_hbm,
    slope_hbm,
    outputs_ref,
    d_second_ref,
    normal1_ref,
    inverse1_ref,
    hidden_ref,
    lse_ref,
    sums_ref,
    x_seq,
    small_all,
    w_qkv,
    w_out,
    w_up,
    w_down,
    q_s,
    k_s,
    v_s,
    o_s,
    act_s,
    slope_s,
    acc,
    z_send,
    z_recv,
    small_send,
    small_recv,
    local,
    load,
    save,
    *spread_sems,
):
    p = Place()
    rows, model = acc.shape
    width = q_s.shape[2]
    half_index = lax.rem(p.t, 2)
    seq = lax.div(p.t, 2)
    own_rows = pl.ds(pl.multiple_of(half_index * rows, rows), rows)
    fulls = [qkv_full, out_full, up_full, down_full]
    spreads = [Spread(p, full, spread_sems, i) for i, full in enumerate(fulls)]
    QKV, OUT, UP, DOWN = range(4)

    own = [(w_qkv.at[0], None), (w_out.at[0], wo_hbm), (w_up.at[0], wu_hbm), (w_down.at[0], wd_hbm)]
    x_load = pltpu.make_async_copy(
        x_hbm.at[pl.ds(pl.multiple_of(seq * LEN, LEN), LEN)], x_seq, local.at[0]
    )
    own_loads = [
        pltpu.make_async_copy(w, w_qkv.at[0, :, :, :, pl.ds(i * width, width)], local.at[1 + i])
        for i, w in enumerate((wq_hbm, wk_hbm, wv_hbm))
    ]
    x_load.start()
    for copy in own_loads:
        copy.start()
    out_loads = [pltpu.make_async_copy(wo_hbm, w_out.at[0], local.at[4])]
    up_load = pltpu.make_async_copy(wu_hbm, w_up.at[0], local.at[5])
    down_load = pltpu.make_async_copy(wd_hbm, w_down.at[0], local.at[6])
    own_saves = [
        pltpu.make_async_copy(w_qkv.at[0], qkv_full.at[p.t], local.at[7]),
        pltpu.make_async_copy(wo_hbm, out_full.at[p.t], local.at[8]),
        pltpu.make_async_copy(wu_hbm, up_full.at[p.t], local.at[9]),
        pltpu.make_async_copy(wd_hbm, down_full.at[p.t], local.at[10]),
    ]

    p.greet()

    def z_copies(array, step):
        slot = array * 4 + step
        if array == QKV:
            return [
                remote(
                    w.at[p.quad, p.core],
                    qkv_full.at[p.t, p.quad, p.core, :, pl.ds(i * width, width)],
                    z_send,
                    z_recv,
                    slot if i == 0 else 16 + 4 * (i - 1) + step,
                    p.to_z(step),
                )
                for i, w in enumerate((wq_hbm, wk_hbm, wv_hbm))
            ]
        w = (None, wo_hbm, wu_hbm, wd_hbm)[array]
        return [
            remote(
                w.at[p.quad, p.core],
                fulls[array].at[p.t, p.quad, p.core],
                z_send,
                z_recv,
                slot,
                p.to_z(step),
            )
        ]

    def small_copy(step):
        return remote(
            small_ref, small_all.at[p.t], small_send, small_recv, step, p.to_z(step)
        )

    def z_start(array, step):
        for copy in z_copies(array, step):
            copy.start()

    def z_sent(array, step):
        for copy in z_copies(array, step):
            copy.wait_send()

    def z_first(array, step):
        for copy in z_copies(array, step):
            copy.wait_recv()
        spreads[array].first(step)

    small_all[p.t] = small_ref[...]
    for step in (1, 2, 3):
        small_copy(step).start()
    for step in (1, 2, 3):
        z_start(QKV, step)
    for step in (1, 2, 3):
        z_start(OUT, step)

    def load_copy(array, step, slot):
        vmem = (w_qkv, w_out, w_up, w_down)[array]
        return pltpu.make_async_copy(
            fulls[array].at[mix(p.t, jnp.int32(step))], vmem.at[slot], load.at[array * 4 + step]
        )

    def attend(step):
        group = mix(p.t, step)
        slot = lax.rem(step, 2)
        weights = w_qkv[slot].reshape(model, 3 * width)
        bias = small_all[group, 0:1]
        x_own = x_seq[own_rows, :]
        queries = (product(x_own, weights[:, :width]) + bias[:, :width]).astype(BF)
        q_s[step] = (queries.astype(F32) * HD ** (-0.5)).astype(BF)
        k_s[step] = product(x_seq[...], weights[:, width : 2 * width]).astype(BF)
        v_s[step] = (
            product(x_seq[...], weights[:, 2 * width :]) + bias[:, width : 2 * width]
        ).astype(BF)
        length = len_ref[seq]
        key_slot = lax.broadcasted_iota(jnp.int32, (LEN, rows), 0)
        lane = lax.broadcasted_iota(jnp.int32, (rows, PAIR), 1)
        for pair in range(width // PAIR):
            cols = slice(pair * PAIR, (pair + 1) * PAIR)
            keys, values, q_pair = k_s[step, :, cols], v_s[step, :, cols], q_s[step, :, cols]
            parts = []
            for head in range(2):
                mine = jnp.where((lane >= HD) == (head == 1), q_pair, jnp.zeros_like(q_pair))
                scores = jnp.where(key_slot < length, product(keys, mine, NT), -1e30)
                top = jnp.max(scores, axis=0, keepdims=True)
                exponent = jnp.exp(scores - top)
                total = jnp.sum(exponent, axis=0, keepdims=True)
                mixed = product(values, exponent.astype(BF), TN)
                parts.append(mixed[head * HD : (head + 1) * HD] * (1.0 / total))
                lse_ref[group, pl.ds(pair * 2 + head, 1), :] = top + jnp.log(total)
            o_s[step, :, cols] = jnp.concatenate(parts, axis=0).T.astype(BF)

    def attend_saves(step):
        group = mix(p.t, jnp.int32(step))
        pairs = ((q_s, q_hbm), (k_s, k_hbm), (v_s, v_hbm), (o_s, o_hbm))
        return [
            pltpu.make_async_copy(vmem.at[step], hbm.at[group], save.at[4 * step + i])
            for i, (vmem, hbm) in enumerate(pairs)
        ]

    def on(step, at, action):
        @pl.when(step == at)
        def _():
            action()

    x_load.wait()
    for copy in own_loads:
        copy.wait()
    for copy in own_saves:
        copy.start()
    out_loads[0].start()
    up_load.start()
    down_load.start()
    for step in (1, 2, 3):
        small_copy(step).wait_recv()

    def after_first():
        z_first(QKV, 1)
        z_start(UP, 1)
        spreads[QKV].second(1)
        spreads[QKV].third(1)
        spreads[QKV].arrived(1)
        load_copy(QKV, 1, 1).start()
        for step in (2, 3):
            z_first(QKV, step)
        load_copy(QKV, 1, 1).wait()

    def after_second():
        for step in (2, 3):
            z_start(UP, step)
        own_saves[0].wait()
        for step in (2, 3):
            spreads[QKV].second(step)
        for step in (1, 2, 3):
            z_first(OUT, step)
        for step in (2, 3):
            spreads[QKV].third(step)
        spreads[QKV].arrived(2)
        load_copy(QKV, 2, 0).start()
        z_first(UP, 1)
        load_copy(QKV, 2, 0).wait()

    def after_third():
        spreads[QKV].arrived(3)
        load_copy(QKV, 3, 1).start()
        for step in (1, 2, 3):
            spreads[OUT].second(step)
        spreads[UP].second(1)
        for step in (2, 3):
            z_first(UP, step)
        z_start(DOWN, 1)
        z_start(DOWN, 2)
        for step in (1, 2, 3):
            spreads[OUT].third(step)
        spreads[UP].third(1)
        load_copy(QKV, 3, 1).wait()

    def after_fourth():
        for step in (1, 2, 3):
            spreads[OUT].arrived(step)
            load_copy(OUT, step, step).start()
        spreads[UP].arrived(1)
        load_copy(UP, 1, 1).start()
        for step in (2, 3):
            spreads[UP].second(step)
        z_start(DOWN, 3)

    def attend_step(step, carry):
        attend(step)
        for i in range(4):
            on(step, i, lambda i=i: [copy.start() for copy in attend_saves(i)])
        on(step, 0, after_first)
        on(step, 1, after_second)
        on(step, 2, after_third)
        on(step, 3, after_fourth)
        return carry

    lax.fori_loop(0, 4, attend_step, 0)

    out_loads[0].wait()
    for step in (1, 2, 3):
        load_copy(OUT, step, step).wait()
    total = x_seq[own_rows, :].astype(F32) + vec_ref[0:1]
    for step in range(4):
        total = total + product(o_s[step], w_out[step].reshape(width, model))
    normal1, inverse1 = norm_center(total)
    normal1_ref[...] = normal1
    inverse1_ref[...] = jnp.broadcast_to(inverse1, inverse1_ref.shape)
    normed1 = normal1 * vec_ref[1:2] + vec_ref[2:3]
    hidden_ref[...] = normed1.astype(BF)
    acc[...] = normed1 + vec_ref[3:4]
    for step in (2, 3):
        spreads[UP].third(step)
    z_first(DOWN, 1)

    def mlp_saves(step):
        part = mix(p.t, jnp.int32(step))
        return [
            pltpu.make_async_copy(act_s.at[step], act_hbm.at[part], save.at[16 + 2 * step]),
            pltpu.make_async_copy(slope_s.at[step], slope_hbm.at[part], save.at[17 + 2 * step]),
        ]

    def up_step(step, carry):
        slot = lax.rem(step, 2)
        on(step, 0, up_load.wait)
        on(step, 1, load_copy(UP, 1, 1).wait)
        on(step, 2, load_copy(UP, 2, 0).wait)
        on(step, 3, load_copy(UP, 3, 1).wait)
        weights = w_up[slot].reshape(model, model)
        upper = product(hidden_ref[...], weights) + small_all[mix(p.t, step), 1:2]
        cdf = 0.5 * (1.0 + lax.erf(upper * 0.7071067811865476))
        act_s[step] = (upper * cdf).astype(BF)
        density = jnp.exp(-0.5 * upper * upper) * 0.3989422804014327
        slope_s[step] = (cdf + upper * density).astype(BF)
        for i in range(4):
            on(step, i, lambda i=i: [copy.start() for copy in mlp_saves(i)])

        def zero():
            spreads[UP].arrived(2)
            load_copy(UP, 2, 0).start()
            spreads[UP].arrived(3)
            spreads[DOWN].second(1)
            z_first(DOWN, 2)

        def one():
            load_copy(UP, 3, 1).start()
            spreads[DOWN].third(1)
            z_first(DOWN, 3)
            spreads[DOWN].second(2)

        def two():
            spreads[DOWN].arrived(1)
            load_copy(DOWN, 1, 1).start()
            spreads[DOWN].third(2)

        def three():
            spreads[DOWN].second(3)

        on(step, 0, zero)
        on(step, 1, one)
        on(step, 2, two)
        on(step, 3, three)
        return carry

    lax.fori_loop(0, 4, up_step, 0)

    def down_step(step, carry):
        slot = lax.rem(step, 2)
        on(step, 0, down_load.wait)
        on(step, 1, load_copy(DOWN, 1, 1).wait)
        on(step, 2, load_copy(DOWN, 2, 0).wait)
        on(step, 3, load_copy(DOWN, 3, 1).wait)
        acc[...] += product(act_s[step], w_down[slot].reshape(model, model))

        def zero():
            spreads[DOWN].arrived(2)
            load_copy(DOWN, 2, 0).start()

        def one():
            spreads[DOWN].third(3)
            spreads[DOWN].arrived(3)
            load_copy(DOWN, 3, 1).start()

        on(step, 0, zero)
        on(step, 1, one)
        return carry

    lax.fori_loop(0, 4, down_step, 0)

    normal2, inverse2 = norm_center(acc[...])
    outputs_ref[...] = (normal2 * vec_ref[4:5] + vec_ref[5:6]).astype(BF)
    slot_index = half_index * rows + lax.broadcasted_iota(jnp.int32, (rows, 1), 0)
    grad_out = jnp.where(slot_index < len_ref[seq], cot_ref[...].astype(F32), 0.0)
    d_second = norm_back(grad_out, normal2, inverse2, vec_ref[4:5])
    d_second_ref[...] = d_second
    sums_ref[0:1] = jnp.sum(grad_out * normal2, axis=0, keepdims=True)
    sums_ref[1:2] = jnp.sum(grad_out, axis=0, keepdims=True)
    sums_ref[2:3] = jnp.sum(d_second, axis=0, keepdims=True)
    sums_ref[3:8] = jnp.zeros((5, model), F32)

    for copy in own_saves[1:]:
        copy.wait()
    for step in range(4):
        for copy in attend_saves(step) + mlp_saves(step):
            copy.wait()
    for step in (1, 2, 3):
        small_copy(step).wait_send()
        for array in range(4):
            z_sent(array, step)
            spreads[array].finish(step)


def run_forward(lengths, x, cot, vec, small, wq, wk, wv, wo, wu, wd):
    tensor_size = lax.axis_size("tensor")
    model = x.shape[1]
    rows = x.shape[0] // tensor_size
    width = wo.shape[0]
    pieces = lambda w: w.reshape(4, 2, w.shape[0] // GROUP, w.shape[1])
    anyw = pl.BlockSpec(memory_space=pl.ANY)
    vmem = pl.BlockSpec(memory_space=pltpu.VMEM)
    smem = pl.BlockSpec(memory_space=pltpu.SMEM)
    T = tensor_size
    out = lambda shape, dtype=BF: jax.ShapeDtypeStruct(shape, dtype)
    outs = [
        (out((T, 4, 2, model // GROUP, 3 * width)), anyw),
        (out((T, 4, 2, width // GROUP, model)), anyw),
        (out((T, 4, 2, model // GROUP, wu.shape[1])), anyw),
        (out((T, 4, 2, wd.shape[0] // GROUP, model)), anyw),
        (out((T, rows, width)), anyw),
        (out((T, LEN, width)), anyw),
        (out((T, LEN, width)), anyw),
        (out((T, rows, width)), anyw),
        (out((T, rows, wu.shape[1])), anyw),
        (out((T, rows, wu.shape[1])), anyw),
        (out((rows, model)), vmem),
        (out((rows, model), F32), vmem),
        (out((rows, model), F32), vmem),
        (out((rows, 128), F32), vmem),
        (out((rows, model)), vmem),
        (out((T, 8, rows), F32), vmem),
        (out((8, model), F32), vmem),
    ]
    scratch = [
        pltpu.VMEM((LEN, model), BF),
        pltpu.VMEM((T, 8, model), F32),
        pltpu.VMEM((2, 4, 2, model // GROUP, 3 * width), BF),
        pltpu.VMEM((T, 4, 2, width // GROUP, model), BF),
        pltpu.VMEM((2, 4, 2, model // GROUP, wu.shape[1]), BF),
        pltpu.VMEM((2, 4, 2, wd.shape[0] // GROUP, model), BF),
        pltpu.VMEM((T, rows, width), BF),
        pltpu.VMEM((T, LEN, width), BF),
        pltpu.VMEM((T, LEN, width), BF),
        pltpu.VMEM((T, rows, width), BF),
        pltpu.VMEM((T, rows, wu.shape[1]), BF),
        pltpu.VMEM((T, rows, wu.shape[1]), BF),
        pltpu.VMEM((rows, model), F32),
        pltpu.SemaphoreType.DMA((24,)),
        pltpu.SemaphoreType.DMA((24,)),
        pltpu.SemaphoreType.DMA((4,)),
        pltpu.SemaphoreType.DMA((4,)),
        pltpu.SemaphoreType.DMA((11,)),
        pltpu.SemaphoreType.DMA((16,)),
        pltpu.SemaphoreType.DMA((24,)),
        *Spread.scratch(4),
    ]
    return pl.pallas_call(
        forward_kernel,
        in_specs=[smem, anyw, vmem, vmem, vmem] + [anyw] * 6,
        out_specs=[spec for _, spec in outs],
        out_shape=[shape for shape, _ in outs],
        scratch_shapes=scratch,
        compiler_params=pltpu.CompilerParams(
            collective_id=0, has_side_effects=True, vmem_limit_bytes=VMEM_LIMIT
        ),
        cost_estimate=pl.CostEstimate(
            flops=40 * 10**9, bytes_accessed=60 << 20, transcendentals=16 << 20
        ),
        name="forward",
    )(
        lengths,
        x,
        cot,
        vec,
        small,
        pieces(wq),
        pieces(wk),
        pieces(wv),
        pieces(wo),
        pieces(wu),
        pieces(wd),
    )


class Reduce:
    def __init__(self, place, bufs, sems):
        self.p = place
        self.g, self.s, self.rc, self.ra, self.rb, self.zs, self.rz, self.own = bufs
        self.sems = sems

    @staticmethod
    def scratch(piece, cols, arrays):
        return [
            pltpu.VMEM((2, 4, 2, piece, cols), BF),
            pltpu.VMEM((3, 4, piece, cols), BF),
            pltpu.VMEM((2, 4, piece, cols), BF),
            pltpu.VMEM((3, 2, piece // 2, cols), BF),
            pltpu.VMEM((3, 2, piece, cols), BF),
            pltpu.VMEM((3, piece, cols), BF),
            pltpu.VMEM((arrays, 4, piece, cols), BF),
            pltpu.VMEM((arrays, piece, cols), BF),
        ]

    @staticmethod
    def semaphores(units):
        return [pltpu.SemaphoreType.DMA((units,))] * 12

    def core_copy(self, u):
        other = 1 - self.p.core
        return remote(
            self.g.at[lax.rem(u, 2), :, other],
            self.rc.at[lax.rem(u, 2)],
            self.sems[0],
            self.sems[1],
            u,
            self.p.to_core,
        )

    def corner_copies(self, u):
        p, slot = self.p, lax.rem(u, 3)
        half = self.ra.shape[2]
        return (
            remote(
                self.s.at[slot, p.quad_xy, pl.ds(0, half)],
                self.ra.at[slot, 0],
                self.sems[2],
                self.sems[3],
                u,
                p.to_y,
            ),
            remote(
                self.s.at[slot, p.quad_xy, pl.ds(half, half)],
                self.ra.at[slot, 1],
                self.sems[4],
                self.sems[5],
                u,
                p.to_x,
            ),
        )

    def side_copies(self, u):
        p, slot = self.p, lax.rem(u, 3)
        return (
            remote(
                self.s.at[slot, p.quad_x], self.rb.at[slot, 0], self.sems[6], self.sems[7], u, p.to_x
            ),
            remote(
                self.s.at[slot, p.quad_y], self.rb.at[slot, 1], self.sems[8], self.sems[9], u, p.to_y
            ),
        )

    def z_copy(self, u, array, step):
        return remote(
            self.zs.at[lax.rem(u, 3)],
            self.rz.at[array, step],
            self.sems[10],
            self.sems[11],
            array * 4 + step,
            (self.p.dp, mix(self.p.t, step)),
        )

    def free_g(self, u):
        if not isinstance(u, int):
            pl.when(u >= 2)(lambda: self.core_copy(u - 2).wait_send())
        elif u >= 2:
            self.core_copy(jnp.int32(u - 2)).wait_send()

    def send(self, u):
        self.core_copy(u).start()

    def fold_core(self, u):
        slot = lax.rem(u, 3)

        def freed():
            for copy in self.side_copies(u - 3) + self.corner_copies(u - 3):
                copy.wait_send()

        pl.when(u >= 3)(freed)
        self.core_copy(u).wait_recv()
        mine = self.g[lax.rem(u, 2), :, self.p.core].astype(F32)
        self.s[slot] = (mine + self.rc[lax.rem(u, 2)].astype(F32)).astype(BF)
        for copy in self.corner_copies(u):
            copy.start()

    def fold_corner(self, u):
        p, slot = self.p, lax.rem(u, 3)
        half = self.ra.shape[2]
        for copy in self.corner_copies(u):
            copy.wait_recv()
        lower = self.s[slot, p.quad_x, :half].astype(F32) + self.ra[slot, 0].astype(F32)
        self.s[slot, p.quad_x, :half] = lower.astype(BF)
        upper = self.s[slot, p.quad_y, half:].astype(F32) + self.ra[slot, 1].astype(F32)
        self.s[slot, p.quad_y, half:] = upper.astype(BF)
        for copy in self.side_copies(u):
            copy.start()

    def fold_sides(self, u, array, step, before):
        p, slot = self.p, lax.rem(u, 3)
        for copy in self.side_copies(u):
            copy.wait_recv()
        total = (
            self.s[slot, p.quad].astype(F32)
            + self.rb[slot, 0].astype(F32)
            + self.rb[slot, 1].astype(F32)
        ).astype(BF)

        if before is not None:
            old_array, old_step, valid = before
            pl.when(valid)(lambda: self.z_copy(u - 3, old_array, old_step).wait_send())

        def store():
            self.own[array] = total

        def pass_on():
            self.zs[slot] = total
            self.z_copy(u, array, step).start()

        pl.when(step == 0)(store)
        pl.when(step != 0)(pass_on)

    def finish(self, array, out, sem):
        total = self.own[array].astype(F32)
        for step in (1, 2, 3):
            self.z_copy(jnp.int32(0), jnp.int32(array), jnp.int32(step)).wait_recv()
            total = total + self.rz[array, step].astype(F32)
        self.own[array] = total.astype(BF)
        copy = pltpu.make_async_copy(self.own.at[array], out.at[0, self.p.quad, self.p.core], sem)
        copy.start()
        copy.wait()


def backward_kernel(
    len_ref,
    x_hbm,
    vec_ref,
    sums_in,
    qkv_full,
    out_full,
    up_full,
    down_full,
    q_hbm,
    k_hbm,
    v_hbm,
    o_hbm,
    act_hbm,
    slope_hbm,
    d_second_hbm,
    normal1_hbm,
    inverse1_ref,
    hidden_ref,
    lse_ref,
    down_grad,
    up_grad,
    proj_grad,
    acc,
    sums_ref,
    w_s,
    w_out,
    act_s,
    slope_s,
    d2_s,
    d1_s,
    x_own,
    q_s,
    k_s,
    v_s,
    o_s,
    d_att,
    kv_temp,
    wide,
    kv_send,
    kv_recv,
    d_all,
    small,
    small_recv,
    load,
    att_load,
    misc,
    kv_ssem,
    kv_rsem,
    small_ssem,
    small_rsem,
    *rest,
):
    p = Place()
    reduce = Reduce(p, rest[:8], rest[8:20])
    spread_sems = rest[20:]
    rows, model = acc.shape
    width = q_s.shape[2]
    half_index = lax.rem(p.t, 2)
    seq = lax.div(p.t, 2)
    own_at = pl.multiple_of(half_index * rows, rows)
    other_at = pl.multiple_of((1 - half_index) * rows, rows)
    grads = (down_grad, up_grad, proj_grad)
    spreads = [Spread(p, grad, spread_sems, i) for i, grad in enumerate(grads)]
    for spread in spreads:
        spread.block = lambda step: 0
    DOWN, UP, PROJ = range(3)

    acc_load = pltpu.make_async_copy(d_second_hbm, acc, misc.at[0])
    x_load = pltpu.make_async_copy(
        x_hbm.at[pl.ds(pl.multiple_of(p.t * rows, rows), rows)], x_own, misc.at[1]
    )
    normal_load = pltpu.make_async_copy(normal1_hbm, wide, misc.at[2])

    def mlp_loads(i):
        f, slot = mix(p.t, 3 - i), lax.rem(i, 2)
        pairs = (
            (act_hbm.at[f], act_s.at[slot]),
            (down_full.at[f], w_s.at[slot]),
            (slope_hbm.at[f], slope_s.at[slot]),
            (up_full.at[f], w_s.at[2 + slot]),
        )
        return [
            pltpu.make_async_copy(src, dst, load.at[4 * i + n]) for n, (src, dst) in enumerate(pairs)
        ]

    def group_at(i):
        return 2 * lax.rem(lax.div(p.t, 2) + 1 + lax.div(i, 2), 2) + lax.rem(i, 2)

    def att_loads(i):
        g, slot = group_at(i), lax.rem(i, 2)
        pairs = (
            (q_hbm.at[g], q_s.at[slot]),
            (k_hbm.at[g], k_s.at[slot]),
            (v_hbm.at[g], v_s.at[slot]),
            (o_hbm.at[g], o_s.at[slot]),
            (out_full.at[g], w_out.at[slot]),
        )
        return [
            pltpu.make_async_copy(src, dst, att_load.at[6 * i + n])
            for n, (src, dst) in enumerate(pairs)
        ]

    def proj_load(i):
        g, slot = group_at(i), lax.rem(i, 2)
        return pltpu.make_async_copy(
            qkv_full.at[g], w_s.at[slot, :, :, :, pl.ds(0, 3 * width)], att_load.at[6 * i + 5]
        )

    def begin(copies):
        for copy in copies:
            copy.start()

    def end(copies):
        for copy in copies:
            copy.wait()

    acc_load.start()
    begin(mlp_loads(jnp.int32(0)))
    x_load.start()
    normal_load.start()
    begin(att_loads(jnp.int32(0)))
    small[0] = jnp.zeros(small.shape[1:], F32)
    small[0, 0:3] = sums_in[0:3]
    p.greet()
    acc_load.wait()
    d2_s[...] = acc[...].astype(BF)

    def unit_of(u):
        return lax.rem(u, 2), 3 - lax.div(u, 2)

    def fold_sides(u):
        array, step = unit_of(u)
        old_array, old_step = unit_of(jnp.maximum(u - 3, 0))
        reduce.fold_sides(u, array, step, (old_array, old_step, jnp.logical_and(u >= 3, old_step != 0)))

    def tick(u):
        pl.when(u >= 1)(lambda: reduce.fold_core(u - 1))
        reduce.send(u)
        pl.when(u >= 2)(lambda: reduce.fold_corner(u - 2))
        pl.when(u >= 3)(lambda: fold_sides(u - 3))

    block = (4, 2, model // GROUP, model)

    def mlp_step(i, carry):
        slot = lax.rem(i, 2)
        f = mix(p.t, 3 - i)
        pl.when(i < 3)(lambda: begin(mlp_loads(i + 1)))
        act_c, down_c, slope_c, up_c = mlp_loads(i)
        act_c.wait()
        u = 2 * i
        reduce.free_g(u)
        reduce.g[0] = product(act_s[slot], d2_s[...], TN).astype(BF).reshape(block)
        tick(u)
        down_c.wait()
        slope_c.wait()
        d_act = product(d2_s[...], w_s[slot].reshape(model, model), NT)
        d_up = (d_act * slope_s[slot].astype(F32)).astype(BF)
        slope_s[slot] = d_up
        small[0, pl.ds(6 + f, 1), :] = jnp.sum(d_up.astype(F32), axis=0, keepdims=True)
        reduce.free_g(u + 1)
        reduce.g[1] = product(hidden_ref[...], slope_s[slot], TN).astype(BF).reshape(block)
        tick(u + 1)
        up_c.wait()
        acc[...] += product(slope_s[slot], w_s[2 + slot].reshape(model, model), NT)
        return carry

    lax.fori_loop(0, 4, mlp_step, 0)

    proj_load(jnp.int32(0)).start()
    normal_load.wait()
    normal1 = wide[...]
    small[0, 3:4] = jnp.sum(acc[...] * normal1, axis=0, keepdims=True)
    small[0, 4:5] = jnp.sum(acc[...], axis=0, keepdims=True)
    d_first = norm_back(acc[...], normal1, inverse1_ref[:, 0:1], vec_ref[1:2])
    acc[...] = d_first
    d1_s[...] = d_first.astype(BF)
    small[0, 5:6] = jnp.sum(d_first, axis=0, keepdims=True)
    reduce.fold_core(jnp.int32(7))
    reduce.fold_corner(jnp.int32(6))
    fold_sides(jnp.int32(5))
    x_load.wait()

    def kv_copy(i, pair):
        slot = lax.rem(i, 2)
        return remote(
            kv_send.at[slot, pair], kv_recv.at[i, pair], kv_ssem, kv_rsem, 2 * i + pair, p.to_z(1)
        )

    def wide_at(slot, n, pair):
        return pl.ds(pl.multiple_of((2 * slot + n) * width + pair * PAIR, PAIR), PAIR)

    def attend_back(i):
        slot = lax.rem(i, 2)
        g = group_at(i)
        length = len_ref[seq]
        d_att[...] = product(d1_s[...], w_out[slot].reshape(width, model), NT).astype(BF)
        key_slot = lax.broadcasted_iota(jnp.int32, (LEN, rows), 0)
        lane = lax.broadcasted_iota(jnp.int32, (rows, PAIR), 1)
        for pair in range(width // PAIR):
            cols = slice(pair * PAIR, (pair + 1) * PAIR)
            keys, values, queries = k_s[slot, :, cols], v_s[slot, :, cols], q_s[slot, :, cols]
            d_out = d_att[:, cols]
            inner_all = (d_out.astype(F32) * o_s[slot, :, cols].astype(F32)).T
            value_part, key_part, query_parts = None, None, []
            for head in range(2):
                mine = (lane >= HD) == (head == 1)
                own_q = jnp.where(mine, queries, jnp.zeros_like(queries))
                own_d = jnp.where(mine, d_out, jnp.zeros_like(d_out))
                inner = jnp.sum(inner_all[head * HD : (head + 1) * HD], axis=0, keepdims=True)
                scores = jnp.where(key_slot < length, product(keys, own_q, NT), -1e30)
                probs = jnp.exp(scores - lse_ref[g, pl.ds(pair * 2 + head, 1), :])
                d_probs = product(values, own_d, NT)
                d_scores = (probs * (d_probs - inner) * HD ** (-0.5)).astype(BF)
                d_values = product(probs.astype(BF), own_d)
                d_keys = product(d_scores, own_q)
                value_part = d_values if head == 0 else value_part + d_values
                key_part = d_keys if head == 0 else key_part + d_keys
                query_parts.append(product(keys, d_scores, TN)[head * HD : (head + 1) * HD])
            kv_temp[0] = key_part * HD**0.5
            kv_temp[1] = value_part
            d_all[slot, :, cols] = jnp.concatenate(query_parts, axis=0).T.astype(BF)
            pl.when(i >= 2)(lambda: kv_copy(i - 2, pair).wait_send())
            for n in range(2):
                wide[:, wide_at(slot, n, pair)] = kv_temp[n, pl.ds(own_at, rows), :]
                kv_send[slot, pair, n] = kv_temp[n, pl.ds(other_at, rows), :].astype(BF)
            kv_copy(i, pair).start()

    def finish_group(i, u):
        slot = lax.rem(i, 2)
        g = group_at(i)
        for pair in range(width // PAIR):
            kv_copy(i, pair).wait_recv()
            for n in range(2):
                at = (n + 1) * width + pair * PAIR
                both = wide[:, wide_at(slot, n, pair)] + kv_recv[i, pair, n].astype(F32)
                d_all[slot, :, at : at + PAIR] = both.astype(BF)
        grad = d_all[slot]
        small[0, pl.ds(10 + g, 1), 0 : 3 * width] = jnp.sum(
            grad.astype(F32), axis=0, keepdims=True
        )
        pl.when(u >= 2)(lambda: reduce.core_copy(u - 2).wait_send())
        g_slot = lax.rem(u, 2)
        part = (4, 2, model // GROUP)
        reduce.g[g_slot, :, :, :, 0 : 3 * width] = (
            product(x_own[...], grad, TN).astype(BF).reshape(part + (3 * width,))
        )
        reduce.g[g_slot, :, :, :, 3 * width :] = (
            product(d1_s[...], o_s[slot], TN).astype(BF).reshape(part + (width,))
        )
        reduce.send(u)
        proj_load(i).wait()
        weights = w_s[slot, :, :, :, 0 : 3 * width].reshape(model, 3 * width)
        acc[...] += product(grad, weights, NT)

    def proj_step(u):
        return mix(p.t, group_at(jnp.int32(u - 8)))

    def fold_proj_sides(u):
        if u - 3 >= 8:
            old_step = proj_step(u - 3)
            before = (jnp.int32(PROJ), old_step, old_step != 0)
        else:
            array, old_step = unit_of(jnp.int32(u - 3))
            before = (array, old_step, old_step != 0)
        reduce.fold_sides(jnp.int32(u), jnp.int32(PROJ), proj_step(u), before)

    def on(i, at, action):
        pl.when(i == at)(action)

    def att_step(i, carry):
        end(att_loads(i))
        attend_back(i)

        def zero():
            reduce.fold_corner(jnp.int32(7))
            fold_sides(jnp.int32(6))
            reduce.finish(DOWN, down_grad, misc.at[3])
            spreads[DOWN].first(0)

        def two():
            reduce.fold_core(jnp.int32(8))

        def three():
            reduce.fold_core(jnp.int32(9))
            reduce.fold_corner(jnp.int32(8))

        on(i, 0, zero)
        on(i, 2, two)
        on(i, 3, three)
        pl.when(i >= 1)(lambda: finish_group(i - 1, i + 7))

        def next_loads():
            begin(att_loads(i + 1))
            proj_load(i + 1).start()

        pl.when(i < 3)(next_loads)

        def after_one():
            fold_sides(jnp.int32(7))
            spreads[DOWN].second(0)
            reduce.finish(UP, up_grad, misc.at[4])
            spreads[UP].first(0)

        def after_two():
            spreads[DOWN].third(0)
            spreads[UP].second(0)

        def after_three():
            fold_proj_sides(8)
            spreads[DOWN].arrived(0)
            spreads[UP].third(0)

        on(i, 1, after_one)
        on(i, 2, after_two)
        on(i, 3, after_three)
        return carry

    lax.fori_loop(0, 4, att_step, 0)
    reduce.fold_core(jnp.int32(10))
    reduce.fold_corner(jnp.int32(9))
    finish_group(jnp.int32(3), jnp.int32(11))
    peers = [p.to_core, p.to_x, p.to_y, p.to_z(1), p.to_z(2)]

    def small_copy(n):
        return remote(small.at[n], small_recv.at[n], small_ssem, small_rsem, n, peers[n])

    def small_next(n):
        small_copy(n).wait_recv()
        small[n + 1] = small[n] + small_recv[n]
        if n < 4:
            small_copy(n + 1).start()

    small_copy(0).start()
    fold_proj_sides(9)
    reduce.fold_core(jnp.int32(11))
    reduce.fold_corner(jnp.int32(10))
    small_next(0)
    fold_proj_sides(10)
    reduce.fold_corner(jnp.int32(11))
    small_next(1)
    spreads[UP].arrived(0)
    fold_proj_sides(11)
    reduce.finish(PROJ, proj_grad, misc.at[5])
    spreads[PROJ].first(0)
    small_next(2)
    spreads[PROJ].second(0)
    small_next(3)
    spreads[PROJ].third(0)
    small_next(4)
    sums_ref[...] = small[5]
    spreads[PROJ].arrived(0)

    for u in (10, 11):
        reduce.core_copy(jnp.int32(u)).wait_send()
    for u in (9, 10, 11):
        for copy in reduce.side_copies(jnp.int32(u)) + reduce.corner_copies(jnp.int32(u)):
            copy.wait_send()
    for u in (9, 10, 11):
        last = reduce.z_copy(jnp.int32(u), jnp.int32(PROJ), proj_step(u))
        pl.when(proj_step(u) != 0)(last.wait_send)
    for i in (2, 3):
        for pair in range(width // PAIR):
            kv_copy(jnp.int32(i), pair).wait_send()
    for n in range(5):
        small_copy(n).wait_send()
    for spread in spreads:
        spread.finish(0)


def run_backward(lengths, x, vec, saved):
    (
        qkv_full,
        out_full,
        up_full,
        down_full,
        q,
        k,
        v,
        o,
        act,
        slope,
        _,
        d_second,
        normal1,
        inverse1,
        hidden,
        lse,
        sums,
    ) = saved
    T, rows, width = q.shape
    model = x.shape[1]
    piece = model // GROUP
    anyw = pl.BlockSpec(memory_space=pl.ANY)
    vmem = pl.BlockSpec(memory_space=pltpu.VMEM)
    smem = pl.BlockSpec(memory_space=pltpu.SMEM)
    grad = jax.ShapeDtypeStruct((1, 4, 2, piece, model), BF)
    dma = pltpu.SemaphoreType.DMA
    return pl.pallas_call(
        backward_kernel,
        in_specs=[smem, anyw, vmem, vmem] + [anyw] * 12 + [vmem] * 3,
        out_specs=[anyw] * 3 + [vmem] * 2,
        out_shape=[grad] * 3
        + [jax.ShapeDtypeStruct((rows, model), F32), jax.ShapeDtypeStruct((16, model), F32)],
        scratch_shapes=[
            pltpu.VMEM((4, 4, 2, piece, model), BF),
            pltpu.VMEM((2,) + out_full.shape[1:], BF),
            pltpu.VMEM((2, rows, model), BF),
            pltpu.VMEM((2, rows, model), BF),
            pltpu.VMEM((rows, model), BF),
            pltpu.VMEM((rows, model), BF),
            pltpu.VMEM((rows, model), BF),
            pltpu.VMEM((2, rows, width), BF),
            pltpu.VMEM((2, LEN, width), BF),
            pltpu.VMEM((2, LEN, width), BF),
            pltpu.VMEM((2, rows, width), BF),
            pltpu.VMEM((rows, width), BF),
            pltpu.VMEM((2, LEN, PAIR), F32),
            pltpu.VMEM((rows, model), F32),
            pltpu.VMEM((2, width // PAIR, 2, rows, PAIR), BF),
            pltpu.VMEM((4, width // PAIR, 2, rows, PAIR), BF),
            pltpu.VMEM((2, rows, 3 * width), BF),
            pltpu.VMEM((6, 16, model), F32),
            pltpu.VMEM((5, 16, model), F32),
            dma((16,)),
            dma((24,)),
            dma((6,)),
            dma((8,)),
            dma((8,)),
            dma((5,)),
            dma((5,)),
            *Reduce.scratch(piece, model, 3),
            *Reduce.semaphores(12),
            *Spread.scratch(3),
        ],
        compiler_params=pltpu.CompilerParams(
            collective_id=1, has_side_effects=True, vmem_limit_bytes=VMEM_LIMIT
        ),
        cost_estimate=pl.CostEstimate(
            flops=60 * 10**9, bytes_accessed=80 << 20, transcendentals=8 << 20
        ),
        name="backward",
    )(
        lengths,
        x,
        vec,
        sums,
        qkv_full,
        out_full,
        up_full,
        down_full,
        q,
        k,
        v,
        o,
        act,
        slope,
        d_second,
        normal1,
        inverse1,
        hidden,
        lse,
    )


def on_device(
    inputs,
    cotangent,
    lengths,
    query_weight,
    key_weight,
    value_weight,
    query_bias,
    value_bias,
    out_weight,
    out_bias,
    norm1_gain,
    norm1_bias,
    up_weight,
    up_bias,
    down_weight,
    down_bias,
    norm2_gain,
    norm2_bias,
):
    t = lax.axis_index("tensor")
    model = inputs.shape[1]
    width = out_weight.shape[0]
    zero_row = jnp.zeros((model,), F32)
    vec = jnp.stack(
        [out_bias, norm1_gain, norm1_bias, down_bias, norm2_gain, norm2_bias, zero_row, zero_row]
    )
    small = jnp.stack(
        [jnp.concatenate([query_bias, value_bias, zero_row[2 * width :]]), up_bias] + [zero_row] * 6
    )
    saved = run_forward(
        lengths,
        inputs,
        cotangent,
        vec,
        small,
        query_weight,
        key_weight,
        value_weight,
        out_weight,
        up_weight,
        down_weight,
    )
    down_grad, up_grad, proj_grad, input_grad, sums = run_backward(lengths, inputs, vec, saved)
    grads = [g.reshape(model, model).astype(F32) for g in (down_grad, up_grad, proj_grad)]
    size = lax.axis_size("dp")
    if size > GROUP:
        groups = [list(range(first, size, GROUP)) for first in range(GROUP)]
        *grads, sums = lax.psum((*grads, sums), "dp", axis_index_groups=groups)
    down_grad, up_grad, proj_grad = grads
    up_bias_grad = lax.dynamic_index_in_dim(sums[6:10], t, 0, keepdims=False)
    proj_bias = lax.dynamic_index_in_dim(sums[10:14], t, 0, keepdims=False)
    return (
        saved[10],
        input_grad,
        proj_grad[:, :width],
        proj_grad[:, width : 2 * width],
        proj_grad[:, 2 * width : 3 * width],
        proj_bias[:width],
        proj_bias[2 * width : 3 * width],
        proj_grad[:, 3 * width :].T,
        sums[5],
        sums[3],
        sums[4],
        up_grad,
        up_bias_grad,
        down_grad,
        sums[2],
        sums[0],
        sums[1],
    )


def solution(mesh):
    rows = P(("dp", "tensor"), None)
    by_col = P(None, "tensor")
    by_row = P("tensor", None)
    split = P("tensor")
    whole = P()
    return jax.shard_map(
        on_device,
        mesh=mesh,
        in_specs=(
            P("dp", None),
            rows,
            P("dp"),
            by_col,
            by_col,
            by_col,
            split,
            split,
            by_row,
            whole,
            whole,
            whole,
            by_col,
            split,
            by_row,
            whole,
            whole,
            whole,
        ),
        out_specs=(
            rows,
            rows,
            by_col,
            by_col,
            by_col,
            split,
            split,
            by_row,
            whole,
            whole,
            whole,
            by_col,
            split,
            by_row,
            whole,
            whole,
            whole,
        ),
        check_vma=False,
    )
```

```python
import functools

import jax
import jax.numpy as jnp
from jax import lax
from jax.experimental import pallas as pl
from jax.experimental.pallas import tpu as pltpu
from jax.sharding import PartitionSpec as P

HD = 64
LEN = 1024
PAIR = 2 * HD
GROUP = 8
F32 = jnp.float32
BF = jnp.bfloat16
NN = (((1,), (0,)), ((), ()))
NT = (((1,), (1,)), ((), ()))
TN = (((0,), (0,)), ((), ()))
MESH = pl.DeviceIdType.MESH
VMEM_LIMIT = 62 << 20


def product(left, right, dims=NN):
    return lax.dot_general(left, right, dims, preferred_element_type=F32)


def flip(index, bit):
    return index + bit * (1 - 2 * lax.rem(lax.div(index, bit), 2))


def mix(index, step):
    low = lax.rem(index + step, 2)
    high = lax.rem(lax.div(index, 2) + lax.div(step, 2), 2)
    return 2 * high + low


class Place:
    def __init__(self):
        self.dp = lax.axis_index("dp")
        self.t = lax.axis_index("tensor")
        self.e = lax.rem(self.dp, GROUP)
        self.core = lax.rem(self.e, 2)
        self.quad = lax.div(self.e, 2)
        self.to_core = (flip(self.dp, 1), self.t)
        self.to_x = (flip(self.dp, 2), self.t)
        self.to_y = (flip(self.dp, 4), self.t)
        self.quad_x = flip(self.quad, 1)
        self.quad_y = flip(self.quad, 2)
        self.quad_xy = flip(self.quad_x, 2)

    def to_z(self, step):
        return (self.dp, mix(self.t, jnp.int32(step)))

    def greet(self):
        barrier = pltpu.get_barrier_semaphore()
        peers = [self.to_core, self.to_x, self.to_y, self.to_z(1), self.to_z(2), self.to_z(3)]
        for peer in peers:
            pl.semaphore_signal(barrier, inc=1, device_id=peer, device_id_type=MESH)
        pl.semaphore_wait(barrier, len(peers))


def remote(src, dst, send, recv, index, device):
    return pltpu.make_async_remote_copy(
        src_ref=src,
        dst_ref=dst,
        send_sem=send.at[index],
        recv_sem=recv.at[index],
        device_id=device,
        device_id_type=MESH,
    )


class Spread:
    def __init__(self, place, full, sems, index):
        self.p = place
        self.full = full
        self.sems = sems
        self.index = index

    def block(self, step):
        return mix(self.p.t, jnp.int32(step)) if step else self.p.t

    def slot(self, step):
        return self.index * 4 + step

    def x_copy(self, step):
        p = self.p
        ref = self.full.at[self.block(step), p.quad, p.core]
        return remote(ref, ref, self.sems[0], self.sems[1], self.slot(step), p.to_x)

    def y_copy(self, step):
        p = self.p
        ref = self.full.at[self.block(step), p.quad, p.core]
        return remote(ref, ref, self.sems[2], self.sems[3], self.slot(step), p.to_y)

    def half_copies(self, step):
        p = self.p
        half = self.full.shape[3] // 2
        first = self.full.at[self.block(step), p.quad_x, p.core, pl.ds(0, half)]
        second = self.full.at[self.block(step), p.quad_y, p.core, pl.ds(half, half)]
        return (
            remote(first, first, self.sems[4], self.sems[5], self.slot(step), p.to_y),
            remote(second, second, self.sems[6], self.sems[7], self.slot(step), p.to_x),
        )

    def core_copy(self, step):
        p = self.p
        ref = self.full.at[self.block(step), :, p.core]
        return remote(ref, ref, self.sems[8], self.sems[9], self.slot(step), p.to_core)

    def first(self, step):
        self.x_copy(step).start()
        self.y_copy(step).start()

    def second(self, step):
        self.x_copy(step).wait_recv()
        self.y_copy(step).wait_recv()
        for copy in self.half_copies(step):
            copy.start()

    def third(self, step):
        for copy in self.half_copies(step):
            copy.wait_recv()
        self.core_copy(step).start()

    def arrived(self, step):
        self.core_copy(step).wait_recv()

    def finish(self, step):
        self.x_copy(step).wait_send()
        self.y_copy(step).wait_send()
        for copy in self.half_copies(step):
            copy.wait_send()
        self.core_copy(step).wait_send()

    @staticmethod
    def scratch(count):
        return [pltpu.SemaphoreType.DMA((4 * count,))] * 10


def norm_center(values):
    center = values - jnp.mean(values, axis=-1, keepdims=True)
    inverse = lax.rsqrt(jnp.mean(center * center, axis=-1, keepdims=True) + 1e-05)
    return center * inverse, inverse


def norm_back(grad, normal, inverse, gain):
    scaled = grad * gain
    first_mean = jnp.mean(scaled, axis=-1, keepdims=True)
    second_mean = jnp.mean(scaled * normal, axis=-1, keepdims=True)
    return inverse * (scaled - first_mean - normal * second_mean)


def forward_kernel(
    len_ref,
    x_hbm,
    cot_ref,
    vec_ref,
    small_ref,
    wq_hbm,
    wk_hbm,
    wv_hbm,
    wo_hbm,
    wu_hbm,
    wd_hbm,
    qkv_full,
    out_full,
    up_full,
    down_full,
    q_hbm,
    k_hbm,
    v_hbm,
    o_hbm,
    act_hbm,
    slope_hbm,
    outputs_ref,
    d_second_ref,
    normal1_ref,
    inverse1_ref,
    hidden_ref,
    lse_ref,
    sums_ref,
    x_seq,
    small_all,
    w_qkv,
    w_out,
    w_up,
    w_down,
    q_s,
    k_s,
    v_s,
    o_s,
    act_s,
    slope_s,
    acc,
    z_send,
    z_recv,
    small_send,
    small_recv,
    local,
    load,
    save,
    *spread_sems,
):
    p = Place()
    rows, model = acc.shape
    width = q_s.shape[2]
    half_index = lax.rem(p.t, 2)
    seq = lax.div(p.t, 2)
    own_rows = pl.ds(pl.multiple_of(half_index * rows, rows), rows)
    fulls = [qkv_full, out_full, up_full, down_full]
    spreads = [Spread(p, full, spread_sems, i) for i, full in enumerate(fulls)]
    QKV, OUT, UP, DOWN = range(4)

    x_load = pltpu.make_async_copy(
        x_hbm.at[pl.ds(pl.multiple_of(seq * LEN, LEN), LEN)], x_seq, local.at[0]
    )
    own_loads = [
        pltpu.make_async_copy(w, w_qkv.at[0, :, :, :, pl.ds(i * width, width)], local.at[1 + i])
        for i, w in enumerate((wq_hbm, wk_hbm, wv_hbm))
    ]
    x_load.start()
    for copy in own_loads:
        copy.start()
    out_loads = [pltpu.make_async_copy(wo_hbm, w_out.at[0], local.at[4])]
    up_load = pltpu.make_async_copy(wu_hbm, w_up.at[0], local.at[5])
    down_load = pltpu.make_async_copy(wd_hbm, w_down.at[0], local.at[6])
    own_saves = [
        pltpu.make_async_copy(w_qkv.at[0], qkv_full.at[p.t], local.at[7]),
        pltpu.make_async_copy(w_out.at[0], out_full.at[p.t], local.at[8]),
        pltpu.make_async_copy(w_up.at[0], up_full.at[p.t], local.at[9]),
        pltpu.make_async_copy(w_down.at[0], down_full.at[p.t], local.at[10]),
    ]

    p.greet()

    def z_copies(array, step):
        slot = array * 4 + step
        if array == QKV:
            return [
                remote(
                    w.at[p.quad, p.core],
                    qkv_full.at[p.t, p.quad, p.core, :, pl.ds(i * width, width)],
                    z_send,
                    z_recv,
                    slot if i == 0 else 16 + 4 * (i - 1) + step,
                    p.to_z(step),
                )
                for i, w in enumerate((wq_hbm, wk_hbm, wv_hbm))
            ]
        w = (None, wo_hbm, wu_hbm, wd_hbm)[array]
        return [
            remote(
                w.at[p.quad, p.core],
                fulls[array].at[p.t, p.quad, p.core],
                z_send,
                z_recv,
                slot,
                p.to_z(step),
            )
        ]

    def small_copy(step):
        return remote(
            small_ref, small_all.at[p.t], small_send, small_recv, step, p.to_z(step)
        )

    def z_start(array, step):
        for copy in z_copies(array, step):
            copy.start()

    def z_sent(array, step):
        for copy in z_copies(array, step):
            copy.wait_send()

    def z_first(array, step):
        for copy in z_copies(array, step):
            copy.wait_recv()
        spreads[array].first(step)

    small_all[p.t] = small_ref[...]
    for step in (1, 2, 3):
        small_copy(step).start()
    for array in (QKV, OUT, UP, DOWN):
        for step in (1, 2, 3):
            z_start(array, step)

    def load_copy(array, step):
        vmem = (w_qkv, w_out, w_up, w_down)[array]
        return pltpu.make_async_copy(
            fulls[array].at[mix(p.t, jnp.int32(step))],
            vmem.at[step % 2 if array == QKV else step],
            load.at[array * 4 + step],
        )

    def attend(step):
        group = mix(p.t, step)
        slot = lax.rem(step, 2)
        weights = w_qkv[slot].reshape(model, 3 * width)
        bias = small_all[group, 0:1]
        x_own = x_seq[own_rows, :]
        queries = (product(x_own, weights[:, :width]) + bias[:, :width]).astype(BF)
        q_s[step] = (queries.astype(F32) * HD ** (-0.5)).astype(BF)
        k_s[step] = product(x_seq[...], weights[:, width : 2 * width]).astype(BF)
        v_s[step] = (
            product(x_seq[...], weights[:, 2 * width :]) + bias[:, width : 2 * width]
        ).astype(BF)
        passed(step, "start")
        length = len_ref[seq]
        key_slot = lax.broadcasted_iota(jnp.int32, (LEN, rows), 0)
        lane = lax.broadcasted_iota(jnp.int32, (rows, PAIR), 1)
        for pair in range(width // PAIR):
            if pair == 1:
                passed(step, "mid")
            cols = slice(pair * PAIR, (pair + 1) * PAIR)
            keys, values, q_pair = k_s[step, :, cols], v_s[step, :, cols], q_s[step, :, cols]
            parts = []
            for head in range(2):
                mine = jnp.where((lane >= HD) == (head == 1), q_pair, jnp.zeros_like(q_pair))
                scores = jnp.where(key_slot < length, product(keys, mine, NT), -1e30)
                top = jnp.max(scores, axis=0, keepdims=True)
                exponent = jnp.exp(scores - top)
                total = jnp.sum(exponent, axis=0, keepdims=True)
                mixed = product(values, exponent.astype(BF), TN)
                parts.append(mixed[head * HD : (head + 1) * HD] * (1.0 / total))
                lse_ref[group, pl.ds(pair * 2 + head, 1), :] = top + jnp.log(total)
            o_s[step, :, cols] = jnp.concatenate(parts, axis=0).T.astype(BF)

    def attend_saves(step):
        group = mix(p.t, jnp.int32(step))
        pairs = ((q_s, q_hbm), (k_s, k_hbm), (v_s, v_hbm), (o_s, o_hbm))
        return [
            pltpu.make_async_copy(vmem.at[step], hbm.at[group], save.at[4 * step + i])
            for i, (vmem, hbm) in enumerate(pairs)
        ]

    def on(step, at, action):
        @pl.when(step == at)
        def _():
            action()

    x_load.wait()
    for copy in own_loads:
        copy.wait()
    own_saves[0].start()
    out_loads[0].start()
    up_load.start()
    down_load.start()
    for step in (1, 2, 3):
        small_copy(step).wait_recv()

    def relay(plan):
        for array, legs in plan:
            spread = spreads[array]
            for leg in legs.split():
                kind, step = leg[0], int(leg[1])
                if kind == "f":
                    z_first(array, step)
                elif kind == "s":
                    spread.second(step)
                elif kind == "t":
                    spread.third(step)
                else:
                    spread.arrived(step)
                    load_copy(array, step).start()

    def passed(step, place):
        plans = {
            (0, "end"): [
                (QKV, "f1 f2 s1 f3 s2"),
                (OUT, "f1"),
                (QKV, "t1"),
                (OUT, "f2 f3"),
                (QKV, "a1 s3"),
            ],
            (1, "mid"): [(QKV, "t2"), (OUT, "s1")],
            (1, "end"): [(OUT, "s2 s3"), (UP, "f1"), (QKV, "a2")],
            (2, "start"): [(QKV, "t3"), (OUT, "t1 t2")],
            (2, "mid"): [(OUT, "t3")],
            (2, "end"): [(QKV, "a3"), (OUT, "a1 a2 a3"), (UP, "f2")],
            (3, "start"): [(UP, "s1 f3")],
            (3, "end"): [(UP, "s2")],
        }
        for (at, where), plan in plans.items():
            if where == place:
                on(step, at, lambda plan=plan: relay(plan))

    def attend_step(step, carry):
        for i in (1, 2, 3):
            on(step, i, load_copy(QKV, i).wait)
        attend(step)
        for i in range(4):
            on(step, i, lambda i=i: [copy.start() for copy in attend_saves(i)])
        on(step, 1, own_saves[0].wait)
        passed(step, "end")
        return carry

    lax.fori_loop(0, 4, attend_step, 0)

    out_loads[0].wait()
    own_saves[1].start()
    for step in (1, 2, 3):
        load_copy(OUT, step).wait()
    total = x_seq[own_rows, :].astype(F32) + vec_ref[0:1]
    for step in range(4):
        total = total + product(o_s[step], w_out[step].reshape(width, model))
    normal1, inverse1 = norm_center(total)
    normal1_ref[...] = normal1
    inverse1_ref[...] = jnp.broadcast_to(inverse1, inverse1_ref.shape)
    normed1 = normal1 * vec_ref[1:2] + vec_ref[2:3]
    hidden_ref[...] = normed1.astype(BF)
    acc[...] = normed1 + vec_ref[3:4]
    relay([(UP, "t1")])

    def mlp_saves(step):
        part = mix(p.t, jnp.int32(step))
        return [
            pltpu.make_async_copy(act_s.at[step], act_hbm.at[part], save.at[16 + 2 * step]),
            pltpu.make_async_copy(slope_s.at[step], slope_hbm.at[part], save.at[17 + 2 * step]),
        ]

    def up_step(step, carry):
        on(step, 0, lambda: [up_load.wait(), own_saves[2].start()])
        for i in (1, 2, 3):
            on(step, i, load_copy(UP, i).wait)
        weights = w_up[step].reshape(model, model)
        upper = product(hidden_ref[...], weights) + small_all[mix(p.t, step), 1:2]
        cdf = 0.5 * (1.0 + lax.erf(upper * 0.7071067811865476))
        act_s[step] = (upper * cdf).astype(BF)
        density = jnp.exp(-0.5 * upper * upper) * 0.3989422804014327
        slope_s[step] = (cdf + upper * density).astype(BF)
        for i in range(4):
            on(step, i, lambda i=i: [copy.start() for copy in mlp_saves(i)])

        on(step, 0, lambda: relay([(UP, "a1 s3"), (DOWN, "f1")]))
        on(step, 1, lambda: relay([(UP, "t2"), (DOWN, "f2"), (UP, "t3"), (DOWN, "f3"), (UP, "a2")]))
        on(step, 2, lambda: relay([(UP, "a3"), (DOWN, "s1")]))
        on(step, 3, lambda: relay([(DOWN, "s2")]))
        return carry

    lax.fori_loop(0, 4, up_step, 0)

    def down_step(step, carry):
        on(step, 0, lambda: [down_load.wait(), own_saves[3].start()])
        for i in (1, 2, 3):
            on(step, i, load_copy(DOWN, i).wait)
        acc[...] += product(act_s[step], w_down[step].reshape(model, model))

        on(step, 0, lambda: relay([(DOWN, "s3 t1 t2 a1")]))
        on(step, 1, lambda: relay([(DOWN, "t3 a2")]))
        on(step, 2, lambda: relay([(DOWN, "a3")]))
        return carry

    lax.fori_loop(0, 4, down_step, 0)

    normal2, inverse2 = norm_center(acc[...])
    outputs_ref[...] = (normal2 * vec_ref[4:5] + vec_ref[5:6]).astype(BF)
    slot_index = half_index * rows + lax.broadcasted_iota(jnp.int32, (rows, 1), 0)
    grad_out = jnp.where(slot_index < len_ref[seq], cot_ref[...].astype(F32), 0.0)
    d_second = norm_back(grad_out, normal2, inverse2, vec_ref[4:5])
    d_second_ref[...] = d_second
    sums_ref[0:1] = jnp.sum(grad_out * normal2, axis=0, keepdims=True)
    sums_ref[1:2] = jnp.sum(grad_out, axis=0, keepdims=True)
    sums_ref[2:3] = jnp.sum(d_second, axis=0, keepdims=True)
    sums_ref[3:8] = jnp.zeros((5, model), F32)

    for copy in own_saves[1:]:
        copy.wait()
    for step in range(4):
        for copy in attend_saves(step) + mlp_saves(step):
            copy.wait()
    for step in (1, 2, 3):
        small_copy(step).wait_send()
        for array in range(4):
            z_sent(array, step)
            spreads[array].finish(step)


def run_forward(lengths, x, cot, vec, small, wq, wk, wv, wo, wu, wd):
    tensor_size = lax.axis_size("tensor")
    model = x.shape[1]
    rows = x.shape[0] // tensor_size
    width = wo.shape[0]
    pieces = lambda w: w.reshape(4, 2, w.shape[0] // GROUP, w.shape[1])
    anyw = pl.BlockSpec(memory_space=pl.ANY)
    vmem = pl.BlockSpec(memory_space=pltpu.VMEM)
    smem = pl.BlockSpec(memory_space=pltpu.SMEM)
    T = tensor_size
    out = lambda shape, dtype=BF: jax.ShapeDtypeStruct(shape, dtype)
    outs = [
        (out((T, 4, 2, model // GROUP, 3 * width)), anyw),
        (out((T, 4, 2, width // GROUP, model)), anyw),
        (out((T, 4, 2, model // GROUP, wu.shape[1])), anyw),
        (out((T, 4, 2, wd.shape[0] // GROUP, model)), anyw),
        (out((T, rows, width)), anyw),
        (out((T, LEN, width)), anyw),
        (out((T, LEN, width)), anyw),
        (out((T, rows, width)), anyw),
        (out((T, rows, wu.shape[1])), anyw),
        (out((T, rows, wu.shape[1])), anyw),
        (out((rows, model)), vmem),
        (out((rows, model), F32), vmem),
        (out((rows, model), F32), vmem),
        (out((rows, 128), F32), vmem),
        (out((rows, model)), vmem),
        (out((T, 8, rows), F32), vmem),
        (out((8, model), F32), vmem),
    ]
    scratch = [
        pltpu.VMEM((LEN, model), BF),
        pltpu.VMEM((T, 8, model), F32),
        pltpu.VMEM((2, 4, 2, model // GROUP, 3 * width), BF),
        pltpu.VMEM((T, 4, 2, width // GROUP, model), BF),
        pltpu.VMEM((T, 4, 2, model // GROUP, wu.shape[1]), BF),
        pltpu.VMEM((T, 4, 2, wd.shape[0] // GROUP, model), BF),
        pltpu.VMEM((T, rows, width), BF),
        pltpu.VMEM((T, LEN, width), BF),
        pltpu.VMEM((T, LEN, width), BF),
        pltpu.VMEM((T, rows, width), BF),
        pltpu.VMEM((T, rows, wu.shape[1]), BF),
        pltpu.VMEM((T, rows, wu.shape[1]), BF),
        pltpu.VMEM((rows, model), F32),
        pltpu.SemaphoreType.DMA((24,)),
        pltpu.SemaphoreType.DMA((24,)),
        pltpu.SemaphoreType.DMA((4,)),
        pltpu.SemaphoreType.DMA((4,)),
        pltpu.SemaphoreType.DMA((11,)),
        pltpu.SemaphoreType.DMA((16,)),
        pltpu.SemaphoreType.DMA((24,)),
        *Spread.scratch(4),
    ]
    return pl.pallas_call(
        forward_kernel,
        in_specs=[smem, anyw, vmem, vmem, vmem] + [anyw] * 6,
        out_specs=[spec for _, spec in outs],
        out_shape=[shape for shape, _ in outs],
        scratch_shapes=scratch,
        compiler_params=pltpu.CompilerParams(
            collective_id=0, has_side_effects=True, vmem_limit_bytes=VMEM_LIMIT
        ),
        cost_estimate=pl.CostEstimate(
            flops=40 * 10**9, bytes_accessed=60 << 20, transcendentals=16 << 20
        ),
        name="forward",
    )(
        lengths,
        x,
        cot,
        vec,
        small,
        pieces(wq),
        pieces(wk),
        pieces(wv),
        pieces(wo),
        pieces(wu),
        pieces(wd),
    )


class Reduce:
    def __init__(self, place, bufs, sems):
        self.p = place
        self.g, self.s, self.rc, self.ra, self.rb, self.zs, self.rz, self.own = bufs
        self.sems = sems

    @staticmethod
    def scratch(piece, cols, arrays):
        return [
            pltpu.VMEM((2, 4, 2, piece, cols), BF),
            pltpu.VMEM((3, 4, piece, cols), BF),
            pltpu.VMEM((2, 4, piece, cols), BF),
            pltpu.VMEM((3, 2, piece // 2, cols), BF),
            pltpu.VMEM((3, 2, piece, cols), BF),
            pltpu.VMEM((3, piece, cols), BF),
            pltpu.VMEM((arrays, 4, piece, cols), BF),
            pltpu.VMEM((arrays, piece, cols), BF),
        ]

    @staticmethod
    def semaphores(units):
        return [pltpu.SemaphoreType.DMA((units,))] * 12

    def core_copy(self, u):
        other = 1 - self.p.core
        return remote(
            self.g.at[lax.rem(u, 2), :, other],
            self.rc.at[lax.rem(u, 2)],
            self.sems[0],
            self.sems[1],
            u,
            self.p.to_core,
        )

    def corner_copies(self, u):
        p, slot = self.p, lax.rem(u, 3)
        half = self.ra.shape[2]
        return (
            remote(
                self.s.at[slot, p.quad_xy, pl.ds(0, half)],
                self.ra.at[slot, 0],
                self.sems[2],
                self.sems[3],
                u,
                p.to_y,
            ),
            remote(
                self.s.at[slot, p.quad_xy, pl.ds(half, half)],
                self.ra.at[slot, 1],
                self.sems[4],
                self.sems[5],
                u,
                p.to_x,
            ),
        )

    def side_copies(self, u):
        p, slot = self.p, lax.rem(u, 3)
        return (
            remote(
                self.s.at[slot, p.quad_x], self.rb.at[slot, 0], self.sems[6], self.sems[7], u, p.to_x
            ),
            remote(
                self.s.at[slot, p.quad_y], self.rb.at[slot, 1], self.sems[8], self.sems[9], u, p.to_y
            ),
        )

    def z_copy(self, u, array, step):
        return remote(
            self.zs.at[lax.rem(u, 3)],
            self.rz.at[array, step],
            self.sems[10],
            self.sems[11],
            array * 4 + step,
            (self.p.dp, mix(self.p.t, step)),
        )

    def free_g(self, u):
        if not isinstance(u, int):
            pl.when(u >= 2)(lambda: self.core_copy(u - 2).wait_send())
        elif u >= 2:
            self.core_copy(jnp.int32(u - 2)).wait_send()

    def send(self, u):
        self.core_copy(u).start()

    def fold_core(self, u):
        slot = lax.rem(u, 3)

        def freed():
            for copy in self.side_copies(u - 3) + self.corner_copies(u - 3):
                copy.wait_send()

        pl.when(u >= 3)(freed)
        self.core_copy(u).wait_recv()
        mine = self.g[lax.rem(u, 2), :, self.p.core].astype(F32)
        self.s[slot] = (mine + self.rc[lax.rem(u, 2)].astype(F32)).astype(BF)
        for copy in self.corner_copies(u):
            copy.start()

    def fold_corner(self, u):
        p, slot = self.p, lax.rem(u, 3)
        half = self.ra.shape[2]
        for copy in self.corner_copies(u):
            copy.wait_recv()
        lower = self.s[slot, p.quad_x, :half].astype(F32) + self.ra[slot, 0].astype(F32)
        self.s[slot, p.quad_x, :half] = lower.astype(BF)
        upper = self.s[slot, p.quad_y, half:].astype(F32) + self.ra[slot, 1].astype(F32)
        self.s[slot, p.quad_y, half:] = upper.astype(BF)
        for copy in self.side_copies(u):
            copy.start()

    def fold_sides(self, u, array, step, before):
        p, slot = self.p, lax.rem(u, 3)
        for copy in self.side_copies(u):
            copy.wait_recv()
        total = (
            self.s[slot, p.quad].astype(F32)
            + self.rb[slot, 0].astype(F32)
            + self.rb[slot, 1].astype(F32)
        ).astype(BF)

        if before is not None:
            old_array, old_step, valid = before
            pl.when(valid)(lambda: self.z_copy(u - 3, old_array, old_step).wait_send())

        def store():
            self.own[array] = total

        def pass_on():
            self.zs[slot] = total
            self.z_copy(u, array, step).start()

        pl.when(step == 0)(store)
        pl.when(step != 0)(pass_on)

    def finish(self, array, out, sem):
        total = self.own[array].astype(F32)
        for step in (1, 2, 3):
            self.z_copy(jnp.int32(0), jnp.int32(array), jnp.int32(step)).wait_recv()
            total = total + self.rz[array, step].astype(F32)
        self.own[array] = total.astype(BF)
        copy = pltpu.make_async_copy(self.own.at[array], out.at[0, self.p.quad, self.p.core], sem)
        copy.start()
        copy.wait()


def backward_kernel(
    len_ref,
    x_hbm,
    vec_ref,
    sums_in,
    qkv_full,
    out_full,
    up_full,
    down_full,
    q_hbm,
    k_hbm,
    v_hbm,
    o_hbm,
    act_hbm,
    slope_hbm,
    d_second_hbm,
    normal1_hbm,
    inverse1_ref,
    hidden_ref,
    lse_ref,
    down_grad,
    up_grad,
    proj_grad,
    acc,
    sums_ref,
    w_s,
    w_out,
    act_s,
    slope_s,
    d2_s,
    d1_s,
    x_own,
    q_s,
    k_s,
    v_s,
    o_s,
    d_att,
    kv_temp,
    wide,
    kv_send,
    kv_recv,
    d_all,
    small,
    small_recv,
    load,
    att_load,
    misc,
    kv_ssem,
    kv_rsem,
    small_ssem,
    small_rsem,
    *rest,
):
    p = Place()
    reduce = Reduce(p, rest[:8], rest[8:20])
    spread_sems = rest[20:]
    rows, model = acc.shape
    width = q_s.shape[2]
    half_index = lax.rem(p.t, 2)
    seq = lax.div(p.t, 2)
    own_at = pl.multiple_of(half_index * rows, rows)
    other_at = pl.multiple_of((1 - half_index) * rows, rows)
    grads = (down_grad, up_grad, proj_grad)
    spreads = [Spread(p, grad, spread_sems, i) for i, grad in enumerate(grads)]
    for spread in spreads:
        spread.block = lambda step: 0
    DOWN, UP, PROJ = range(3)

    acc_load = pltpu.make_async_copy(d_second_hbm, acc, misc.at[0])
    x_load = pltpu.make_async_copy(
        x_hbm.at[pl.ds(pl.multiple_of(p.t * rows, rows), rows)], x_own, misc.at[1]
    )
    normal_load = pltpu.make_async_copy(normal1_hbm, wide, misc.at[2])

    def mlp_loads(i):
        f, slot = mix(p.t, 3 - i), lax.rem(i, 2)
        pairs = (
            (act_hbm.at[f], act_s.at[slot]),
            (down_full.at[f], w_s.at[slot]),
            (slope_hbm.at[f], slope_s.at[slot]),
            (up_full.at[f], w_s.at[2 + slot]),
        )
        return [
            pltpu.make_async_copy(src, dst, load.at[4 * i + n]) for n, (src, dst) in enumerate(pairs)
        ]

    def group_at(i):
        return 2 * lax.rem(lax.div(p.t, 2) + 1 + lax.div(i, 2), 2) + lax.rem(i, 2)

    def att_loads(i):
        g, slot = group_at(i), lax.rem(i, 2)
        pairs = (
            (q_hbm.at[g], q_s.at[slot]),
            (k_hbm.at[g], k_s.at[slot]),
            (v_hbm.at[g], v_s.at[slot]),
            (o_hbm.at[g], o_s.at[slot]),
            (out_full.at[g], w_out.at[slot]),
        )
        return [
            pltpu.make_async_copy(src, dst, att_load.at[6 * i + n])
            for n, (src, dst) in enumerate(pairs)
        ]

    def proj_load(i):
        g, slot = group_at(i), lax.rem(i, 2)
        return pltpu.make_async_copy(
            qkv_full.at[g], w_s.at[slot, :, :, :, pl.ds(0, 3 * width)], att_load.at[6 * i + 5]
        )

    def begin(copies):
        for copy in copies:
            copy.start()

    def end(copies):
        for copy in copies:
            copy.wait()

    acc_load.start()
    begin(mlp_loads(jnp.int32(0)))
    x_load.start()
    normal_load.start()
    begin(att_loads(jnp.int32(0)))
    small[0] = jnp.zeros(small.shape[1:], F32)
    small[0, 0:3] = sums_in[0:3]
    p.greet()
    acc_load.wait()
    d2_s[...] = acc[...].astype(BF)

    def unit_of(u):
        return lax.rem(u, 2), 3 - lax.div(u, 2)

    def fold_sides(u):
        array, step = unit_of(u)
        old_array, old_step = unit_of(jnp.maximum(u - 3, 0))
        reduce.fold_sides(u, array, step, (old_array, old_step, jnp.logical_and(u >= 3, old_step != 0)))

    def tick(u):
        pl.when(u >= 1)(lambda: reduce.fold_core(u - 1))
        reduce.send(u)
        pl.when(u >= 2)(lambda: reduce.fold_corner(u - 2))
        pl.when(u >= 3)(lambda: fold_sides(u - 3))

    block = (4, 2, model // GROUP, model)

    def mlp_step(i, carry):
        slot = lax.rem(i, 2)
        f = mix(p.t, 3 - i)
        pl.when(i < 3)(lambda: begin(mlp_loads(i + 1)))
        act_c, down_c, slope_c, up_c = mlp_loads(i)
        act_c.wait()
        u = 2 * i
        reduce.free_g(u)
        reduce.g[0] = product(act_s[slot], d2_s[...], TN).astype(BF).reshape(block)
        tick(u)
        down_c.wait()
        slope_c.wait()
        d_act = product(d2_s[...], w_s[slot].reshape(model, model), NT)
        d_up = (d_act * slope_s[slot].astype(F32)).astype(BF)
        slope_s[slot] = d_up
        small[0, pl.ds(6 + f, 1), :] = jnp.sum(d_up.astype(F32), axis=0, keepdims=True)
        reduce.free_g(u + 1)
        reduce.g[1] = product(hidden_ref[...], slope_s[slot], TN).astype(BF).reshape(block)
        tick(u + 1)
        up_c.wait()
        acc[...] += product(slope_s[slot], w_s[2 + slot].reshape(model, model), NT)
        return carry

    lax.fori_loop(0, 4, mlp_step, 0)

    proj_load(jnp.int32(0)).start()
    normal_load.wait()
    normal1 = wide[...]
    small[0, 3:4] = jnp.sum(acc[...] * normal1, axis=0, keepdims=True)
    small[0, 4:5] = jnp.sum(acc[...], axis=0, keepdims=True)
    d_first = norm_back(acc[...], normal1, inverse1_ref[:, 0:1], vec_ref[1:2])
    acc[...] = d_first
    d1_s[...] = d_first.astype(BF)
    small[0, 5:6] = jnp.sum(d_first, axis=0, keepdims=True)
    reduce.fold_core(jnp.int32(7))
    reduce.fold_corner(jnp.int32(6))
    fold_sides(jnp.int32(5))
    x_load.wait()

    def kv_copy(i, pair):
        slot = lax.rem(i, 2)
        return remote(
            kv_send.at[slot, pair], kv_recv.at[i, pair], kv_ssem, kv_rsem, 2 * i + pair, p.to_z(1)
        )

    def wide_at(slot, n, pair):
        return pl.ds(pl.multiple_of((2 * slot + n) * width + pair * PAIR, PAIR), PAIR)

    def attend_back(i):
        slot = lax.rem(i, 2)
        g = group_at(i)
        length = len_ref[seq]
        d_att[...] = product(d1_s[...], w_out[slot].reshape(width, model), NT).astype(BF)
        key_slot = lax.broadcasted_iota(jnp.int32, (LEN, rows), 0)
        lane = lax.broadcasted_iota(jnp.int32, (rows, PAIR), 1)
        for pair in range(width // PAIR):
            cols = slice(pair * PAIR, (pair + 1) * PAIR)
            keys, values, queries = k_s[slot, :, cols], v_s[slot, :, cols], q_s[slot, :, cols]
            d_out = d_att[:, cols]
            inner_all = (d_out.astype(F32) * o_s[slot, :, cols].astype(F32)).T
            value_part, key_part, query_parts = None, None, []
            for head in range(2):
                mine = (lane >= HD) == (head == 1)
                own_q = jnp.where(mine, queries, jnp.zeros_like(queries))
                own_d = jnp.where(mine, d_out, jnp.zeros_like(d_out))
                inner = jnp.sum(inner_all[head * HD : (head + 1) * HD], axis=0, keepdims=True)
                scores = jnp.where(key_slot < length, product(keys, own_q, NT), -1e30)
                probs = jnp.exp(scores - lse_ref[g, pl.ds(pair * 2 + head, 1), :])
                d_probs = product(values, own_d, NT)
                d_scores = (probs * (d_probs - inner) * HD ** (-0.5)).astype(BF)
                d_values = product(probs.astype(BF), own_d)
                d_keys = product(d_scores, own_q)
                value_part = d_values if head == 0 else value_part + d_values
                key_part = d_keys if head == 0 else key_part + d_keys
                query_parts.append(product(keys, d_scores, TN)[head * HD : (head + 1) * HD])
            kv_temp[0] = key_part * HD**0.5
            kv_temp[1] = value_part
            d_all[slot, :, cols] = jnp.concatenate(query_parts, axis=0).T.astype(BF)
            pl.when(i >= 2)(lambda: kv_copy(i - 2, pair).wait_send())
            for n in range(2):
                wide[:, wide_at(slot, n, pair)] = kv_temp[n, pl.ds(own_at, rows), :]
                kv_send[slot, pair, n] = kv_temp[n, pl.ds(other_at, rows), :].astype(BF)
            kv_copy(i, pair).start()

    def finish_group(i, u):
        slot = lax.rem(i, 2)
        g = group_at(i)
        for pair in range(width // PAIR):
            kv_copy(i, pair).wait_recv()
            for n in range(2):
                at = (n + 1) * width + pair * PAIR
                both = wide[:, wide_at(slot, n, pair)] + kv_recv[i, pair, n].astype(F32)
                d_all[slot, :, at : at + PAIR] = both.astype(BF)
        grad = d_all[slot]
        small[0, pl.ds(10 + g, 1), 0 : 3 * width] = jnp.sum(
            grad.astype(F32), axis=0, keepdims=True
        )
        pl.when(u >= 2)(lambda: reduce.core_copy(u - 2).wait_send())
        g_slot = lax.rem(u, 2)
        part = (4, 2, model // GROUP)
        reduce.g[g_slot, :, :, :, 0 : 3 * width] = (
            product(x_own[...], grad, TN).astype(BF).reshape(part + (3 * width,))
        )
        reduce.g[g_slot, :, :, :, 3 * width :] = (
            product(d1_s[...], o_s[slot], TN).astype(BF).reshape(part + (width,))
        )
        reduce.send(u)
        proj_load(i).wait()
        weights = w_s[slot, :, :, :, 0 : 3 * width].reshape(model, 3 * width)
        acc[...] += product(grad, weights, NT)

    def proj_step(u):
        return mix(p.t, group_at(jnp.int32(u - 8)))

    def fold_proj_sides(u):
        if u - 3 >= 8:
            old_step = proj_step(u - 3)
            before = (jnp.int32(PROJ), old_step, old_step != 0)
        else:
            array, old_step = unit_of(jnp.int32(u - 3))
            before = (array, old_step, old_step != 0)
        reduce.fold_sides(jnp.int32(u), jnp.int32(PROJ), proj_step(u), before)

    def on(i, at, action):
        pl.when(i == at)(action)

    def att_step(i, carry):
        end(att_loads(i))
        attend_back(i)

        def zero():
            reduce.fold_corner(jnp.int32(7))
            fold_sides(jnp.int32(6))
            reduce.finish(DOWN, down_grad, misc.at[3])
            spreads[DOWN].first(0)

        def two():
            reduce.fold_core(jnp.int32(8))

        def three():
            reduce.fold_core(jnp.int32(9))
            reduce.fold_corner(jnp.int32(8))

        on(i, 0, zero)
        on(i, 2, two)
        on(i, 3, three)
        pl.when(i >= 1)(lambda: finish_group(i - 1, i + 7))

        def next_loads():
            begin(att_loads(i + 1))
            proj_load(i + 1).start()

        pl.when(i < 3)(next_loads)

        def after_one():
            fold_sides(jnp.int32(7))
            spreads[DOWN].second(0)
            reduce.finish(UP, up_grad, misc.at[4])
            spreads[UP].first(0)

        def after_two():
            spreads[DOWN].third(0)
            spreads[UP].second(0)

        def after_three():
            fold_proj_sides(8)
            spreads[DOWN].arrived(0)
            spreads[UP].third(0)

        on(i, 1, after_one)
        on(i, 2, after_two)
        on(i, 3, after_three)
        return carry

    lax.fori_loop(0, 4, att_step, 0)
    reduce.fold_core(jnp.int32(10))
    reduce.fold_corner(jnp.int32(9))
    finish_group(jnp.int32(3), jnp.int32(11))
    peers = [p.to_core, p.to_x, p.to_y, p.to_z(1), p.to_z(2)]

    def small_copy(n):
        return remote(small.at[n], small_recv.at[n], small_ssem, small_rsem, n, peers[n])

    def small_next(n):
        small_copy(n).wait_recv()
        small[n + 1] = small[n] + small_recv[n]
        if n < 4:
            small_copy(n + 1).start()

    small_copy(0).start()
    fold_proj_sides(9)
    reduce.fold_core(jnp.int32(11))
    reduce.fold_corner(jnp.int32(10))
    small_next(0)
    fold_proj_sides(10)
    reduce.fold_corner(jnp.int32(11))
    small_next(1)
    spreads[UP].arrived(0)
    fold_proj_sides(11)
    reduce.finish(PROJ, proj_grad, misc.at[5])
    spreads[PROJ].first(0)
    small_next(2)
    spreads[PROJ].second(0)
    small_next(3)
    spreads[PROJ].third(0)
    small_next(4)
    sums_ref[...] = small[5]
    spreads[PROJ].arrived(0)

    for u in (10, 11):
        reduce.core_copy(jnp.int32(u)).wait_send()
    for u in (9, 10, 11):
        for copy in reduce.side_copies(jnp.int32(u)) + reduce.corner_copies(jnp.int32(u)):
            copy.wait_send()
    for u in (9, 10, 11):
        last = reduce.z_copy(jnp.int32(u), jnp.int32(PROJ), proj_step(u))
        pl.when(proj_step(u) != 0)(last.wait_send)
    for i in (2, 3):
        for pair in range(width // PAIR):
            kv_copy(jnp.int32(i), pair).wait_send()
    for n in range(5):
        small_copy(n).wait_send()
    for spread in spreads:
        spread.finish(0)


def run_backward(lengths, x, vec, saved):
    (
        qkv_full,
        out_full,
        up_full,
        down_full,
        q,
        k,
        v,
        o,
        act,
        slope,
        _,
        d_second,
        normal1,
        inverse1,
        hidden,
        lse,
        sums,
    ) = saved
    T, rows, width = q.shape
    model = x.shape[1]
    piece = model // GROUP
    anyw = pl.BlockSpec(memory_space=pl.ANY)
    vmem = pl.BlockSpec(memory_space=pltpu.VMEM)
    smem = pl.BlockSpec(memory_space=pltpu.SMEM)
    grad = jax.ShapeDtypeStruct((1, 4, 2, piece, model), BF)
    dma = pltpu.SemaphoreType.DMA
    return pl.pallas_call(
        backward_kernel,
        in_specs=[smem, anyw, vmem, vmem] + [anyw] * 12 + [vmem] * 3,
        out_specs=[anyw] * 3 + [vmem] * 2,
        out_shape=[grad] * 3
        + [jax.ShapeDtypeStruct((rows, model), F32), jax.ShapeDtypeStruct((16, model), F32)],
        scratch_shapes=[
            pltpu.VMEM((4, 4, 2, piece, model), BF),
            pltpu.VMEM((2,) + out_full.shape[1:], BF),
            pltpu.VMEM((2, rows, model), BF),
            pltpu.VMEM((2, rows, model), BF),
            pltpu.VMEM((rows, model), BF),
            pltpu.VMEM((rows, model), BF),
            pltpu.VMEM((rows, model), BF),
            pltpu.VMEM((2, rows, width), BF),
            pltpu.VMEM((2, LEN, width), BF),
            pltpu.VMEM((2, LEN, width), BF),
            pltpu.VMEM((2, rows, width), BF),
            pltpu.VMEM((rows, width), BF),
            pltpu.VMEM((2, LEN, PAIR), F32),
            pltpu.VMEM((rows, model), F32),
            pltpu.VMEM((2, width // PAIR, 2, rows, PAIR), BF),
            pltpu.VMEM((4, width // PAIR, 2, rows, PAIR), BF),
            pltpu.VMEM((2, rows, 3 * width), BF),
            pltpu.VMEM((6, 16, model), F32),
            pltpu.VMEM((5, 16, model), F32),
            dma((16,)),
            dma((24,)),
            dma((6,)),
            dma((8,)),
            dma((8,)),
            dma((5,)),
            dma((5,)),
            *Reduce.scratch(piece, model, 3),
            *Reduce.semaphores(12),
            *Spread.scratch(3),
        ],
        compiler_params=pltpu.CompilerParams(
            collective_id=1, has_side_effects=True, vmem_limit_bytes=VMEM_LIMIT
        ),
        cost_estimate=pl.CostEstimate(
            flops=60 * 10**9, bytes_accessed=80 << 20, transcendentals=8 << 20
        ),
        name="backward",
    )(
        lengths,
        x,
        vec,
        sums,
        qkv_full,
        out_full,
        up_full,
        down_full,
        q,
        k,
        v,
        o,
        act,
        slope,
        d_second,
        normal1,
        inverse1,
        hidden,
        lse,
    )


def on_device(
    inputs,
    cotangent,
    lengths,
    query_weight,
    key_weight,
    value_weight,
    query_bias,
    value_bias,
    out_weight,
    out_bias,
    norm1_gain,
    norm1_bias,
    up_weight,
    up_bias,
    down_weight,
    down_bias,
    norm2_gain,
    norm2_bias,
):
    t = lax.axis_index("tensor")
    model = inputs.shape[1]
    width = out_weight.shape[0]
    zero_row = jnp.zeros((model,), F32)
    vec = jnp.stack(
        [out_bias, norm1_gain, norm1_bias, down_bias, norm2_gain, norm2_bias, zero_row, zero_row]
    )
    small = jnp.stack(
        [jnp.concatenate([query_bias, value_bias, zero_row[2 * width :]]), up_bias] + [zero_row] * 6
    )
    saved = run_forward(
        lengths,
        inputs,
        cotangent,
        vec,
        small,
        query_weight,
        key_weight,
        value_weight,
        out_weight,
        up_weight,
        down_weight,
    )
    down_grad, up_grad, proj_grad, input_grad, sums = run_backward(lengths, inputs, vec, saved)
    grads = [g.reshape(model, model).astype(F32) for g in (down_grad, up_grad, proj_grad)]
    size = lax.axis_size("dp")
    if size > GROUP:
        groups = [list(range(first, size, GROUP)) for first in range(GROUP)]
        *grads, sums = lax.psum((*grads, sums), "dp", axis_index_groups=groups)
    down_grad, up_grad, proj_grad = grads
    up_bias_grad = lax.dynamic_index_in_dim(sums[6:10], t, 0, keepdims=False)
    proj_bias = lax.dynamic_index_in_dim(sums[10:14], t, 0, keepdims=False)
    return (
        saved[10],
        input_grad,
        proj_grad[:, :width],
        proj_grad[:, width : 2 * width],
        proj_grad[:, 2 * width : 3 * width],
        proj_bias[:width],
        proj_bias[2 * width : 3 * width],
        proj_grad[:, 3 * width :].T,
        sums[5],
        sums[3],
        sums[4],
        up_grad,
        up_bias_grad,
        down_grad,
        sums[2],
        sums[0],
        sums[1],
    )


def solution(mesh):
    rows = P(("dp", "tensor"), None)
    by_col = P(None, "tensor")
    by_row = P("tensor", None)
    split = P("tensor")
    whole = P()
    return jax.shard_map(
        on_device,
        mesh=mesh,
        in_specs=(
            P("dp", None),
            rows,
            P("dp"),
            by_col,
            by_col,
            by_col,
            split,
            split,
            by_row,
            whole,
            whole,
            whole,
            by_col,
            split,
            by_row,
            whole,
            whole,
            whole,
        ),
        out_specs=(
            rows,
            rows,
            by_col,
            by_col,
            by_col,
            split,
            split,
            by_row,
            whole,
            whole,
            whole,
            by_col,
            split,
            by_row,
            whole,
            whole,
            whole,
        ),
        check_vma=False,
    )
```

```python
import functools

import jax
import jax.numpy as jnp
from jax import lax
from jax.experimental import pallas as pl
from jax.experimental.pallas import tpu as pltpu
from jax.sharding import PartitionSpec as P

HD = 64
LEN = 1024
PAIR = 2 * HD
GROUP = 8
F32 = jnp.float32
BF = jnp.bfloat16
NN = (((1,), (0,)), ((), ()))
NT = (((1,), (1,)), ((), ()))
TN = (((0,), (0,)), ((), ()))
MESH = pl.DeviceIdType.MESH
VMEM_LIMIT = 63 << 20


def product(left, right, dims=NN):
    return lax.dot_general(left, right, dims, preferred_element_type=F32)


def flip(index, bit):
    return index + bit * (1 - 2 * lax.rem(lax.div(index, bit), 2))


def mix(index, step):
    low = lax.rem(index + step, 2)
    high = lax.rem(lax.div(index, 2) + lax.div(step, 2), 2)
    return 2 * high + low


class Place:
    def __init__(self):
        self.dp = lax.axis_index("dp")
        self.t = lax.axis_index("tensor")
        self.e = lax.rem(self.dp, GROUP)
        self.core = lax.rem(self.e, 2)
        self.quad = lax.div(self.e, 2)
        self.to_core = (flip(self.dp, 1), self.t)
        self.to_x = (flip(self.dp, 2), self.t)
        self.to_y = (flip(self.dp, 4), self.t)
        self.quad_x = flip(self.quad, 1)
        self.quad_y = flip(self.quad, 2)
        self.quad_xy = flip(self.quad_x, 2)

    def to_z(self, step):
        return (self.dp, mix(self.t, jnp.int32(step)))

    def greet(self):
        barrier = pltpu.get_barrier_semaphore()
        peers = [self.to_core, self.to_x, self.to_y, self.to_z(1), self.to_z(2), self.to_z(3)]
        for peer in peers:
            pl.semaphore_signal(barrier, inc=1, device_id=peer, device_id_type=MESH)
        pl.semaphore_wait(barrier, len(peers))


def remote(src, dst, send, recv, index, device):
    return pltpu.make_async_remote_copy(
        src_ref=src,
        dst_ref=dst,
        send_sem=send.at[index],
        recv_sem=recv.at[index],
        device_id=device,
        device_id_type=MESH,
    )


class Spread:
    def __init__(self, place, full, sems, index):
        self.p = place
        self.full = full
        self.sems = sems
        self.index = index

    def block(self, step):
        return mix(self.p.t, jnp.int32(step)) if step else self.p.t

    def slot(self, step):
        return self.index * 4 + step

    def x_copy(self, step):
        p = self.p
        ref = self.full.at[self.block(step), p.quad, p.core]
        return remote(ref, ref, self.sems[0], self.sems[1], self.slot(step), p.to_x)

    def y_copy(self, step):
        p = self.p
        ref = self.full.at[self.block(step), p.quad, p.core]
        return remote(ref, ref, self.sems[2], self.sems[3], self.slot(step), p.to_y)

    def half_copies(self, step):
        p = self.p
        half = self.full.shape[3] // 2
        first = self.full.at[self.block(step), p.quad_x, p.core, pl.ds(0, half)]
        second = self.full.at[self.block(step), p.quad_y, p.core, pl.ds(half, half)]
        return (
            remote(first, first, self.sems[4], self.sems[5], self.slot(step), p.to_y),
            remote(second, second, self.sems[6], self.sems[7], self.slot(step), p.to_x),
        )

    def core_copy(self, step):
        p = self.p
        ref = self.full.at[self.block(step), :, p.core]
        return remote(ref, ref, self.sems[8], self.sems[9], self.slot(step), p.to_core)

    def first(self, step):
        self.x_copy(step).start()
        self.y_copy(step).start()

    def second(self, step):
        self.x_copy(step).wait_recv()
        self.y_copy(step).wait_recv()
        for copy in self.half_copies(step):
            copy.start()

    def third(self, step):
        for copy in self.half_copies(step):
            copy.wait_recv()
        self.core_copy(step).start()

    def arrived(self, step):
        self.core_copy(step).wait_recv()

    def finish(self, step):
        self.x_copy(step).wait_send()
        self.y_copy(step).wait_send()
        for copy in self.half_copies(step):
            copy.wait_send()
        self.core_copy(step).wait_send()

    @staticmethod
    def scratch(count):
        return [pltpu.SemaphoreType.DMA((4 * count,))] * 10


def norm_center(values):
    center = values - jnp.mean(values, axis=-1, keepdims=True)
    inverse = lax.rsqrt(jnp.mean(center * center, axis=-1, keepdims=True) + 1e-05)
    return center * inverse, inverse


def norm_back(grad, normal, inverse, gain):
    scaled = grad * gain
    first_mean = jnp.mean(scaled, axis=-1, keepdims=True)
    second_mean = jnp.mean(scaled * normal, axis=-1, keepdims=True)
    return inverse * (scaled - first_mean - normal * second_mean)


class Reduce:
    def __init__(self, place, bufs, sems):
        self.p = place
        self.g, self.s, self.rc, self.ra, self.rb, self.zs, self.rz, self.own = bufs
        self.sems = sems

    @staticmethod
    def scratch(piece, cols, arrays):
        return [
            pltpu.VMEM((2, 4, 2, piece, cols), BF),
            pltpu.VMEM((3, 4, piece, cols), BF),
            pltpu.VMEM((2, 4, piece, cols), BF),
            pltpu.VMEM((3, 2, piece // 2, cols), BF),
            pltpu.VMEM((3, 2, piece, cols), BF),
            pltpu.VMEM((3, piece, cols), BF),
            pltpu.VMEM((arrays, 3, piece, cols), BF),
            pltpu.VMEM((arrays, piece, cols), BF),
        ]

    @staticmethod
    def semaphores(units):
        return [pltpu.SemaphoreType.DMA((units,))] * 12

    def core_copy(self, u):
        other = 1 - self.p.core
        return remote(
            self.g.at[lax.rem(u, 2), :, other],
            self.rc.at[lax.rem(u, 2)],
            self.sems[0],
            self.sems[1],
            u,
            self.p.to_core,
        )

    def corner_copies(self, u):
        p, slot = self.p, lax.rem(u, 3)
        half = self.ra.shape[2]
        return (
            remote(
                self.s.at[slot, p.quad_xy, pl.ds(0, half)],
                self.ra.at[slot, 0],
                self.sems[2],
                self.sems[3],
                u,
                p.to_y,
            ),
            remote(
                self.s.at[slot, p.quad_xy, pl.ds(half, half)],
                self.ra.at[slot, 1],
                self.sems[4],
                self.sems[5],
                u,
                p.to_x,
            ),
        )

    def side_copies(self, u):
        p, slot = self.p, lax.rem(u, 3)
        return (
            remote(
                self.s.at[slot, p.quad_x], self.rb.at[slot, 0], self.sems[6], self.sems[7], u, p.to_x
            ),
            remote(
                self.s.at[slot, p.quad_y], self.rb.at[slot, 1], self.sems[8], self.sems[9], u, p.to_y
            ),
        )

    def z_copy(self, u, array, step):
        return remote(
            self.zs.at[lax.rem(u, 3)],
            self.rz.at[array, step - 1],
            self.sems[10],
            self.sems[11],
            array * 4 + step,
            (self.p.dp, mix(self.p.t, step)),
        )

    def free_g(self, u):
        if not isinstance(u, int):
            pl.when(u >= 2)(lambda: self.core_copy(u - 2).wait_send())
        elif u >= 2:
            self.core_copy(jnp.int32(u - 2)).wait_send()

    def send(self, u):
        self.core_copy(u).start()

    def fold_core(self, u):
        slot = lax.rem(u, 3)

        def freed():
            for copy in self.side_copies(u - 3) + self.corner_copies(u - 3):
                copy.wait_send()

        pl.when(u >= 3)(freed)
        self.core_copy(u).wait_recv()
        mine = self.g[lax.rem(u, 2), :, self.p.core].astype(F32)
        self.s[slot] = (mine + self.rc[lax.rem(u, 2)].astype(F32)).astype(BF)
        for copy in self.corner_copies(u):
            copy.start()

    def fold_corner(self, u):
        p, slot = self.p, lax.rem(u, 3)
        half = self.ra.shape[2]
        for copy in self.corner_copies(u):
            copy.wait_recv()
        lower = self.s[slot, p.quad_x, :half].astype(F32) + self.ra[slot, 0].astype(F32)
        self.s[slot, p.quad_x, :half] = lower.astype(BF)
        upper = self.s[slot, p.quad_y, half:].astype(F32) + self.ra[slot, 1].astype(F32)
        self.s[slot, p.quad_y, half:] = upper.astype(BF)
        for copy in self.side_copies(u):
            copy.start()

    def fold_sides(self, u, array, step, before):
        p, slot = self.p, lax.rem(u, 3)
        for copy in self.side_copies(u):
            copy.wait_recv()
        total = (
            self.s[slot, p.quad].astype(F32)
            + self.rb[slot, 0].astype(F32)
            + self.rb[slot, 1].astype(F32)
        ).astype(BF)

        if before is not None:
            old_array, old_step, valid = before
            pl.when(valid)(lambda: self.z_copy(u - 3, old_array, old_step).wait_send())

        def store():
            self.own[array] = total

        def pass_on():
            self.zs[slot] = total
            self.z_copy(u, array, step).start()

        pl.when(step == 0)(store)
        pl.when(step != 0)(pass_on)

    def finish(self, array, out, sem):
        total = self.own[array].astype(F32)
        for step in (1, 2, 3):
            self.z_copy(jnp.int32(0), jnp.int32(array), jnp.int32(step)).wait_recv()
            total = total + self.rz[array, step - 1].astype(F32)
        self.own[array] = total.astype(BF)
        copy = pltpu.make_async_copy(self.own.at[array], out.at[0, self.p.quad, self.p.core], sem)
        copy.start()
        copy.wait()


def layer_kernel(
    len_ref,
    x_hbm,
    cot_hbm,
    vec_ref,
    bias_ref,
    wq_hbm,
    wk_hbm,
    wv_hbm,
    wo_hbm,
    wu_hbm,
    wd_hbm,
    qkv_full,
    out_full,
    up_full,
    down_full,
    q_hbm,
    k_hbm,
    v_hbm,
    outputs_hbm,
    down_grad,
    up_grad,
    proj_grad,
    acc,
    sums_ref,
    x_seq,
    bias_all,
    w_s,
    w_out,
    q_s,
    k_s,
    v_s,
    o_s,
    act_s,
    slope_s,
    wide,
    hidden_s,
    low_s,
    inverse_s,
    lse_s,
    d_att,
    kv_temp,
    kv_send,
    kv_recv,
    d_all,
    small,
    small_recv,
    z_send,
    z_recv,
    bias_send,
    bias_recv,
    local,
    load,
    save,
    att_load,
    back_load,
    kv_ssem,
    kv_rsem,
    small_ssem,
    small_rsem,
    *rest,
):
    p = Place()
    reduce = Reduce(p, rest[:8], rest[8:20])
    rows, model = acc.shape
    width = q_s.shape[2]
    half_index = lax.rem(p.t, 2)
    seq = lax.div(p.t, 2)
    own_at = pl.multiple_of(half_index * rows, rows)
    other_at = pl.multiple_of((1 - half_index) * rows, rows)
    own_rows = pl.ds(own_at, rows)
    fulls = [qkv_full, out_full, up_full, down_full]
    spreads = [Spread(p, full, rest[20:30], i) for i, full in enumerate(fulls)]
    QKV, OUT, UP, DOWN = range(4)
    qkv_cols = pl.ds(0, 3 * width)

    def on(step, at, *actions):
        @pl.when(step == at)
        def _():
            for action in actions:
                action()

    def begin(copies):
        for copy in copies:
            copy.start()

    def end(copies):
        for copy in copies:
            copy.wait()

    x_load = pltpu.make_async_copy(
        x_hbm.at[pl.ds(pl.multiple_of(seq * LEN, LEN), LEN)], x_seq, local.at[0]
    )
    own_loads = [
        pltpu.make_async_copy(w, w_s.at[2, :, :, :, pl.ds(i * width, width)], local.at[1 + i])
        for i, w in enumerate((wq_hbm, wk_hbm, wv_hbm))
    ]
    out_load = pltpu.make_async_copy(wo_hbm, w_out.at[0], local.at[4])
    up_load = pltpu.make_async_copy(wu_hbm, w_s.at[0], local.at[5])
    down_load = pltpu.make_async_copy(wd_hbm, w_s.at[0], local.at[6])
    cot_load = pltpu.make_async_copy(cot_hbm, low_s, local.at[7])
    qkv_save = pltpu.make_async_copy(w_s.at[2, :, :, :, qkv_cols], qkv_full.at[p.t], local.at[8])
    up_save = pltpu.make_async_copy(w_s.at[0], up_full.at[p.t], local.at[9])
    outputs_s = reduce.g.at[1, 0:2]
    outputs_save = pltpu.make_async_copy(outputs_s, outputs_hbm, local.at[10])
    begin(own_loads)
    x_load.start()
    out_load.start()
    up_load.start()
    cot_load.start()
    bias_all[p.t] = bias_ref[...]
    p.greet()

    def z_copies(array, step):
        slot = array * 4 + step
        if array == QKV:
            return [
                remote(
                    w.at[p.quad, p.core],
                    qkv_full.at[p.t, p.quad, p.core, :, pl.ds(i * width, width)],
                    z_send,
                    z_recv,
                    slot if i == 0 else 16 + 4 * (i - 1) + step,
                    p.to_z(step),
                )
                for i, w in enumerate((wq_hbm, wk_hbm, wv_hbm))
            ]
        w = (None, wo_hbm, wu_hbm, wd_hbm)[array]
        place = fulls[array].at[p.t, p.quad, p.core]
        return [remote(w.at[p.quad, p.core], place, z_send, z_recv, slot, p.to_z(step))]

    def bias_copy(step):
        return remote(bias_ref, bias_all.at[p.t], bias_send, bias_recv, step, p.to_z(step))

    for step in (1, 2, 3):
        bias_copy(step).start()
    for array in (QKV, OUT, UP, DOWN):
        for step in (1, 2, 3):
            begin(z_copies(array, step))

    def load_copy(array, step):
        if array == QKV:
            dst = w_s.at[2 + step % 2, :, :, :, qkv_cols]
        elif array == OUT:
            dst = w_out.at[step]
        else:
            dst = w_s.at[step]
        src = fulls[array].at[mix(p.t, jnp.int32(step))]
        return pltpu.make_async_copy(src, dst, load.at[array * 4 + step])

    def relay(plan):
        for array, legs in plan:
            spread = spreads[array]
            for leg in legs.split():
                kind, step = leg[0], int(leg[1])
                if kind == "f":
                    for copy in z_copies(array, step):
                        copy.wait_recv()
                    spread.first(step)
                elif kind == "s":
                    spread.second(step)
                elif kind == "t":
                    spread.third(step)
                else:
                    spread.arrived(step)
                    load_copy(array, step).start()

    def passed(step, place):
        plans = {
            (0, "end"): [
                (QKV, "f1 f2 s1 f3 s2"),
                (OUT, "f1"),
                (QKV, "t1"),
                (OUT, "f2 f3"),
                (QKV, "a1 s3"),
            ],
            (1, "mid"): [(QKV, "t2"), (OUT, "s1")],
            (1, "end"): [(OUT, "s2 s3"), (UP, "f1"), (QKV, "a2")],
            (2, "start"): [(QKV, "t3"), (OUT, "t1 t2")],
            (2, "mid"): [(OUT, "t3")],
            (2, "end"): [(QKV, "a3"), (OUT, "a1 a2 a3"), (UP, "f2")],
            (3, "start"): [(UP, "s1 f3")],
            (3, "end"): [(UP, "s2")],
        }
        for (at, where), plan in plans.items():
            if where == place:
                on(step, at, lambda plan=plan: relay(plan))

    def attend_saves(step):
        group, slot = mix(p.t, step), lax.rem(step, 2)
        pairs = ((q_s, q_hbm), (k_s, k_hbm), (v_s, v_hbm))
        return [
            pltpu.make_async_copy(vmem.at[slot], hbm.at[group], save.at[3 * step + i])
            for i, (vmem, hbm) in enumerate(pairs)
        ]

    def attend(step):
        group, slot = mix(p.t, step), lax.rem(step, 2)
        weights = w_s[2 + slot, :, :, :, qkv_cols].reshape(model, 3 * width)
        bias = bias_all[group, 0:1]
        queries = (product(x_seq[own_rows, :], weights[:, :width]) + bias[:, :width]).astype(BF)
        q_s[slot] = (queries.astype(F32) * HD ** (-0.5)).astype(BF)
        k_s[slot] = product(x_seq[...], weights[:, width : 2 * width]).astype(BF)
        v_s[slot] = (
            product(x_seq[...], weights[:, 2 * width :]) + bias[:, width : 2 * width]
        ).astype(BF)
        passed(step, "start")
        length = len_ref[seq]
        key_slot = lax.broadcasted_iota(jnp.int32, (LEN, rows), 0)
        lane = lax.broadcasted_iota(jnp.int32, (rows, PAIR), 1)
        for pair in range(width // PAIR):
            if pair == 1:
                passed(step, "mid")
            cols = slice(pair * PAIR, (pair + 1) * PAIR)
            keys, values, q_pair = k_s[slot, :, cols], v_s[slot, :, cols], q_s[slot, :, cols]
            parts = []
            for head in range(2):
                mine = jnp.where((lane >= HD) == (head == 1), q_pair, jnp.zeros_like(q_pair))
                scores = jnp.where(key_slot < length, product(keys, mine, NT), -1e30)
                top = jnp.max(scores, axis=0, keepdims=True)
                exponent = jnp.exp(scores - top)
                total = jnp.sum(exponent, axis=0, keepdims=True)
                mixed = product(values, exponent.astype(BF), TN)
                parts.append(mixed[head * HD : (head + 1) * HD] * (1.0 / total))
                lse_s[group, pl.ds(pair * 2 + head, 1), :] = top + jnp.log(total)
            o_s[step, :, cols] = jnp.concatenate(parts, axis=0).T.astype(BF)

    x_load.wait()
    end(own_loads)
    qkv_save.start()
    for step in (1, 2, 3):
        bias_copy(step).wait_recv()

    def attend_step(step, carry):
        for i in (1, 2, 3):
            on(step, i, load_copy(QKV, i).wait)
        pl.when(step >= 2)(lambda: end(attend_saves(step - 2)))
        attend(step)
        begin(attend_saves(step))
        on(step, 1, qkv_save.wait)
        passed(step, "end")
        return carry

    lax.fori_loop(0, 4, attend_step, 0)

    out_load.wait()
    for step in (1, 2, 3):
        load_copy(OUT, step).wait()
    acc[...] = x_seq[own_rows, :].astype(F32) + vec_ref[0:1]
    for step in range(4):
        acc[...] += product(o_s[step], w_out[step].reshape(width, model))
    normal1, inverse1 = norm_center(acc[...])
    wide[...] = normal1
    inverse_s[...] = jnp.broadcast_to(inverse1, inverse_s.shape)
    normed1 = normal1 * vec_ref[1:2] + vec_ref[2:3]
    hidden_s[...] = normed1.astype(BF)
    acc[...] = normed1 + vec_ref[3:4]
    relay([(UP, "t1")])

    def up_step(step, carry):
        on(step, 0, up_load.wait, up_save.start)
        for i in (1, 2, 3):
            on(step, i, load_copy(UP, i).wait)
        upper = product(hidden_s[...], w_s[step].reshape(model, model))
        upper = upper + bias_all[mix(p.t, step), 1:2]
        cdf = 0.5 * (1.0 + lax.erf(upper * 0.7071067811865476))
        act_s[step] = (upper * cdf).astype(BF)
        density = jnp.exp(-0.5 * upper * upper) * 0.3989422804014327
        slope_s[step] = (cdf + upper * density).astype(BF)
        on(step, 0, lambda: relay([(UP, "a1 s3"), (DOWN, "f1")]))
        on(step, 1, up_save.wait, down_load.start)
        on(step, 1, lambda: relay([(UP, "t2"), (DOWN, "f2"), (UP, "t3"), (DOWN, "f3"), (UP, "a2")]))
        on(step, 2, lambda: relay([(UP, "a3"), (DOWN, "s1")]))
        on(step, 3, lambda: relay([(DOWN, "s2")]))
        return carry

    lax.fori_loop(0, 4, up_step, 0)
    for step in (2, 3):
        end(attend_saves(jnp.int32(step)))

    def down_step(step, carry):
        on(step, 0, down_load.wait)
        for i in (1, 2, 3):
            on(step, i, load_copy(DOWN, i).wait)
        acc[...] += product(act_s[step], w_s[step].reshape(model, model))
        on(step, 0, lambda: relay([(DOWN, "s3 t1 t2 a1")]))
        on(step, 1, lambda: relay([(DOWN, "t3 a2")]))
        on(step, 2, lambda: relay([(DOWN, "a3")]))
        return carry

    lax.fori_loop(0, 4, down_step, 0)

    cot_load.wait()
    normal2, inverse2 = norm_center(acc[...])
    outputs = (normal2 * vec_ref[4:5] + vec_ref[5:6]).astype(BF)
    reduce.g[1, 0:2] = outputs.reshape(2, 2, rows // 4, model)
    outputs_save.start()
    slot_index = half_index * rows + lax.broadcasted_iota(jnp.int32, (rows, 1), 0)
    grad_out = jnp.where(slot_index < len_ref[seq], low_s[...].astype(F32), 0.0)
    d_second = norm_back(grad_out, normal2, inverse2, vec_ref[4:5])
    acc[...] = d_second
    low_s[...] = d_second.astype(BF)
    small[0] = jnp.zeros(small.shape[1:], F32)
    small[0, 0:1] = jnp.sum(grad_out * normal2, axis=0, keepdims=True)
    small[0, 1:2] = jnp.sum(grad_out, axis=0, keepdims=True)
    small[0, 2:3] = jnp.sum(d_second, axis=0, keepdims=True)

    grads = (down_grad, up_grad, proj_grad)
    back_spreads = [Spread(p, grad, rest[30:40], i) for i, grad in enumerate(grads)]
    for spread in back_spreads:
        spread.block = lambda step: 0
    B_DOWN, B_UP, B_PROJ = range(3)

    def group_at(i):
        return 2 * lax.rem(lax.div(p.t, 2) + 1 + lax.div(i, 2), 2) + lax.rem(i, 2)

    def att_loads(i):
        g, slot = group_at(i), lax.rem(i, 2)
        pairs = ((q_hbm, q_s), (k_hbm, k_s), (v_hbm, v_s))
        return [
            pltpu.make_async_copy(hbm.at[g], vmem.at[slot], att_load.at[4 * i + n])
            for n, (hbm, vmem) in enumerate(pairs)
        ]

    def proj_load(i):
        slot = lax.rem(i, 2)
        return pltpu.make_async_copy(
            qkv_full.at[group_at(i)], w_s.at[slot, :, :, :, qkv_cols], att_load.at[4 * i + 3]
        )

    def up_again(step):
        return pltpu.make_async_copy(up_full.at[mix(p.t, step)], w_s.at[step], back_load.at[step])

    begin(att_loads(jnp.int32(0)))

    def unit_of(u):
        return lax.rem(u, 2), 3 - lax.div(u, 2)

    def fold_sides(u):
        array, step = unit_of(u)
        old_array, old_step = unit_of(jnp.maximum(u - 3, 0))
        reduce.fold_sides(
            u, array, step, (old_array, old_step, jnp.logical_and(u >= 3, old_step != 0))
        )

    def tick(u):
        pl.when(u >= 1)(lambda: reduce.fold_core(u - 1))
        reduce.send(u)
        pl.when(u >= 2)(lambda: reduce.fold_corner(u - 2))
        pl.when(u >= 3)(lambda: fold_sides(u - 3))

    def store_unit(slot, left, right):
        part = model // 4
        for quad in range(4):
            terms = product(left(slice(quad * part, (quad + 1) * part)), right, TN)
            reduce.g[slot, quad] = terms.astype(BF).reshape(2, part // 2, right.shape[1])

    def mlp_step(i, carry):
        step = 3 - i
        u = 2 * i
        reduce.free_g(u)
        store_unit(0, lambda cols: act_s[step, :, cols], low_s[...])
        tick(u)
        d_act = product(low_s[...], w_s[step].reshape(model, model), NT)
        d_up = (d_act * slope_s[step].astype(F32)).astype(BF)
        slope_s[step] = d_up
        up_again(step).start()
        at = pl.ds(6 + mix(p.t, step), 1)
        small[0, at, :] = jnp.sum(d_up.astype(F32), axis=0, keepdims=True)
        reduce.free_g(u + 1)
        on(i, 0, outputs_save.wait)
        store_unit(1, lambda cols: hidden_s[:, cols], slope_s[step])
        tick(u + 1)
        up_again(step).wait()
        acc[...] += product(slope_s[step], w_s[step].reshape(model, model), NT)
        return carry

    lax.fori_loop(0, 4, mlp_step, 0)

    proj_load(jnp.int32(0)).start()
    normal1 = wide[...]
    small[0, 3:4] = jnp.sum(acc[...] * normal1, axis=0, keepdims=True)
    small[0, 4:5] = jnp.sum(acc[...], axis=0, keepdims=True)
    d_first = norm_back(acc[...], normal1, inverse_s[:, 0:1], vec_ref[1:2])
    acc[...] = d_first
    low_s[...] = d_first.astype(BF)
    small[0, 5:6] = jnp.sum(d_first, axis=0, keepdims=True)
    reduce.fold_core(jnp.int32(7))
    reduce.fold_corner(jnp.int32(6))
    fold_sides(jnp.int32(5))

    def kv_copy(i, pair):
        slot = lax.rem(i, 2)
        return remote(
            kv_send.at[slot, pair], kv_recv.at[i, pair], kv_ssem, kv_rsem, 2 * i + pair, p.to_z(1)
        )

    def wide_at(slot, n, pair):
        return pl.ds(pl.multiple_of((2 * slot + n) * width + pair * PAIR, PAIR), PAIR)

    def attend_back(i):
        slot = lax.rem(i, 2)
        g = group_at(i)
        step = mix(p.t, g)
        length = len_ref[seq]
        d_att[...] = product(low_s[...], w_out[step].reshape(width, model), NT).astype(BF)
        key_slot = lax.broadcasted_iota(jnp.int32, (LEN, rows), 0)
        lane = lax.broadcasted_iota(jnp.int32, (rows, PAIR), 1)
        for pair in range(width // PAIR):
            cols = slice(pair * PAIR, (pair + 1) * PAIR)
            keys, values, queries = k_s[slot, :, cols], v_s[slot, :, cols], q_s[slot, :, cols]
            d_out = d_att[:, cols]
            inner_all = (d_out.astype(F32) * o_s[step, :, cols].astype(F32)).T
            query_parts = []
            for head in range(2):
                mine = (lane >= HD) == (head == 1)
                own_q = jnp.where(mine, queries, jnp.zeros_like(queries))
                own_d = jnp.where(mine, d_out, jnp.zeros_like(d_out))
                inner = jnp.sum(inner_all[head * HD : (head + 1) * HD], axis=0, keepdims=True)
                scores = jnp.where(key_slot < length, product(keys, own_q, NT), -1e30)
                probs = jnp.exp(scores - lse_s[g, pl.ds(pair * 2 + head, 1), :])
                d_probs = product(values, own_d, NT)
                d_scores = (probs * (d_probs - inner) * HD ** (-0.5)).astype(BF)
                d_values = product(probs.astype(BF), own_d)
                d_keys = product(d_scores, own_q) * HD**0.5
                if head == 0:
                    kv_temp[0] = d_keys
                    kv_temp[1] = d_values
                else:
                    kv_temp[0] += d_keys
                    kv_temp[1] += d_values
                query_parts.append(product(keys, d_scores, TN)[head * HD : (head + 1) * HD])
            d_all[slot, :, cols] = jnp.concatenate(query_parts, axis=0).T.astype(BF)
            pl.when(i >= 2)(lambda: kv_copy(i - 2, pair).wait_send())
            for n in range(2):
                wide[:, wide_at(slot, n, pair)] = kv_temp[n, own_rows, :]
                kv_send[slot, pair, n] = kv_temp[n, pl.ds(other_at, rows), :].astype(BF)
            kv_copy(i, pair).start()

    def finish_group(i, u):
        slot = lax.rem(i, 2)
        g = group_at(i)
        for pair in range(width // PAIR):
            kv_copy(i, pair).wait_recv()
            for n in range(2):
                at = (n + 1) * width + pair * PAIR
                both = wide[:, wide_at(slot, n, pair)] + kv_recv[i, pair, n].astype(F32)
                d_all[slot, :, at : at + PAIR] = both.astype(BF)
        grad = d_all[slot]
        small[0, pl.ds(10 + g, 1), 0 : 3 * width] = jnp.sum(
            grad.astype(F32), axis=0, keepdims=True
        )
        reduce.core_copy(u - 2).wait_send()
        g_slot = lax.rem(u, 2)
        out_terms = product(o_s[mix(p.t, g)], low_s[...], TN).astype(BF)
        for quad in range(4):
            cols = slice(quad * width, (quad + 1) * width)
            terms = product(x_seq[own_rows, cols], grad, TN).astype(BF)
            reduce.g[g_slot, quad, :, :, 0 : 3 * width] = terms.reshape(2, width // 2, 3 * width)
            block = out_terms[:, cols].reshape(2, width // 2, width)
            reduce.g[g_slot, quad, :, :, 3 * width :] = block
        reduce.send(u)
        proj_load(i).wait()
        weights = w_s[slot, :, :, :, qkv_cols].reshape(model, 3 * width)
        acc[...] += product(grad, weights, NT)

    def proj_step(u):
        return mix(p.t, group_at(jnp.int32(u - 8)))

    def fold_proj_sides(u):
        if u - 3 >= 8:
            old_step = proj_step(u - 3)
            before = (jnp.int32(B_PROJ), old_step, old_step != 0)
        else:
            array, old_step = unit_of(jnp.int32(u - 3))
            before = (array, old_step, old_step != 0)
        reduce.fold_sides(jnp.int32(u), jnp.int32(B_PROJ), proj_step(u), before)

    def att_step(i, carry):
        end(att_loads(i))
        attend_back(i)

        def zero():
            reduce.fold_corner(jnp.int32(7))
            fold_sides(jnp.int32(6))
            reduce.finish(B_DOWN, down_grad, local.at[11])
            back_spreads[B_DOWN].first(0)

        def two():
            reduce.fold_core(jnp.int32(8))

        def three():
            reduce.fold_core(jnp.int32(9))
            reduce.fold_corner(jnp.int32(8))

        on(i, 0, zero)
        on(i, 2, two)
        on(i, 3, three)
        pl.when(i >= 1)(lambda: finish_group(i - 1, i + 7))

        def next_loads():
            begin(att_loads(i + 1))
            proj_load(i + 1).start()

        pl.when(i < 3)(next_loads)

        def after_one():
            fold_sides(jnp.int32(7))
            back_spreads[B_DOWN].second(0)
            reduce.finish(B_UP, up_grad, local.at[12])
            back_spreads[B_UP].first(0)

        def after_two():
            back_spreads[B_DOWN].third(0)
            back_spreads[B_UP].second(0)

        def after_three():
            fold_proj_sides(8)
            back_spreads[B_DOWN].arrived(0)
            back_spreads[B_UP].third(0)

        on(i, 1, after_one)
        on(i, 2, after_two)
        on(i, 3, after_three)
        return carry

    lax.fori_loop(0, 4, att_step, 0)
    reduce.fold_core(jnp.int32(10))
    reduce.fold_corner(jnp.int32(9))
    finish_group(jnp.int32(3), jnp.int32(11))
    peers = [p.to_core, p.to_x, p.to_y, p.to_z(1), p.to_z(2)]

    def small_copy(n):
        return remote(small.at[n], small_recv.at[n], small_ssem, small_rsem, n, peers[n])

    def small_next(n):
        small_copy(n).wait_recv()
        small[n + 1] = small[n] + small_recv[n]
        if n < 4:
            small_copy(n + 1).start()

    small_copy(0).start()
    fold_proj_sides(9)
    reduce.fold_core(jnp.int32(11))
    reduce.fold_corner(jnp.int32(10))
    small_next(0)
    fold_proj_sides(10)
    reduce.fold_corner(jnp.int32(11))
    small_next(1)
    back_spreads[B_UP].arrived(0)
    fold_proj_sides(11)
    reduce.finish(B_PROJ, proj_grad, local.at[13])
    back_spreads[B_PROJ].first(0)
    small_next(2)
    back_spreads[B_PROJ].second(0)
    small_next(3)
    back_spreads[B_PROJ].third(0)
    small_next(4)
    sums_ref[...] = small[5]

    for step in (1, 2, 3):
        bias_copy(step).wait_send()
        for array in range(4):
            for copy in z_copies(array, step):
                copy.wait_send()
            spreads[array].finish(step)
    for u in (10, 11):
        reduce.core_copy(jnp.int32(u)).wait_send()
    for u in (9, 10, 11):
        for copy in reduce.side_copies(jnp.int32(u)) + reduce.corner_copies(jnp.int32(u)):
            copy.wait_send()
        last = reduce.z_copy(jnp.int32(u), jnp.int32(B_PROJ), proj_step(u))
        pl.when(proj_step(u) != 0)(last.wait_send)
    for i in (2, 3):
        for pair in range(width // PAIR):
            kv_copy(jnp.int32(i), pair).wait_send()
    for n in range(5):
        small_copy(n).wait_send()
    back_spreads[B_PROJ].arrived(0)
    for spread in back_spreads:
        spread.finish(0)


def run_layer(lengths, x, cot, vec, bias, wq, wk, wv, wo, wu, wd):
    T = lax.axis_size("tensor")
    model = x.shape[1]
    rows = x.shape[0] // T
    width = wo.shape[0]
    piece = model // GROUP

    def pieces(w):
        return w.reshape(4, 2, w.shape[0] // GROUP, w.shape[1])

    def out(*shape, dtype=BF):
        return jax.ShapeDtypeStruct(shape, dtype)

    anyw = pl.BlockSpec(memory_space=pl.ANY)
    vmem = pl.BlockSpec(memory_space=pltpu.VMEM)
    smem = pl.BlockSpec(memory_space=pltpu.SMEM)
    dma = pltpu.SemaphoreType.DMA
    outs = [
        out(T, 4, 2, piece, 3 * width),
        out(T, 4, 2, width // GROUP, model),
        out(T, 4, 2, piece, model),
        out(T, 4, 2, piece, model),
        out(T, rows, width),
        out(T, LEN, width),
        out(T, LEN, width),
        out(2, 2, rows // 4, model),
        *[out(1, 4, 2, piece, model)] * 3,
        out(rows, model, dtype=F32),
        out(16, model, dtype=F32),
    ]
    return pl.pallas_call(
        layer_kernel,
        in_specs=[smem, anyw, anyw, vmem, vmem] + [anyw] * 6,
        out_specs=[anyw] * 11 + [vmem] * 2,
        out_shape=outs,
        scratch_shapes=[
            pltpu.VMEM((LEN, model), BF),
            pltpu.VMEM((T, 8, model), F32),
            pltpu.VMEM((4, 4, 2, piece, model), BF),
            pltpu.VMEM((T, 4, 2, width // GROUP, model), BF),
            pltpu.VMEM((2, rows, width), BF),
            pltpu.VMEM((2, LEN, width), BF),
            pltpu.VMEM((2, LEN, width), BF),
            pltpu.VMEM((T, rows, width), BF),
            pltpu.VMEM((T, rows, model), BF),
            pltpu.VMEM((T, rows, model), BF),
            pltpu.VMEM((rows, model), F32),
            pltpu.VMEM((rows, model), BF),
            pltpu.VMEM((rows, model), BF),
            pltpu.VMEM((rows, 128), F32),
            pltpu.VMEM((T, 8, rows), F32),
            pltpu.VMEM((rows, width), BF),
            pltpu.VMEM((2, LEN, PAIR), F32),
            pltpu.VMEM((2, width // PAIR, 2, rows, PAIR), BF),
            pltpu.VMEM((4, width // PAIR, 2, rows, PAIR), BF),
            pltpu.VMEM((2, rows, 3 * width), BF),
            pltpu.VMEM((6, 16, model), F32),
            pltpu.VMEM((5, 16, model), F32),
            dma((24,)),
            dma((24,)),
            dma((4,)),
            dma((4,)),
            dma((14,)),
            dma((16,)),
            dma((12,)),
            dma((16,)),
            dma((4,)),
            dma((8,)),
            dma((8,)),
            dma((5,)),
            dma((5,)),
            *Reduce.scratch(piece, model, 3),
            *Reduce.semaphores(12),
            *Spread.scratch(4),
            *Spread.scratch(3),
        ],
        compiler_params=pltpu.CompilerParams(
            collective_id=0, has_side_effects=True, vmem_limit_bytes=VMEM_LIMIT
        ),
        cost_estimate=pl.CostEstimate(
            flops=100 * 10**9, bytes_accessed=120 << 20, transcendentals=24 << 20
        ),
        name="layer",
    )(
        lengths,
        x,
        cot,
        vec,
        bias,
        pieces(wq),
        pieces(wk),
        pieces(wv),
        pieces(wo),
        pieces(wu),
        pieces(wd),
    )


def on_device(
    inputs,
    cotangent,
    lengths,
    query_weight,
    key_weight,
    value_weight,
    query_bias,
    value_bias,
    out_weight,
    out_bias,
    norm1_gain,
    norm1_bias,
    up_weight,
    up_bias,
    down_weight,
    down_bias,
    norm2_gain,
    norm2_bias,
):
    t = lax.axis_index("tensor")
    model = inputs.shape[1]
    rows = cotangent.shape[0]
    width = out_weight.shape[0]
    zero_row = jnp.zeros((model,), F32)
    vec = jnp.stack(
        [out_bias, norm1_gain, norm1_bias, down_bias, norm2_gain, norm2_bias, zero_row, zero_row]
    )
    bias = jnp.stack(
        [jnp.concatenate([query_bias, value_bias, zero_row[2 * width :]]), up_bias] + [zero_row] * 6
    )
    results = run_layer(
        lengths,
        inputs,
        cotangent,
        vec,
        bias,
        query_weight,
        key_weight,
        value_weight,
        out_weight,
        up_weight,
        down_weight,
    )
    outputs, down_grad, up_grad, proj_grad, input_grad, sums = results[7:]
    grads = [g.reshape(model, model).astype(F32) for g in (down_grad, up_grad, proj_grad)]
    size = lax.axis_size("dp")
    if size > GROUP:
        groups = [list(range(first, size, GROUP)) for first in range(GROUP)]
        *grads, sums = lax.psum((*grads, sums), "dp", axis_index_groups=groups)
    down_grad, up_grad, proj_grad = grads
    up_bias_grad = lax.dynamic_index_in_dim(sums[6:10], t, 0, keepdims=False)
    proj_bias = lax.dynamic_index_in_dim(sums[10:14], t, 0, keepdims=False)
    out_grad = jnp.concatenate(
        [proj_grad[c * width : (c + 1) * width, 3 * width :] for c in range(4)], axis=1
    )
    return (
        outputs.reshape(rows, model),
        input_grad,
        proj_grad[:, :width],
        proj_grad[:, width : 2 * width],
        proj_grad[:, 2 * width : 3 * width],
        proj_bias[:width],
        proj_bias[2 * width : 3 * width],
        out_grad,
        sums[5],
        sums[3],
        sums[4],
        up_grad,
        up_bias_grad,
        down_grad,
        sums[2],
        sums[0],
        sums[1],
    )


def solution(mesh):
    rows = P(("dp", "tensor"), None)
    by_col = P(None, "tensor")
    by_row = P("tensor", None)
    split = P("tensor")
    whole = P()
    return jax.shard_map(
        on_device,
        mesh=mesh,
        in_specs=(
            P("dp", None),
            rows,
            P("dp"),
            by_col,
            by_col,
            by_col,
            split,
            split,
            by_row,
            whole,
            whole,
            whole,
            by_col,
            split,
            by_row,
            whole,
            whole,
            whole,
        ),
        out_specs=(
            rows,
            rows,
            by_col,
            by_col,
            by_col,
            split,
            split,
            by_row,
            whole,
            whole,
            whole,
            by_col,
            split,
            by_row,
            whole,
            whole,
            whole,
        ),
        check_vma=False,
    )
```

```python
import functools

import jax
import jax.numpy as jnp
from jax import lax
from jax.experimental import pallas as pl
from jax.experimental.pallas import tpu as pltpu
from jax.sharding import PartitionSpec as P

HD = 64
LEN = 1024
PAIR = 2 * HD
GROUP = 8
F32 = jnp.float32
BF = jnp.bfloat16
NN = (((1,), (0,)), ((), ()))
NT = (((1,), (1,)), ((), ()))
TN = (((0,), (0,)), ((), ()))
MESH = pl.DeviceIdType.MESH
VMEM_LIMIT = 63 << 20


def product(left, right, dims=NN):
    return lax.dot_general(left, right, dims, preferred_element_type=F32)


def flip(index, bit):
    return index + bit * (1 - 2 * lax.rem(lax.div(index, bit), 2))


def mix(index, step):
    low = lax.rem(index + step, 2)
    high = lax.rem(lax.div(index, 2) + lax.div(step, 2), 2)
    return 2 * high + low


class Place:
    def __init__(self):
        self.dp = lax.axis_index("dp")
        self.t = lax.axis_index("tensor")
        self.e = lax.rem(self.dp, GROUP)
        self.core = lax.rem(self.e, 2)
        self.quad = lax.div(self.e, 2)
        self.to_core = (flip(self.dp, 1), self.t)
        self.to_x = (flip(self.dp, 2), self.t)
        self.to_y = (flip(self.dp, 4), self.t)
        self.quad_x = flip(self.quad, 1)
        self.quad_y = flip(self.quad, 2)
        self.quad_xy = flip(self.quad_x, 2)

    def to_z(self, step):
        return (self.dp, mix(self.t, jnp.int32(step)))

    def greet(self):
        barrier = pltpu.get_barrier_semaphore()
        peers = [self.to_core, self.to_x, self.to_y, self.to_z(1), self.to_z(2), self.to_z(3)]
        for peer in peers:
            pl.semaphore_signal(barrier, inc=1, device_id=peer, device_id_type=MESH)
        pl.semaphore_wait(barrier, len(peers))


def remote(src, dst, send, recv, index, device):
    return pltpu.make_async_remote_copy(
        src_ref=src,
        dst_ref=dst,
        send_sem=send.at[index],
        recv_sem=recv.at[index],
        device_id=device,
        device_id_type=MESH,
    )


class Spread:
    def __init__(self, place, full, sems, index):
        self.p = place
        self.full = full
        self.sems = sems
        self.index = index

    def block(self, step):
        return mix(self.p.t, jnp.int32(step)) if step else self.p.t

    def slot(self, step):
        return self.index * 4 + step

    def x_copy(self, step, src=None):
        p = self.p
        ref = self.full.at[self.block(step), p.quad, p.core]
        return remote(ref if src is None else src, ref, self.sems[0], self.sems[1], self.slot(step), p.to_x)

    def y_copy(self, step, src=None):
        p = self.p
        ref = self.full.at[self.block(step), p.quad, p.core]
        return remote(ref if src is None else src, ref, self.sems[2], self.sems[3], self.slot(step), p.to_y)

    def half_copies(self, step):
        p = self.p
        half = self.full.shape[3] // 2
        first = self.full.at[self.block(step), p.quad_x, p.core, pl.ds(0, half)]
        second = self.full.at[self.block(step), p.quad_y, p.core, pl.ds(half, half)]
        return (
            remote(first, first, self.sems[4], self.sems[5], self.slot(step), p.to_y),
            remote(second, second, self.sems[6], self.sems[7], self.slot(step), p.to_x),
        )

    def core_copy(self, step):
        p = self.p
        ref = self.full.at[self.block(step), :, p.core]
        return remote(ref, ref, self.sems[8], self.sems[9], self.slot(step), p.to_core)

    def first(self, step, src=None):
        self.x_copy(step, src).start()
        self.y_copy(step, src).start()

    def second(self, step):
        self.x_copy(step).wait_recv()
        self.y_copy(step).wait_recv()
        for copy in self.half_copies(step):
            copy.start()

    def third(self, step):
        for copy in self.half_copies(step):
            copy.wait_recv()
        self.core_copy(step).start()

    def arrived(self, step):
        self.core_copy(step).wait_recv()

    def finish(self, step):
        self.x_copy(step).wait_send()
        self.y_copy(step).wait_send()
        for copy in self.half_copies(step):
            copy.wait_send()
        self.core_copy(step).wait_send()

    @staticmethod
    def scratch(count):
        return [pltpu.SemaphoreType.DMA((4 * count,))] * 10


def norm_center(values):
    center = values - jnp.mean(values, axis=-1, keepdims=True)
    inverse = lax.rsqrt(jnp.mean(center * center, axis=-1, keepdims=True) + 1e-05)
    return center * inverse, inverse


def norm_back(grad, normal, inverse, gain):
    scaled = grad * gain
    first_mean = jnp.mean(scaled, axis=-1, keepdims=True)
    second_mean = jnp.mean(scaled * normal, axis=-1, keepdims=True)
    return inverse * (scaled - first_mean - normal * second_mean)


class Reduce:
    def __init__(self, place, bufs, sems):
        self.p = place
        self.g, self.s, self.rc, self.ra, self.rb, self.zs, self.rz, self.own = bufs
        self.sems = sems

    @staticmethod
    def scratch(piece, cols, arrays):
        return [
            pltpu.VMEM((2, 4, 2, piece, cols), BF),
            pltpu.VMEM((3, 4, piece, cols), BF),
            pltpu.VMEM((2, 4, piece, cols), BF),
            pltpu.VMEM((3, 2, piece // 2, cols), BF),
            pltpu.VMEM((3, 2, piece, cols), BF),
            pltpu.VMEM((3, piece, cols), BF),
            pltpu.VMEM((arrays, 3, piece, cols), BF),
            pltpu.VMEM((arrays, piece, cols), BF),
        ]

    @staticmethod
    def semaphores(units):
        return [pltpu.SemaphoreType.DMA((units,))] * 12

    def core_copy(self, u):
        other = 1 - self.p.core
        return remote(
            self.g.at[lax.rem(u, 2), :, other],
            self.rc.at[lax.rem(u, 2)],
            self.sems[0],
            self.sems[1],
            u,
            self.p.to_core,
        )

    def corner_copies(self, u):
        p, slot = self.p, lax.rem(u, 3)
        half = self.ra.shape[2]
        return (
            remote(
                self.s.at[slot, p.quad_xy, pl.ds(0, half)],
                self.ra.at[slot, 0],
                self.sems[2],
                self.sems[3],
                u,
                p.to_y,
            ),
            remote(
                self.s.at[slot, p.quad_xy, pl.ds(half, half)],
                self.ra.at[slot, 1],
                self.sems[4],
                self.sems[5],
                u,
                p.to_x,
            ),
        )

    def side_copies(self, u):
        p, slot = self.p, lax.rem(u, 3)
        return (
            remote(
                self.s.at[slot, p.quad_x], self.rb.at[slot, 0], self.sems[6], self.sems[7], u, p.to_x
            ),
            remote(
                self.s.at[slot, p.quad_y], self.rb.at[slot, 1], self.sems[8], self.sems[9], u, p.to_y
            ),
        )

    def z_copy(self, u, array, step):
        return remote(
            self.zs.at[lax.rem(u, 3)],
            self.rz.at[array, step - 1],
            self.sems[10],
            self.sems[11],
            array * 4 + step,
            (self.p.dp, mix(self.p.t, step)),
        )

    def free_g(self, u):
        if not isinstance(u, int):
            pl.when(u >= 2)(lambda: self.core_copy(u - 2).wait_send())
        elif u >= 2:
            self.core_copy(jnp.int32(u - 2)).wait_send()

    def send(self, u):
        self.core_copy(u).start()

    def fold_core(self, u):
        slot = lax.rem(u, 3)

        def freed():
            for copy in self.side_copies(u - 3) + self.corner_copies(u - 3):
                copy.wait_send()

        pl.when(u >= 3)(freed)
        self.core_copy(u).wait_recv()
        mine = self.g[lax.rem(u, 2), :, self.p.core].astype(F32)
        self.s[slot] = (mine + self.rc[lax.rem(u, 2)].astype(F32)).astype(BF)
        for copy in self.corner_copies(u):
            copy.start()

    def fold_corner(self, u):
        p, slot = self.p, lax.rem(u, 3)
        half = self.ra.shape[2]
        for copy in self.corner_copies(u):
            copy.wait_recv()
        lower = self.s[slot, p.quad_x, :half].astype(F32) + self.ra[slot, 0].astype(F32)
        self.s[slot, p.quad_x, :half] = lower.astype(BF)
        upper = self.s[slot, p.quad_y, half:].astype(F32) + self.ra[slot, 1].astype(F32)
        self.s[slot, p.quad_y, half:] = upper.astype(BF)
        for copy in self.side_copies(u):
            copy.start()

    def fold_sides(self, u, array, step, before):
        p, slot = self.p, lax.rem(u, 3)
        for copy in self.side_copies(u):
            copy.wait_recv()
        total = (
            self.s[slot, p.quad].astype(F32)
            + self.rb[slot, 0].astype(F32)
            + self.rb[slot, 1].astype(F32)
        ).astype(BF)

        if before is not None:
            old_array, old_step, valid = before
            pl.when(valid)(lambda: self.z_copy(u - 3, old_array, old_step).wait_send())

        def store():
            self.own[array] = total

        def pass_on():
            self.zs[slot] = total
            self.z_copy(u, array, step).start()

        pl.when(step == 0)(store)
        pl.when(step != 0)(pass_on)

    def finish(self, array):
        total = self.own[array].astype(F32)
        for step in (1, 2, 3):
            self.z_copy(jnp.int32(0), jnp.int32(array), jnp.int32(step)).wait_recv()
            total = total + self.rz[array, step - 1].astype(F32)
        self.own[array] = total.astype(BF)


def layer_kernel(
    len_ref,
    x_hbm,
    cot_hbm,
    vec_ref,
    bias_ref,
    wq_hbm,
    wk_hbm,
    wv_hbm,
    wo_hbm,
    wu_hbm,
    wd_hbm,
    qkv_full,
    out_full,
    up_full,
    down_full,
    q_hbm,
    k_hbm,
    v_hbm,
    outputs_hbm,
    down_grad,
    up_grad,
    proj_grad,
    acc,
    sums_ref,
    x_seq,
    bias_all,
    w_s,
    w_out,
    q_s,
    k_s,
    v_s,
    o_s,
    act_s,
    slope_s,
    wide,
    hidden_s,
    low_s,
    inverse_s,
    lse_s,
    d_att,
    kv_temp,
    rows_recv,
    small,
    small_recv,
    z_send,
    z_recv,
    bias_send,
    bias_recv,
    local,
    load,
    save,
    att_load,
    back_load,
    rows_send_sem,
    rows_recv_sem,
    small_ssem,
    small_rsem,
    *rest,
):
    p = Place()
    reduce = Reduce(p, rest[:8], rest[8:20])
    rows, model = acc.shape
    width = q_s.shape[2]
    half_index = lax.rem(p.t, 2)
    seq = lax.div(p.t, 2)
    own_at = pl.multiple_of(half_index * rows, rows)
    other_at = pl.multiple_of((1 - half_index) * rows, rows)
    own_rows, other_rows = pl.ds(own_at, rows), pl.ds(other_at, rows)
    fulls = [qkv_full, out_full, up_full, down_full]
    spreads = [Spread(p, full, rest[20:30], i) for i, full in enumerate(fulls)]
    QKV, OUT, UP, DOWN = range(4)
    qkv_cols = pl.ds(0, 3 * width)

    def on(step, at, *actions):
        @pl.when(step == at)
        def _():
            for action in actions:
                action()

    def begin(copies):
        for copy in copies:
            copy.start()

    def end(copies):
        for copy in copies:
            copy.wait()

    x_load = pltpu.make_async_copy(
        x_hbm.at[pl.ds(pl.multiple_of(seq * LEN, LEN), LEN)], x_seq, local.at[0]
    )
    own_loads = [
        pltpu.make_async_copy(w, w_s.at[2, :, :, :, pl.ds(i * width, width)], local.at[1 + i])
        for i, w in enumerate((wq_hbm, wk_hbm, wv_hbm))
    ]
    out_load = pltpu.make_async_copy(wo_hbm, w_out.at[0], local.at[4])
    up_load = pltpu.make_async_copy(wu_hbm, w_s.at[0], local.at[5])
    down_load = pltpu.make_async_copy(wd_hbm, w_s.at[0], local.at[6])
    cot_load = pltpu.make_async_copy(cot_hbm, low_s, local.at[7])
    qkv_save = pltpu.make_async_copy(w_s.at[2, :, :, :, qkv_cols], qkv_full.at[p.t], local.at[8])
    up_save = pltpu.make_async_copy(w_s.at[0], up_full.at[p.t], local.at[9])
    outputs_s = reduce.g.at[1, 0:2]
    outputs_save = pltpu.make_async_copy(outputs_s, outputs_hbm, local.at[10])
    begin(own_loads)
    x_load.start()
    out_load.start()
    up_load.start()
    cot_load.start()
    bias_all[p.t] = bias_ref[...]
    p.greet()

    def z_copies(array, step):
        slot = array * 4 + step
        if array == QKV:
            return [
                remote(
                    w.at[p.quad, p.core],
                    qkv_full.at[p.t, p.quad, p.core, :, pl.ds(i * width, width)],
                    z_send,
                    z_recv,
                    slot if i == 0 else 16 + 4 * (i - 1) + step,
                    p.to_z(step),
                )
                for i, w in enumerate((wq_hbm, wk_hbm, wv_hbm))
            ]
        w = (None, wo_hbm, wu_hbm, wd_hbm)[array]
        place = fulls[array].at[p.t, p.quad, p.core]
        return [remote(w.at[p.quad, p.core], place, z_send, z_recv, slot, p.to_z(step))]

    def bias_copy(step):
        return remote(bias_ref, bias_all.at[p.t], bias_send, bias_recv, step, p.to_z(step))

    for step in (1, 2, 3):
        bias_copy(step).start()
    for array in (QKV, OUT, UP, DOWN):
        for step in (1, 2, 3):
            begin(z_copies(array, step))

    def load_copy(array, step):
        if array == QKV:
            dst = w_s.at[2 + step % 2, :, :, :, qkv_cols]
        elif array == OUT:
            dst = w_out.at[step]
        else:
            dst = w_s.at[step]
        src = fulls[array].at[mix(p.t, jnp.int32(step))]
        return pltpu.make_async_copy(src, dst, load.at[array * 4 + step])

    def relay(plan):
        for array, legs in plan:
            spread = spreads[array]
            for leg in legs.split():
                kind, step = leg[0], int(leg[1])
                if kind == "f":
                    for copy in z_copies(array, step):
                        copy.wait_recv()
                    spread.first(step)
                elif kind == "s":
                    spread.second(step)
                elif kind == "t":
                    spread.third(step)
                else:
                    spread.arrived(step)
                    load_copy(array, step).start()

    def passed(step, place):
        plans = {
            (0, "end"): [
                (QKV, "f1 f2 s1 f3 s2"),
                (OUT, "f1"),
                (QKV, "t1"),
                (OUT, "f2 f3"),
                (QKV, "a1 s3"),
            ],
            (1, "mid"): [(QKV, "t2"), (OUT, "s1")],
            (1, "end"): [(OUT, "s2 s3"), (UP, "f1"), (QKV, "a2")],
            (2, "start"): [(QKV, "t3"), (OUT, "t1 t2")],
            (2, "mid"): [(OUT, "t3")],
            (2, "end"): [(QKV, "a3"), (OUT, "a1 a2 a3"), (UP, "f2")],
            (3, "start"): [(UP, "s1 f3")],
            (3, "end"): [(UP, "s2")],
        }
        for (at, where), plan in plans.items():
            if where == place:
                on(step, at, lambda plan=plan: relay(plan))

    def attend_saves(step):
        group, slot = mix(p.t, step), lax.rem(step, 2)
        pairs = ((q_s, q_hbm), (k_s, k_hbm), (v_s, v_hbm))
        return [
            pltpu.make_async_copy(vmem.at[slot], hbm.at[group], save.at[3 * step + i])
            for i, (vmem, hbm) in enumerate(pairs)
        ]

    def attend(step):
        group, slot = mix(p.t, step), lax.rem(step, 2)
        weights = w_s[2 + slot, :, :, :, qkv_cols].reshape(model, 3 * width)
        bias = bias_all[group, 0:1]
        queries = (product(x_seq[own_rows, :], weights[:, :width]) + bias[:, :width]).astype(BF)
        q_s[slot] = (queries.astype(F32) * HD ** (-0.5)).astype(BF)
        k_s[slot] = product(x_seq[...], weights[:, width : 2 * width]).astype(BF)
        v_s[slot] = (
            product(x_seq[...], weights[:, 2 * width :]) + bias[:, width : 2 * width]
        ).astype(BF)
        passed(step, "start")
        length = len_ref[seq]
        key_slot = lax.broadcasted_iota(jnp.int32, (LEN, rows), 0)
        lane = lax.broadcasted_iota(jnp.int32, (rows, PAIR), 1)
        for pair in range(width // PAIR):
            if pair == 1:
                passed(step, "mid")
            cols = slice(pair * PAIR, (pair + 1) * PAIR)
            keys, values, q_pair = k_s[slot, :, cols], v_s[slot, :, cols], q_s[slot, :, cols]
            parts = []
            for head in range(2):
                mine = jnp.where((lane >= HD) == (head == 1), q_pair, jnp.zeros_like(q_pair))
                scores = jnp.where(key_slot < length, product(keys, mine, NT), -1e30)
                top = jnp.max(scores, axis=0, keepdims=True)
                exponent = jnp.exp(scores - top)
                total = jnp.sum(exponent, axis=0, keepdims=True)
                mixed = product(values, exponent.astype(BF), TN)
                parts.append(mixed[head * HD : (head + 1) * HD] * (1.0 / total))
                lse_s[group, pl.ds(pair * 2 + head, 1), :] = top + jnp.log(total)
            o_s[step, :, cols] = jnp.concatenate(parts, axis=0).T.astype(BF)

    x_load.wait()
    end(own_loads)
    qkv_save.start()
    for step in (1, 2, 3):
        bias_copy(step).wait_recv()

    def attend_step(step, carry):
        for i in (1, 2, 3):
            on(step, i, load_copy(QKV, i).wait)
        pl.when(step >= 2)(lambda: end(attend_saves(step - 2)))
        attend(step)
        begin(attend_saves(step))
        on(step, 1, qkv_save.wait)
        passed(step, "end")
        return carry

    lax.fori_loop(0, 4, attend_step, 0)

    out_load.wait()
    for step in (1, 2, 3):
        load_copy(OUT, step).wait()
    acc[...] = x_seq[own_rows, :].astype(F32) + vec_ref[0:1]
    for step in range(4):
        acc[...] += product(o_s[step], w_out[step].reshape(width, model))
    normal1, inverse1 = norm_center(acc[...])
    wide[...] = normal1
    inverse_s[...] = jnp.broadcast_to(inverse1, inverse_s.shape)
    normed1 = normal1 * vec_ref[1:2] + vec_ref[2:3]
    hidden_s[...] = normed1.astype(BF)
    acc[...] = normed1 + vec_ref[3:4]
    relay([(UP, "t1")])

    def up_step(step, carry):
        on(step, 0, up_load.wait, up_save.start)
        for i in (1, 2, 3):
            on(step, i, load_copy(UP, i).wait)
        upper = product(hidden_s[...], w_s[step].reshape(model, model))
        upper = upper + bias_all[mix(p.t, step), 1:2]
        cdf = 0.5 * (1.0 + lax.erf(upper * 0.7071067811865476))
        act_s[step] = (upper * cdf).astype(BF)
        density = jnp.exp(-0.5 * upper * upper) * 0.3989422804014327
        slope_s[step] = (cdf + upper * density).astype(BF)
        on(step, 0, lambda: relay([(UP, "a1 s3"), (DOWN, "f1")]))
        on(step, 1, up_save.wait, down_load.start)
        on(step, 1, lambda: relay([(UP, "t2"), (DOWN, "f2"), (UP, "t3"), (DOWN, "f3"), (UP, "a2")]))
        on(step, 2, lambda: relay([(UP, "a3"), (DOWN, "s1")]))
        on(step, 3, lambda: relay([(DOWN, "s2")]))
        return carry

    lax.fori_loop(0, 4, up_step, 0)
    for step in (2, 3):
        end(attend_saves(jnp.int32(step)))

    def down_step(step, carry):
        on(step, 0, down_load.wait)
        for i in (1, 2, 3):
            on(step, i, load_copy(DOWN, i).wait)
        acc[...] += product(act_s[step], w_s[step].reshape(model, model))
        on(step, 0, lambda: relay([(DOWN, "s3 t1 t2 a1")]))
        on(step, 1, lambda: relay([(DOWN, "t3 a2")]))
        on(step, 2, lambda: relay([(DOWN, "a3")]))
        return carry

    lax.fori_loop(0, 4, down_step, 0)

    cot_load.wait()
    normal2, inverse2 = norm_center(acc[...])
    outputs = (normal2 * vec_ref[4:5] + vec_ref[5:6]).astype(BF)
    reduce.g[1, 0:2] = outputs.reshape(2, 2, rows // 4, model)
    outputs_save.start()
    slot_index = half_index * rows + lax.broadcasted_iota(jnp.int32, (rows, 1), 0)
    grad_out = jnp.where(slot_index < len_ref[seq], low_s[...].astype(F32), 0.0)
    d_second = norm_back(grad_out, normal2, inverse2, vec_ref[4:5])
    acc[...] = d_second
    low_s[...] = d_second.astype(BF)
    small[0] = jnp.zeros(small.shape[1:], F32)
    small[0, 0:1] = jnp.sum(grad_out * normal2, axis=0, keepdims=True)
    small[0, 1:2] = jnp.sum(grad_out, axis=0, keepdims=True)
    small[0, 2:3] = jnp.sum(d_second, axis=0, keepdims=True)

    grads = (down_grad, up_grad, proj_grad)
    back_spreads = [Spread(p, grad, rest[30:40], i) for i, grad in enumerate(grads)]
    for spread in back_spreads:
        spread.block = lambda step: 0
    B_DOWN, B_UP, B_PROJ = range(3)

    def group_at(i):
        return mix(p.t, 3 - i)

    def att_loads(i):
        g, slot = group_at(i), lax.rem(i, 2)
        pairs = ((q_hbm, q_s), (k_hbm, k_s), (v_hbm, v_s))
        return [
            pltpu.make_async_copy(hbm.at[g], vmem.at[slot], att_load.at[4 * i + n])
            for n, (hbm, vmem) in enumerate(pairs)
        ]

    def proj_load(i):
        slot = lax.rem(i, 2)
        return pltpu.make_async_copy(
            qkv_full.at[group_at(i)], w_s.at[slot, :, :, :, qkv_cols], att_load.at[4 * i + 3]
        )

    def up_again(step):
        return pltpu.make_async_copy(up_full.at[mix(p.t, step)], w_s.at[step], back_load.at[step])

    begin(att_loads(jnp.int32(0)))

    def mlp_order(i):
        return 3 - 2 * lax.rem(i, 2) - lax.div(i, 2)

    def unit_of(u):
        if isinstance(u, int) and u >= 8:
            return jnp.int32(B_PROJ), jnp.int32(11 - u)
        u = jnp.int32(u)
        return lax.rem(u, 2), mlp_order(lax.div(u, 2))

    def fold_core(u):
        reduce.fold_core(jnp.int32(u))

    def fold_corner(u):
        reduce.fold_corner(jnp.int32(u))

    def fold_sides(u):
        array, step = unit_of(u)
        if isinstance(u, int):
            old_array, old_step = unit_of(max(u - 3, 0))
            valid = jnp.logical_and(u >= 3, old_step != 0)
            u = jnp.int32(u)
        else:
            old_array, old_step = unit_of(jnp.maximum(u - 3, 0))
            valid = jnp.logical_and(u >= 3, old_step != 0)
        reduce.fold_sides(u, array, step, (old_array, old_step, valid))

    def tick(u):
        pl.when(u >= 4)(lambda: fold_sides(u - 4))
        pl.when(u >= 1)(lambda: fold_core(u - 1))
        reduce.send(u)
        pl.when(u >= 2)(lambda: fold_corner(u - 2))

    def store_unit(slot, left, right):
        part = model // 4
        for quad in range(4):
            terms = product(left(slice(quad * part, (quad + 1) * part)), right, TN)
            reduce.g[slot, quad] = terms.astype(BF).reshape(2, part // 2, right.shape[1])

    def mlp_step(i, carry):
        step = mlp_order(i)
        u = 2 * i
        reduce.free_g(u)
        store_unit(0, lambda cols: act_s[step, :, cols], low_s[...])
        tick(u)
        d_act = product(low_s[...], w_s[step].reshape(model, model), NT)
        d_up = (d_act * slope_s[step].astype(F32)).astype(BF)
        slope_s[step] = d_up
        up_again(step).start()
        at = pl.ds(6 + mix(p.t, step), 1)
        small[0, at, :] = jnp.sum(d_up.astype(F32), axis=0, keepdims=True)
        reduce.free_g(u + 1)
        on(i, 0, outputs_save.wait)
        store_unit(1, lambda cols: hidden_s[:, cols], slope_s[step])
        tick(u + 1)
        up_again(step).wait()
        acc[...] += product(slope_s[step], w_s[step].reshape(model, model), NT)
        return carry

    lax.fori_loop(0, 4, mlp_step, 0)

    proj_load(jnp.int32(0)).start()
    normal1 = wide[...]
    small[0, 3:4] = jnp.sum(acc[...] * normal1, axis=0, keepdims=True)
    small[0, 4:5] = jnp.sum(acc[...], axis=0, keepdims=True)
    d_first = norm_back(acc[...], normal1, inverse_s[:, 0:1], vec_ref[1:2])
    acc[...] = d_first
    low_s[...] = d_first.astype(BF)
    small[0, 5:6] = jnp.sum(d_first, axis=0, keepdims=True)
    d_own, d_other = act_s.at[0], act_s.at[1]

    def attend_back(i):
        slot = lax.rem(i, 2)
        g = group_at(i)
        step = mix(p.t, g)
        length = len_ref[seq]
        d_att[...] = product(low_s[...], w_out[step].reshape(width, model), NT).astype(BF)
        key_slot = lax.broadcasted_iota(jnp.int32, (LEN, rows), 0)
        lane = lax.broadcasted_iota(jnp.int32, (rows, PAIR), 1)
        for pair in range(width // PAIR):
            cols = slice(pair * PAIR, (pair + 1) * PAIR)
            keys, values, queries = k_s[slot, :, cols], v_s[slot, :, cols], q_s[slot, :, cols]
            d_out = d_att[:, cols]
            inner_all = (d_out.astype(F32) * o_s[step, :, cols].astype(F32)).T
            query_parts = []
            for head in range(2):
                mine = (lane >= HD) == (head == 1)
                own_q = jnp.where(mine, queries, jnp.zeros_like(queries))
                own_d = jnp.where(mine, d_out, jnp.zeros_like(d_out))
                inner = jnp.sum(inner_all[head * HD : (head + 1) * HD], axis=0, keepdims=True)
                scores = jnp.where(key_slot < length, product(keys, own_q, NT), -1e30)
                probs = jnp.exp(scores - lse_s[g, pl.ds(pair * 2 + head, 1), :])
                d_probs = product(values, own_d, NT)
                d_scores = (probs * (d_probs - inner) * HD ** (-0.5)).astype(BF)
                d_values = product(probs.astype(BF), own_d)
                d_keys = product(d_scores, own_q) * HD**0.5
                if head == 0:
                    kv_temp[0] = d_keys
                    kv_temp[1] = d_values
                else:
                    kv_temp[0] += d_keys
                    kv_temp[1] += d_values
                query_parts.append(product(keys, d_scores, TN)[head * HD : (head + 1) * HD])
            d_own[:, cols] = jnp.concatenate(query_parts, axis=0).T.astype(BF)
            for n in range(2):
                at = slice((n + 1) * width + pair * PAIR, (n + 1) * width + (pair + 1) * PAIR)
                d_own[:, at] = kv_temp[n, own_rows, :].astype(BF)
                d_other[:, at] = kv_temp[n, other_rows, :].astype(BF)

    def proj_unit(i, u):
        slot = lax.rem(i, 2)
        g = group_at(i)
        qkv, kv = slice(0, 3 * width), slice(width, 3 * width)
        at = pl.ds(10 + g, 1)
        small[0, at, qkv] = jnp.sum(d_own[:, qkv].astype(F32), axis=0, keepdims=True)
        small[0, at, kv] += jnp.sum(d_other[:, kv].astype(F32), axis=0, keepdims=True)
        reduce.core_copy(u - 2).wait_send()
        g_slot = lax.rem(u, 2)
        out_terms = product(o_s[mix(p.t, g)], low_s[...], TN).astype(BF)
        for quad in range(4):
            cols = slice(quad * width, (quad + 1) * width)
            block = (2, width // 2, width)
            x_own, x_other = x_seq[own_rows, cols], x_seq[other_rows, cols]
            queries = product(x_own, d_own[:, :width], TN)
            reduce.g[g_slot, quad, :, :, :width] = queries.astype(BF).reshape(block)
            both = product(x_own, d_own[:, kv], TN) + product(x_other, d_other[:, kv], TN)
            reduce.g[g_slot, quad, :, :, kv] = both.astype(BF).reshape(2, width // 2, 2 * width)
            reduce.g[g_slot, quad, :, :, 3 * width :] = out_terms[:, cols].reshape(block)
        reduce.send(u)
        proj_load(i).wait()
        weights = w_s[slot, :, :, :, qkv_cols].reshape(model, 3 * width)
        acc[...] += product(d_own[:, qkv], weights, NT)
        other = product(d_other[:, kv], weights[:, kv], NT)

        @pl.when(i == 0)
        def _():
            wide[...] = other

        @pl.when(i > 0)
        def _():
            wide[...] += other

    def own_save(array):
        place = grads[array].at[0, p.quad, p.core]
        return pltpu.make_async_copy(reduce.own.at[array], place, local.at[11 + array])

    def start_spread(array):
        reduce.finish(array)
        own_save(array).start()
        back_spreads[array].first(0, reduce.own.at[array])

    def end_spread(array):
        own_save(array).wait()
        back_spreads[array].third(0)

    def att_step(i, carry):
        end(att_loads(i))
        attend_back(i)

        def next_loads():
            begin(att_loads(i + 1))
            proj_load(i + 1).start()

        pl.when(i < 3)(next_loads)

        def passed_back(at):
            fold_sides(4 + at)
            fold_core(7 + at)
            fold_corner(6 + at)
            if at == 2:
                start_spread(B_DOWN)
            if at == 3:
                back_spreads[B_DOWN].second(0)
                start_spread(B_UP)

        for at in range(4):
            on(i, at, lambda at=at: passed_back(at))
        proj_unit(i, i + 8)
        return carry

    lax.fori_loop(0, 4, att_step, 0)
    rows_out = act_s.at[2]
    rows_out[...] = wide[...].astype(BF)
    rows_copy = remote(rows_out, rows_recv, rows_send_sem, rows_recv_sem, 0, p.to_z(1))
    rows_copy.start()
    peers = [p.to_core, p.to_x, p.to_y, p.to_z(1), p.to_z(2)]

    def small_copy(n):
        return remote(small.at[n], small_recv.at[n], small_ssem, small_rsem, n, peers[n])

    def small_next(n):
        small_copy(n).wait_recv()
        small[n + 1] = small[n] + small_recv[n]
        if n < 4:
            small_copy(n + 1).start()

    small_copy(0).start()
    fold_sides(8)
    fold_core(11)
    fold_corner(10)
    end_spread(B_DOWN)
    back_spreads[B_UP].second(0)
    small_next(0)
    fold_sides(9)
    fold_corner(11)
    end_spread(B_UP)
    small_next(1)
    fold_sides(10)
    small_next(2)
    fold_sides(11)
    start_spread(B_PROJ)
    small_next(3)
    back_spreads[B_PROJ].second(0)
    small_next(4)
    end_spread(B_PROJ)
    sums_ref[...] = small[5]

    for step in (1, 2, 3):
        bias_copy(step).wait_send()
        for array in range(4):
            for copy in z_copies(array, step):
                copy.wait_send()
            spreads[array].finish(step)
    rows_copy.wait_recv()
    acc[...] += rows_recv[...].astype(F32)
    rows_copy.wait_send()
    for u in (10, 11):
        reduce.core_copy(jnp.int32(u)).wait_send()
    for u in (9, 10, 11):
        for copy in reduce.side_copies(jnp.int32(u)) + reduce.corner_copies(jnp.int32(u)):
            copy.wait_send()
    for u in (9, 10):
        array, step = unit_of(u)
        reduce.z_copy(jnp.int32(u), array, step).wait_send()
    for n in range(5):
        small_copy(n).wait_send()
    for spread in back_spreads:
        spread.arrived(0)
        spread.finish(0)


def run_layer(lengths, x, cot, vec, bias, wq, wk, wv, wo, wu, wd):
    T = lax.axis_size("tensor")
    model = x.shape[1]
    rows = x.shape[0] // T
    width = wo.shape[0]
    piece = model // GROUP

    def pieces(w):
        return w.reshape(4, 2, w.shape[0] // GROUP, w.shape[1])

    def out(*shape, dtype=BF):
        return jax.ShapeDtypeStruct(shape, dtype)

    anyw = pl.BlockSpec(memory_space=pl.ANY)
    vmem = pl.BlockSpec(memory_space=pltpu.VMEM)
    smem = pl.BlockSpec(memory_space=pltpu.SMEM)
    dma = pltpu.SemaphoreType.DMA
    outs = [
        out(T, 4, 2, piece, 3 * width),
        out(T, 4, 2, width // GROUP, model),
        out(T, 4, 2, piece, model),
        out(T, 4, 2, piece, model),
        out(T, rows, width),
        out(T, LEN, width),
        out(T, LEN, width),
        out(2, 2, rows // 4, model),
        *[out(1, 4, 2, piece, model)] * 3,
        out(rows, model, dtype=F32),
        out(16, model, dtype=F32),
    ]
    return pl.pallas_call(
        layer_kernel,
        in_specs=[smem, anyw, anyw, vmem, vmem] + [anyw] * 6,
        out_specs=[anyw] * 11 + [vmem] * 2,
        out_shape=outs,
        scratch_shapes=[
            pltpu.VMEM((LEN, model), BF),
            pltpu.VMEM((T, 8, model), F32),
            pltpu.VMEM((4, 4, 2, piece, model), BF),
            pltpu.VMEM((T, 4, 2, width // GROUP, model), BF),
            pltpu.VMEM((2, rows, width), BF),
            pltpu.VMEM((2, LEN, width), BF),
            pltpu.VMEM((2, LEN, width), BF),
            pltpu.VMEM((T, rows, width), BF),
            pltpu.VMEM((T, rows, model), BF),
            pltpu.VMEM((T, rows, model), BF),
            pltpu.VMEM((rows, model), F32),
            pltpu.VMEM((rows, model), BF),
            pltpu.VMEM((rows, model), BF),
            pltpu.VMEM((rows, 128), F32),
            pltpu.VMEM((T, 8, rows), F32),
            pltpu.VMEM((rows, width), BF),
            pltpu.VMEM((2, LEN, PAIR), F32),
            pltpu.VMEM((rows, model), BF),
            pltpu.VMEM((6, 16, model), F32),
            pltpu.VMEM((5, 16, model), F32),
            dma((24,)),
            dma((24,)),
            dma((4,)),
            dma((4,)),
            dma((14,)),
            dma((16,)),
            dma((12,)),
            dma((16,)),
            dma((4,)),
            dma((1,)),
            dma((1,)),
            dma((5,)),
            dma((5,)),
            *Reduce.scratch(piece, model, 3),
            *Reduce.semaphores(12),
            *Spread.scratch(4),
            *Spread.scratch(3),
        ],
        compiler_params=pltpu.CompilerParams(
            collective_id=0, has_side_effects=True, vmem_limit_bytes=VMEM_LIMIT
        ),
        cost_estimate=pl.CostEstimate(
            flops=100 * 10**9, bytes_accessed=120 << 20, transcendentals=24 << 20
        ),
        name="layer",
    )(
        lengths,
        x,
        cot,
        vec,
        bias,
        pieces(wq),
        pieces(wk),
        pieces(wv),
        pieces(wo),
        pieces(wu),
        pieces(wd),
    )


def on_device(
    inputs,
    cotangent,
    lengths,
    query_weight,
    key_weight,
    value_weight,
    query_bias,
    value_bias,
    out_weight,
    out_bias,
    norm1_gain,
    norm1_bias,
    up_weight,
    up_bias,
    down_weight,
    down_bias,
    norm2_gain,
    norm2_bias,
):
    t = lax.axis_index("tensor")
    model = inputs.shape[1]
    rows = cotangent.shape[0]
    width = out_weight.shape[0]
    zero_row = jnp.zeros((model,), F32)
    vec = jnp.stack(
        [out_bias, norm1_gain, norm1_bias, down_bias, norm2_gain, norm2_bias, zero_row, zero_row]
    )
    bias = jnp.stack(
        [jnp.concatenate([query_bias, value_bias, zero_row[2 * width :]]), up_bias] + [zero_row] * 6
    )
    results = run_layer(
        lengths,
        inputs,
        cotangent,
        vec,
        bias,
        query_weight,
        key_weight,
        value_weight,
        out_weight,
        up_weight,
        down_weight,
    )
    outputs, down_grad, up_grad, proj_grad, input_grad, sums = results[7:]
    grads = [g.reshape(model, model).astype(F32) for g in (down_grad, up_grad, proj_grad)]
    size = lax.axis_size("dp")
    if size > GROUP:
        groups = [list(range(first, size, GROUP)) for first in range(GROUP)]
        *grads, sums = lax.psum((*grads, sums), "dp", axis_index_groups=groups)
    down_grad, up_grad, proj_grad = grads
    up_bias_grad = lax.dynamic_index_in_dim(sums[6:10], t, 0, keepdims=False)
    proj_bias = lax.dynamic_index_in_dim(sums[10:14], t, 0, keepdims=False)
    out_grad = jnp.concatenate(
        [proj_grad[c * width : (c + 1) * width, 3 * width :] for c in range(4)], axis=1
    )
    return (
        outputs.reshape(rows, model),
        input_grad,
        proj_grad[:, :width],
        proj_grad[:, width : 2 * width],
        proj_grad[:, 2 * width : 3 * width],
        proj_bias[:width],
        proj_bias[2 * width : 3 * width],
        out_grad,
        sums[5],
        sums[3],
        sums[4],
        up_grad,
        up_bias_grad,
        down_grad,
        sums[2],
        sums[0],
        sums[1],
    )


def solution(mesh):
    rows = P(("dp", "tensor"), None)
    by_col = P(None, "tensor")
    by_row = P("tensor", None)
    split = P("tensor")
    whole = P()
    return jax.shard_map(
        on_device,
        mesh=mesh,
        in_specs=(
            P("dp", None),
            rows,
            P("dp"),
            by_col,
            by_col,
            by_col,
            split,
            split,
            by_row,
            whole,
            whole,
            whole,
            by_col,
            split,
            by_row,
            whole,
            whole,
            whole,
        ),
        out_specs=(
            rows,
            rows,
            by_col,
            by_col,
            by_col,
            split,
            split,
            by_row,
            whole,
            whole,
            whole,
            by_col,
            split,
            by_row,
            whole,
            whole,
            whole,
        ),
        check_vma=False,
    )
```

```python
import functools

import jax
import jax.numpy as jnp
from jax import lax
from jax.experimental import pallas as pl
from jax.experimental.pallas import tpu as pltpu
from jax.sharding import PartitionSpec as P

HD = 64
LEN = 1024
PAIR = 2 * HD
GROUP = 8
F32 = jnp.float32
BF = jnp.bfloat16
NN = (((1,), (0,)), ((), ()))
NT = (((1,), (1,)), ((), ()))
TN = (((0,), (0,)), ((), ()))
MESH = pl.DeviceIdType.MESH
VMEM_LIMIT = 63 << 20


def product(left, right, dims=NN):
    return lax.dot_general(left, right, dims, preferred_element_type=F32)


def flip(index, bit):
    return index + bit * (1 - 2 * lax.rem(lax.div(index, bit), 2))


def mix(index, step):
    low = lax.rem(index + step, 2)
    high = lax.rem(lax.div(index, 2) + lax.div(step, 2), 2)
    return 2 * high + low


class Place:
    def __init__(self):
        self.dp = lax.axis_index("dp")
        self.t = lax.axis_index("tensor")
        self.e = lax.rem(self.dp, GROUP)
        self.core = lax.rem(self.e, 2)
        self.quad = lax.div(self.e, 2)
        self.to_core = (flip(self.dp, 1), self.t)
        self.to_x = (flip(self.dp, 2), self.t)
        self.to_y = (flip(self.dp, 4), self.t)
        self.quad_x = flip(self.quad, 1)
        self.quad_y = flip(self.quad, 2)
        self.quad_xy = flip(self.quad_x, 2)

    def to_z(self, step):
        return (self.dp, mix(self.t, jnp.int32(step)))

    def greet(self):
        barrier = pltpu.get_barrier_semaphore()
        peers = [self.to_core, self.to_x, self.to_y, self.to_z(1), self.to_z(2), self.to_z(3)]
        for peer in peers:
            pl.semaphore_signal(barrier, inc=1, device_id=peer, device_id_type=MESH)
        pl.semaphore_wait(barrier, len(peers))


def remote(src, dst, send, recv, index, device):
    return pltpu.make_async_remote_copy(
        src_ref=src,
        dst_ref=dst,
        send_sem=send.at[index],
        recv_sem=recv.at[index],
        device_id=device,
        device_id_type=MESH,
    )


class Spread:
    def __init__(self, place, full, sems, index):
        self.p = place
        self.full = full
        self.sems = sems
        self.index = index

    def block(self, step):
        return mix(self.p.t, jnp.int32(step)) if step else self.p.t

    def slot(self, step):
        return self.index * 4 + step

    def x_copy(self, step, src=None):
        p = self.p
        ref = self.full.at[self.block(step), p.quad, p.core]
        return remote(ref if src is None else src, ref, self.sems[0], self.sems[1], self.slot(step), p.to_x)

    def y_copy(self, step, src=None):
        p = self.p
        ref = self.full.at[self.block(step), p.quad, p.core]
        return remote(ref if src is None else src, ref, self.sems[2], self.sems[3], self.slot(step), p.to_y)

    def half_copies(self, step):
        p = self.p
        half = self.full.shape[3] // 2
        first = self.full.at[self.block(step), p.quad_x, p.core, pl.ds(0, half)]
        second = self.full.at[self.block(step), p.quad_y, p.core, pl.ds(half, half)]
        return (
            remote(first, first, self.sems[4], self.sems[5], self.slot(step), p.to_y),
            remote(second, second, self.sems[6], self.sems[7], self.slot(step), p.to_x),
        )

    def core_copy(self, step):
        p = self.p
        ref = self.full.at[self.block(step), :, p.core]
        return remote(ref, ref, self.sems[8], self.sems[9], self.slot(step), p.to_core)

    def first(self, step, src=None):
        self.x_copy(step, src).start()
        self.y_copy(step, src).start()

    def second(self, step):
        self.x_copy(step).wait_recv()
        self.y_copy(step).wait_recv()
        for copy in self.half_copies(step):
            copy.start()

    def third(self, step):
        for copy in self.half_copies(step):
            copy.wait_recv()
        self.core_copy(step).start()

    def arrived(self, step):
        self.core_copy(step).wait_recv()

    def finish(self, step):
        self.x_copy(step).wait_send()
        self.y_copy(step).wait_send()
        for copy in self.half_copies(step):
            copy.wait_send()
        self.core_copy(step).wait_send()

    @staticmethod
    def scratch(count):
        return [pltpu.SemaphoreType.DMA((4 * count,))] * 10


def norm_center(values):
    center = values - jnp.mean(values, axis=-1, keepdims=True)
    inverse = lax.rsqrt(jnp.mean(center * center, axis=-1, keepdims=True) + 1e-05)
    return center * inverse, inverse


def norm_back(grad, normal, inverse, gain):
    scaled = grad * gain
    first_mean = jnp.mean(scaled, axis=-1, keepdims=True)
    second_mean = jnp.mean(scaled * normal, axis=-1, keepdims=True)
    return inverse * (scaled - first_mean - normal * second_mean)


class Reduce:
    def __init__(self, place, bufs, sems):
        self.p = place
        self.g, self.s, self.rc, self.ra, self.rb, self.zs, self.rz, self.own = bufs
        self.sems = sems

    @staticmethod
    def scratch(piece, cols, arrays):
        return [
            pltpu.VMEM((2, 4, 2, piece, cols), BF),
            pltpu.VMEM((3, 4, piece, cols), BF),
            pltpu.VMEM((2, 4, piece, cols), BF),
            pltpu.VMEM((3, 2, piece // 2, cols), BF),
            pltpu.VMEM((3, 2, piece, cols), BF),
            pltpu.VMEM((3, piece, cols), BF),
            pltpu.VMEM((arrays, 3, piece, cols), BF),
            pltpu.VMEM((arrays, piece, cols), BF),
        ]

    @staticmethod
    def semaphores(units):
        return [pltpu.SemaphoreType.DMA((units,))] * 12

    def core_copy(self, u):
        other = 1 - self.p.core
        return remote(
            self.g.at[lax.rem(u, 2), :, other],
            self.rc.at[lax.rem(u, 2)],
            self.sems[0],
            self.sems[1],
            u,
            self.p.to_core,
        )

    def corner_copies(self, u):
        p, slot = self.p, lax.rem(u, 3)
        half = self.ra.shape[2]
        return (
            remote(
                self.s.at[slot, p.quad_xy, pl.ds(0, half)],
                self.ra.at[slot, 0],
                self.sems[2],
                self.sems[3],
                u,
                p.to_y,
            ),
            remote(
                self.s.at[slot, p.quad_xy, pl.ds(half, half)],
                self.ra.at[slot, 1],
                self.sems[4],
                self.sems[5],
                u,
                p.to_x,
            ),
        )

    def side_copies(self, u):
        p, slot = self.p, lax.rem(u, 3)
        return (
            remote(
                self.s.at[slot, p.quad_x], self.rb.at[slot, 0], self.sems[6], self.sems[7], u, p.to_x
            ),
            remote(
                self.s.at[slot, p.quad_y], self.rb.at[slot, 1], self.sems[8], self.sems[9], u, p.to_y
            ),
        )

    def z_copy(self, u, array, step):
        return remote(
            self.zs.at[lax.rem(u, 3)],
            self.rz.at[array, step - 1],
            self.sems[10],
            self.sems[11],
            array * 4 + step,
            (self.p.dp, mix(self.p.t, step)),
        )

    def free_g(self, u):
        if not isinstance(u, int):
            pl.when(u >= 2)(lambda: self.core_copy(u - 2).wait_send())
        elif u >= 2:
            self.core_copy(jnp.int32(u - 2)).wait_send()

    def send(self, u):
        self.core_copy(u).start()

    def fold_core(self, u):
        slot = lax.rem(u, 3)

        def freed():
            for copy in self.side_copies(u - 3) + self.corner_copies(u - 3):
                copy.wait_send()

        pl.when(u >= 3)(freed)
        self.core_copy(u).wait_recv()
        mine = self.g[lax.rem(u, 2), :, self.p.core].astype(F32)
        self.s[slot] = (mine + self.rc[lax.rem(u, 2)].astype(F32)).astype(BF)
        for copy in self.corner_copies(u):
            copy.start()

    def fold_corner(self, u):
        p, slot = self.p, lax.rem(u, 3)
        half = self.ra.shape[2]
        for copy in self.corner_copies(u):
            copy.wait_recv()
        lower = self.s[slot, p.quad_x, :half].astype(F32) + self.ra[slot, 0].astype(F32)
        self.s[slot, p.quad_x, :half] = lower.astype(BF)
        upper = self.s[slot, p.quad_y, half:].astype(F32) + self.ra[slot, 1].astype(F32)
        self.s[slot, p.quad_y, half:] = upper.astype(BF)
        for copy in self.side_copies(u):
            copy.start()

    def fold_sides(self, u, array, step, before):
        p, slot = self.p, lax.rem(u, 3)
        for copy in self.side_copies(u):
            copy.wait_recv()
        total = (
            self.s[slot, p.quad].astype(F32)
            + self.rb[slot, 0].astype(F32)
            + self.rb[slot, 1].astype(F32)
        ).astype(BF)

        if before is not None:
            old_array, old_step, valid = before
            pl.when(valid)(lambda: self.z_copy(u - 3, old_array, old_step).wait_send())

        def store():
            self.own[array] = total

        def pass_on():
            self.zs[slot] = total
            self.z_copy(u, array, step).start()

        pl.when(step == 0)(store)
        pl.when(step != 0)(pass_on)

    def finish(self, array):
        total = self.own[array].astype(F32)
        for step in (1, 2, 3):
            self.z_copy(jnp.int32(0), jnp.int32(array), jnp.int32(step)).wait_recv()
            total = total + self.rz[array, step - 1].astype(F32)
        self.own[array] = total.astype(BF)


def layer_kernel(
    len_ref,
    x_hbm,
    cot_hbm,
    out_bias_ref,
    gain1_ref,
    shift1_ref,
    down_bias_ref,
    gain2_ref,
    shift2_ref,
    query_bias_ref,
    value_bias_ref,
    up_bias_ref,
    wq_hbm,
    wk_hbm,
    wv_hbm,
    wo_hbm,
    wu_hbm,
    wd_hbm,
    qkv_full,
    out_full,
    up_full,
    down_full,
    q_hbm,
    k_hbm,
    v_hbm,
    outputs_hbm,
    down_grad,
    up_grad,
    proj_grad,
    acc,
    sums_ref,
    x_seq,
    bias_s,
    bias_all,
    w_s,
    w_out,
    q_s,
    k_s,
    v_s,
    o_s,
    act_s,
    slope_s,
    wide,
    hidden_s,
    low_s,
    inverse_s,
    lse_s,
    d_att,
    kv_temp,
    rows_recv,
    small,
    small_recv,
    z_send,
    z_recv,
    bias_send,
    bias_recv,
    local,
    load,
    save,
    att_load,
    back_load,
    rows_send_sem,
    rows_recv_sem,
    small_ssem,
    small_rsem,
    *rest,
):
    p = Place()
    reduce = Reduce(p, rest[:8], rest[8:20])
    rows, model = acc.shape
    width = q_s.shape[2]
    half_index = lax.rem(p.t, 2)
    seq = lax.div(p.t, 2)
    own_at = pl.multiple_of(half_index * rows, rows)
    other_at = pl.multiple_of((1 - half_index) * rows, rows)
    own_rows, other_rows = pl.ds(own_at, rows), pl.ds(other_at, rows)
    fulls = [qkv_full, out_full, up_full, down_full]
    spreads = [Spread(p, full, rest[20:30], i) for i, full in enumerate(fulls)]
    QKV, OUT, UP, DOWN = range(4)
    qkv_cols = pl.ds(0, 3 * width)

    def on(step, at, *actions):
        @pl.when(step == at)
        def _():
            for action in actions:
                action()

    def begin(copies):
        for copy in copies:
            copy.start()

    def end(copies):
        for copy in copies:
            copy.wait()

    x_load = pltpu.make_async_copy(
        x_hbm.at[pl.ds(pl.multiple_of(seq * LEN, LEN), LEN)], x_seq, local.at[0]
    )
    own_loads = [
        pltpu.make_async_copy(w, w_s.at[2, :, :, :, pl.ds(i * width, width)], local.at[1 + i])
        for i, w in enumerate((wq_hbm, wk_hbm, wv_hbm))
    ]
    out_load = pltpu.make_async_copy(wo_hbm, w_out.at[0], local.at[4])
    up_load = pltpu.make_async_copy(wu_hbm, w_s.at[0], local.at[5])
    down_load = pltpu.make_async_copy(wd_hbm, w_s.at[0], local.at[6])
    cot_load = pltpu.make_async_copy(cot_hbm, low_s, local.at[7])
    qkv_save = pltpu.make_async_copy(w_s.at[2, :, :, :, qkv_cols], qkv_full.at[p.t], local.at[8])
    up_save = pltpu.make_async_copy(w_s.at[0], up_full.at[p.t], local.at[9])
    outputs_s = reduce.g.at[1, 0:2]
    outputs_save = pltpu.make_async_copy(outputs_s, outputs_hbm, local.at[10])
    begin(own_loads)
    x_load.start()
    out_load.start()
    up_load.start()
    cot_load.start()
    bias_s[...] = jnp.zeros(bias_s.shape, F32)
    bias_s[0:1, :width] = query_bias_ref[...]
    bias_s[0:1, width : 2 * width] = value_bias_ref[...]
    bias_s[1:2] = up_bias_ref[...]
    bias_all[p.t] = bias_s[...]
    p.greet()

    def z_copies(array, step):
        slot = array * 4 + step
        if array == QKV:
            return [
                remote(
                    w.at[p.quad, p.core],
                    qkv_full.at[p.t, p.quad, p.core, :, pl.ds(i * width, width)],
                    z_send,
                    z_recv,
                    slot if i == 0 else 16 + 4 * (i - 1) + step,
                    p.to_z(step),
                )
                for i, w in enumerate((wq_hbm, wk_hbm, wv_hbm))
            ]
        w = (None, wo_hbm, wu_hbm, wd_hbm)[array]
        place = fulls[array].at[p.t, p.quad, p.core]
        return [remote(w.at[p.quad, p.core], place, z_send, z_recv, slot, p.to_z(step))]

    def bias_copy(step):
        return remote(bias_s, bias_all.at[p.t], bias_send, bias_recv, step, p.to_z(step))

    for step in (1, 2, 3):
        bias_copy(step).start()
    for array in (QKV, OUT, UP, DOWN):
        for step in (1, 2, 3):
            begin(z_copies(array, step))

    def load_copy(array, step):
        if array == QKV:
            dst = w_s.at[2 + step % 2, :, :, :, qkv_cols]
        elif array == OUT:
            dst = w_out.at[step]
        else:
            dst = w_s.at[step]
        src = fulls[array].at[mix(p.t, jnp.int32(step))]
        return pltpu.make_async_copy(src, dst, load.at[array * 4 + step])

    def relay(plan):
        for array, legs in plan:
            spread = spreads[array]
            for leg in legs.split():
                kind, step = leg[0], int(leg[1])
                if kind == "f":
                    for copy in z_copies(array, step):
                        copy.wait_recv()
                    spread.first(step)
                elif kind == "s":
                    spread.second(step)
                elif kind == "t":
                    spread.third(step)
                else:
                    spread.arrived(step)
                    load_copy(array, step).start()

    def passed(step, place):
        plans = {
            (0, "end"): [
                (QKV, "f1 f2 s1 f3 s2"),
                (OUT, "f1"),
                (QKV, "t1"),
                (OUT, "f2 f3"),
                (QKV, "a1 s3"),
            ],
            (1, "mid"): [(QKV, "t2"), (OUT, "s1")],
            (1, "end"): [(OUT, "s2 s3"), (UP, "f1"), (QKV, "a2")],
            (2, "start"): [(QKV, "t3"), (OUT, "t1 t2")],
            (2, "mid"): [(OUT, "t3")],
            (2, "end"): [(QKV, "a3"), (OUT, "a1 a2 a3"), (UP, "f2")],
            (3, "start"): [(UP, "s1 f3")],
            (3, "end"): [(UP, "s2")],
        }
        for (at, where), plan in plans.items():
            if where == place:
                on(step, at, lambda plan=plan: relay(plan))

    def attend_saves(step):
        group, slot = mix(p.t, step), lax.rem(step, 2)
        pairs = ((q_s, q_hbm), (k_s, k_hbm), (v_s, v_hbm))
        return [
            pltpu.make_async_copy(vmem.at[slot], hbm.at[group], save.at[3 * step + i])
            for i, (vmem, hbm) in enumerate(pairs)
        ]

    def attend(step):
        group, slot = mix(p.t, step), lax.rem(step, 2)
        weights = w_s[2 + slot, :, :, :, qkv_cols].reshape(model, 3 * width)
        bias = bias_all[group, 0:1]
        queries = (product(x_seq[own_rows, :], weights[:, :width]) + bias[:, :width]).astype(BF)
        q_s[slot] = (queries.astype(F32) * HD ** (-0.5)).astype(BF)
        k_s[slot] = product(x_seq[...], weights[:, width : 2 * width]).astype(BF)
        v_s[slot] = (
            product(x_seq[...], weights[:, 2 * width :]) + bias[:, width : 2 * width]
        ).astype(BF)
        passed(step, "start")
        length = len_ref[seq]
        key_slot = lax.broadcasted_iota(jnp.int32, (LEN, rows), 0)
        lane = lax.broadcasted_iota(jnp.int32, (rows, PAIR), 1)
        for pair in range(width // PAIR):
            if pair == 1:
                passed(step, "mid")
            cols = slice(pair * PAIR, (pair + 1) * PAIR)
            keys, values, q_pair = k_s[slot, :, cols], v_s[slot, :, cols], q_s[slot, :, cols]
            parts = []
            for head in range(2):
                mine = jnp.where((lane >= HD) == (head == 1), q_pair, jnp.zeros_like(q_pair))
                scores = jnp.where(key_slot < length, product(keys, mine, NT), -1e30)
                top = jnp.max(scores, axis=0, keepdims=True)
                exponent = jnp.exp(scores - top)
                total = jnp.sum(exponent, axis=0, keepdims=True)
                mixed = product(values, exponent.astype(BF), TN)
                parts.append(mixed[head * HD : (head + 1) * HD] * (1.0 / total))
                lse_s[group, pl.ds(pair * 2 + head, 1), :] = top + jnp.log(total)
            o_s[step, :, cols] = jnp.concatenate(parts, axis=0).T.astype(BF)

    x_load.wait()
    end(own_loads)
    qkv_save.start()
    for step in (1, 2, 3):
        bias_copy(step).wait_recv()

    def attend_step(step, carry):
        for i in (1, 2, 3):
            on(step, i, load_copy(QKV, i).wait)
        pl.when(step >= 2)(lambda: end(attend_saves(step - 2)))
        attend(step)
        begin(attend_saves(step))
        on(step, 1, qkv_save.wait)
        passed(step, "end")
        return carry

    lax.fori_loop(0, 4, attend_step, 0)

    out_load.wait()
    for step in (1, 2, 3):
        load_copy(OUT, step).wait()
    acc[...] = x_seq[own_rows, :].astype(F32) + out_bias_ref[...]
    for step in range(4):
        acc[...] += product(o_s[step], w_out[step].reshape(width, model))
    normal1, inverse1 = norm_center(acc[...])
    wide[...] = normal1
    inverse_s[...] = jnp.broadcast_to(inverse1, inverse_s.shape)
    normed1 = normal1 * gain1_ref[...] + shift1_ref[...]
    hidden_s[...] = normed1.astype(BF)
    acc[...] = normed1 + down_bias_ref[...]
    relay([(UP, "t1")])

    def up_step(step, carry):
        on(step, 0, up_load.wait, up_save.start)
        for i in (1, 2, 3):
            on(step, i, load_copy(UP, i).wait)
        upper = product(hidden_s[...], w_s[step].reshape(model, model))
        upper = upper + bias_all[mix(p.t, step), 1:2]
        cdf = 0.5 * (1.0 + lax.erf(upper * 0.7071067811865476))
        act_s[step] = (upper * cdf).astype(BF)
        density = jnp.exp(-0.5 * upper * upper) * 0.3989422804014327
        slope_s[step] = (cdf + upper * density).astype(BF)
        on(step, 0, lambda: relay([(UP, "a1 s3"), (DOWN, "f1")]))
        on(step, 1, up_save.wait, down_load.start)
        on(step, 1, lambda: relay([(UP, "t2"), (DOWN, "f2"), (UP, "t3"), (DOWN, "f3"), (UP, "a2")]))
        on(step, 2, lambda: relay([(UP, "a3"), (DOWN, "s1")]))
        on(step, 3, lambda: relay([(DOWN, "s2")]))
        return carry

    lax.fori_loop(0, 4, up_step, 0)
    for step in (2, 3):
        end(attend_saves(jnp.int32(step)))

    def down_step(step, carry):
        on(step, 0, down_load.wait)
        for i in (1, 2, 3):
            on(step, i, load_copy(DOWN, i).wait)
        acc[...] += product(act_s[step], w_s[step].reshape(model, model))
        on(step, 0, lambda: relay([(DOWN, "s3 t1 t2 a1")]))
        on(step, 1, lambda: relay([(DOWN, "t3 a2")]))
        on(step, 2, lambda: relay([(DOWN, "a3")]))
        return carry

    lax.fori_loop(0, 4, down_step, 0)

    cot_load.wait()
    normal2, inverse2 = norm_center(acc[...])
    outputs = (normal2 * gain2_ref[...] + shift2_ref[...]).astype(BF)
    reduce.g[1, 0:2] = outputs.reshape(2, 2, rows // 4, model)
    outputs_save.start()
    slot_index = half_index * rows + lax.broadcasted_iota(jnp.int32, (rows, 1), 0)
    grad_out = jnp.where(slot_index < len_ref[seq], low_s[...].astype(F32), 0.0)
    d_second = norm_back(grad_out, normal2, inverse2, gain2_ref[...])
    acc[...] = d_second
    low_s[...] = d_second.astype(BF)
    small[0] = jnp.zeros(small.shape[1:], F32)
    small[0, 0:1] = jnp.sum(grad_out * normal2, axis=0, keepdims=True)
    small[0, 1:2] = jnp.sum(grad_out, axis=0, keepdims=True)
    small[0, 2:3] = jnp.sum(d_second, axis=0, keepdims=True)

    grads = (down_grad, up_grad, proj_grad)
    back_spreads = [Spread(p, grad, rest[30:40], i) for i, grad in enumerate(grads)]
    for spread in back_spreads:
        spread.block = lambda step: 0
    B_DOWN, B_UP, B_PROJ = range(3)

    def group_at(i):
        return mix(p.t, 3 - i)

    def att_loads(i):
        g, slot = group_at(i), lax.rem(i, 2)
        pairs = ((q_hbm, q_s), (k_hbm, k_s), (v_hbm, v_s))
        return [
            pltpu.make_async_copy(hbm.at[g], vmem.at[slot], att_load.at[4 * i + n])
            for n, (hbm, vmem) in enumerate(pairs)
        ]

    def proj_load(i):
        slot = lax.rem(i, 2)
        return pltpu.make_async_copy(
            qkv_full.at[group_at(i)], w_s.at[slot, :, :, :, qkv_cols], att_load.at[4 * i + 3]
        )

    def up_again(step):
        return pltpu.make_async_copy(up_full.at[mix(p.t, step)], w_s.at[step], back_load.at[step])

    begin(att_loads(jnp.int32(0)))

    def mlp_order(i):
        return 3 - 2 * lax.rem(i, 2) - lax.div(i, 2)

    def unit_of(u):
        if isinstance(u, int) and u >= 8:
            return jnp.int32(B_PROJ), jnp.int32(11 - u)
        u = jnp.int32(u)
        return lax.rem(u, 2), mlp_order(lax.div(u, 2))

    def fold_core(u):
        reduce.fold_core(jnp.int32(u))

    def fold_corner(u):
        reduce.fold_corner(jnp.int32(u))

    def fold_sides(u):
        array, step = unit_of(u)
        if isinstance(u, int):
            old_array, old_step = unit_of(max(u - 3, 0))
            valid = jnp.logical_and(u >= 3, old_step != 0)
            u = jnp.int32(u)
        else:
            old_array, old_step = unit_of(jnp.maximum(u - 3, 0))
            valid = jnp.logical_and(u >= 3, old_step != 0)
        reduce.fold_sides(u, array, step, (old_array, old_step, valid))

    def tick(u):
        pl.when(u >= 4)(lambda: fold_sides(u - 4))
        pl.when(u >= 1)(lambda: fold_core(u - 1))
        reduce.send(u)
        pl.when(u >= 2)(lambda: fold_corner(u - 2))

    def store_unit(slot, left, right):
        part = model // 4
        for quad in range(4):
            terms = product(left(slice(quad * part, (quad + 1) * part)), right, TN)
            reduce.g[slot, quad] = terms.astype(BF).reshape(2, part // 2, right.shape[1])

    def mlp_step(i, carry):
        step = mlp_order(i)
        u = 2 * i
        reduce.free_g(u)
        store_unit(0, lambda cols: act_s[step, :, cols], low_s[...])
        tick(u)
        d_act = product(low_s[...], w_s[step].reshape(model, model), NT)
        d_up = (d_act * slope_s[step].astype(F32)).astype(BF)
        slope_s[step] = d_up
        up_again(step).start()
        at = pl.ds(6 + mix(p.t, step), 1)
        small[0, at, :] = jnp.sum(d_up.astype(F32), axis=0, keepdims=True)
        reduce.free_g(u + 1)
        on(i, 0, outputs_save.wait)
        store_unit(1, lambda cols: hidden_s[:, cols], slope_s[step])
        tick(u + 1)
        up_again(step).wait()
        acc[...] += product(slope_s[step], w_s[step].reshape(model, model), NT)
        return carry

    lax.fori_loop(0, 4, mlp_step, 0)

    proj_load(jnp.int32(0)).start()
    normal1 = wide[...]
    small[0, 3:4] = jnp.sum(acc[...] * normal1, axis=0, keepdims=True)
    small[0, 4:5] = jnp.sum(acc[...], axis=0, keepdims=True)
    d_first = norm_back(acc[...], normal1, inverse_s[:, 0:1], gain1_ref[...])
    acc[...] = d_first
    low_s[...] = d_first.astype(BF)
    small[0, 5:6] = jnp.sum(d_first, axis=0, keepdims=True)
    d_own, d_other = act_s.at[0], act_s.at[1]

    def attend_back(i):
        slot = lax.rem(i, 2)
        g = group_at(i)
        step = mix(p.t, g)
        length = len_ref[seq]
        d_att[...] = product(low_s[...], w_out[step].reshape(width, model), NT).astype(BF)
        key_slot = lax.broadcasted_iota(jnp.int32, (LEN, rows), 0)
        lane = lax.broadcasted_iota(jnp.int32, (rows, PAIR), 1)
        for pair in range(width // PAIR):
            cols = slice(pair * PAIR, (pair + 1) * PAIR)
            keys, values, queries = k_s[slot, :, cols], v_s[slot, :, cols], q_s[slot, :, cols]
            d_out = d_att[:, cols]
            inner_all = (d_out.astype(F32) * o_s[step, :, cols].astype(F32)).T
            query_parts = []
            for head in range(2):
                mine = (lane >= HD) == (head == 1)
                own_q = jnp.where(mine, queries, jnp.zeros_like(queries))
                own_d = jnp.where(mine, d_out, jnp.zeros_like(d_out))
                inner = jnp.sum(inner_all[head * HD : (head + 1) * HD], axis=0, keepdims=True)
                scores = jnp.where(key_slot < length, product(keys, own_q, NT), -1e30)
                probs = jnp.exp(scores - lse_s[g, pl.ds(pair * 2 + head, 1), :])
                d_probs = product(values, own_d, NT)
                d_scores = (probs * (d_probs - inner) * HD ** (-0.5)).astype(BF)
                d_values = product(probs.astype(BF), own_d)
                d_keys = product(d_scores, own_q) * HD**0.5
                if head == 0:
                    kv_temp[0] = d_keys
                    kv_temp[1] = d_values
                else:
                    kv_temp[0] += d_keys
                    kv_temp[1] += d_values
                query_parts.append(product(keys, d_scores, TN)[head * HD : (head + 1) * HD])
            d_own[:, cols] = jnp.concatenate(query_parts, axis=0).T.astype(BF)
            for n in range(2):
                at = slice((n + 1) * width + pair * PAIR, (n + 1) * width + (pair + 1) * PAIR)
                d_own[:, at] = kv_temp[n, own_rows, :].astype(BF)
                d_other[:, at] = kv_temp[n, other_rows, :].astype(BF)

    def proj_unit(i, u):
        slot = lax.rem(i, 2)
        g = group_at(i)
        qkv, kv = slice(0, 3 * width), slice(width, 3 * width)
        at = pl.ds(10 + g, 1)
        small[0, at, qkv] = jnp.sum(d_own[:, qkv].astype(F32), axis=0, keepdims=True)
        small[0, at, kv] += jnp.sum(d_other[:, kv].astype(F32), axis=0, keepdims=True)
        reduce.core_copy(u - 2).wait_send()
        g_slot = lax.rem(u, 2)
        out_terms = product(o_s[mix(p.t, g)], low_s[...], TN).astype(BF)
        for quad in range(4):
            cols = slice(quad * width, (quad + 1) * width)
            block = (2, width // 2, width)
            x_own, x_other = x_seq[own_rows, cols], x_seq[other_rows, cols]
            queries = product(x_own, d_own[:, :width], TN)
            reduce.g[g_slot, quad, :, :, :width] = queries.astype(BF).reshape(block)
            both = product(x_own, d_own[:, kv], TN) + product(x_other, d_other[:, kv], TN)
            reduce.g[g_slot, quad, :, :, kv] = both.astype(BF).reshape(2, width // 2, 2 * width)
            reduce.g[g_slot, quad, :, :, 3 * width :] = out_terms[:, cols].reshape(block)
        reduce.send(u)
        proj_load(i).wait()
        weights = w_s[slot, :, :, :, qkv_cols].reshape(model, 3 * width)
        acc[...] += product(d_own[:, qkv], weights, NT)
        other = product(d_other[:, kv], weights[:, kv], NT)

        @pl.when(i == 0)
        def _():
            wide[...] = other

        @pl.when(i > 0)
        def _():
            wide[...] += other

    def own_save(array):
        place = grads[array].at[0, p.quad, p.core]
        return pltpu.make_async_copy(reduce.own.at[array], place, local.at[11 + array])

    def start_spread(array):
        reduce.finish(array)
        own_save(array).start()
        back_spreads[array].first(0, reduce.own.at[array])

    def end_spread(array):
        own_save(array).wait()
        back_spreads[array].third(0)

    def att_step(i, carry):
        end(att_loads(i))
        attend_back(i)

        def next_loads():
            begin(att_loads(i + 1))
            proj_load(i + 1).start()

        pl.when(i < 3)(next_loads)

        def passed_back(at):
            fold_sides(4 + at)
            fold_core(7 + at)
            fold_corner(6 + at)
            if at == 2:
                start_spread(B_DOWN)
            if at == 3:
                back_spreads[B_DOWN].second(0)
                start_spread(B_UP)

        for at in range(4):
            on(i, at, lambda at=at: passed_back(at))
        proj_unit(i, i + 8)
        return carry

    lax.fori_loop(0, 4, att_step, 0)
    rows_out = act_s.at[2]
    rows_out[...] = wide[...].astype(BF)

    def rows_copy(part):
        at = pl.ds(part * (rows // 4), rows // 4)
        return remote(
            rows_out.at[at], rows_recv.at[at], rows_send_sem, rows_recv_sem, part, p.to_z(1)
        )

    rows_copy(0).start()
    rows_copy(1).start()
    peers = [p.to_core, p.to_x, p.to_y, p.to_z(1), p.to_z(2)]

    def small_copy(n):
        return remote(small.at[n], small_recv.at[n], small_ssem, small_rsem, n, peers[n])

    def small_next(n):
        small_copy(n).wait_recv()
        small[n + 1] = small[n] + small_recv[n]
        if n < 4:
            small_copy(n + 1).start()

    small_copy(0).start()
    fold_sides(8)
    fold_core(11)
    fold_corner(10)
    end_spread(B_DOWN)
    back_spreads[B_UP].second(0)
    small_next(0)
    fold_sides(9)
    rows_copy(2).start()
    fold_corner(11)
    end_spread(B_UP)
    small_next(1)
    fold_sides(10)
    rows_copy(3).start()
    small_next(2)
    fold_sides(11)
    start_spread(B_PROJ)
    small_next(3)
    back_spreads[B_PROJ].second(0)
    small_next(4)
    end_spread(B_PROJ)
    sums_ref[...] = small[5]

    for step in (1, 2, 3):
        bias_copy(step).wait_send()
        for array in range(4):
            for copy in z_copies(array, step):
                copy.wait_send()
            spreads[array].finish(step)
    for part in range(4):
        rows_copy(part).wait()
    acc[...] += rows_recv[...].astype(F32)
    for u in (10, 11):
        reduce.core_copy(jnp.int32(u)).wait_send()
    for u in (9, 10, 11):
        for copy in reduce.side_copies(jnp.int32(u)) + reduce.corner_copies(jnp.int32(u)):
            copy.wait_send()
    for u in (9, 10):
        array, step = unit_of(u)
        reduce.z_copy(jnp.int32(u), array, step).wait_send()
    for n in range(5):
        small_copy(n).wait_send()
    for spread in back_spreads:
        spread.arrived(0)
        spread.finish(0)


def run_layer(lengths, x, cot, vectors, wq, wk, wv, wo, wu, wd):
    T = lax.axis_size("tensor")
    model = x.shape[1]
    rows = x.shape[0] // T
    width = wo.shape[0]
    piece = model // GROUP

    def pieces(w):
        return w.reshape(4, 2, w.shape[0] // GROUP, w.shape[1])

    def out(*shape, dtype=BF):
        return jax.ShapeDtypeStruct(shape, dtype)

    anyw = pl.BlockSpec(memory_space=pl.ANY)
    vmem = pl.BlockSpec(memory_space=pltpu.VMEM)
    smem = pl.BlockSpec(memory_space=pltpu.SMEM)
    dma = pltpu.SemaphoreType.DMA
    outs = [
        out(T, 4, 2, piece, 3 * width),
        out(T, 4, 2, width // GROUP, model),
        out(T, 4, 2, piece, model),
        out(T, 4, 2, piece, model),
        out(T, rows, width),
        out(T, LEN, width),
        out(T, LEN, width),
        out(2, 2, rows // 4, model),
        *[out(1, 4, 2, piece, model)] * 3,
        out(rows, model, dtype=F32),
        out(16, model, dtype=F32),
    ]
    return pl.pallas_call(
        layer_kernel,
        in_specs=[smem, anyw, anyw] + [vmem] * 9 + [anyw] * 6,
        out_specs=[anyw] * 11 + [vmem] * 2,
        out_shape=outs,
        scratch_shapes=[
            pltpu.VMEM((LEN, model), BF),
            pltpu.VMEM((8, model), F32),
            pltpu.VMEM((T, 8, model), F32),
            pltpu.VMEM((4, 4, 2, piece, model), BF),
            pltpu.VMEM((T, 4, 2, width // GROUP, model), BF),
            pltpu.VMEM((2, rows, width), BF),
            pltpu.VMEM((2, LEN, width), BF),
            pltpu.VMEM((2, LEN, width), BF),
            pltpu.VMEM((T, rows, width), BF),
            pltpu.VMEM((T, rows, model), BF),
            pltpu.VMEM((T, rows, model), BF),
            pltpu.VMEM((rows, model), F32),
            pltpu.VMEM((rows, model), BF),
            pltpu.VMEM((rows, model), BF),
            pltpu.VMEM((rows, 128), F32),
            pltpu.VMEM((T, 8, rows), F32),
            pltpu.VMEM((rows, width), BF),
            pltpu.VMEM((2, LEN, PAIR), F32),
            pltpu.VMEM((rows, model), BF),
            pltpu.VMEM((6, 16, model), F32),
            pltpu.VMEM((5, 16, model), F32),
            dma((24,)),
            dma((24,)),
            dma((4,)),
            dma((4,)),
            dma((14,)),
            dma((16,)),
            dma((12,)),
            dma((16,)),
            dma((4,)),
            dma((4,)),
            dma((4,)),
            dma((5,)),
            dma((5,)),
            *Reduce.scratch(piece, model, 3),
            *Reduce.semaphores(12),
            *Spread.scratch(4),
            *Spread.scratch(3),
        ],
        compiler_params=pltpu.CompilerParams(
            collective_id=0, has_side_effects=True, vmem_limit_bytes=VMEM_LIMIT
        ),
        cost_estimate=pl.CostEstimate(
            flops=100 * 10**9, bytes_accessed=120 << 20, transcendentals=24 << 20
        ),
        name="layer",
    )(
        lengths,
        x,
        cot,
        *[v.reshape(1, -1) for v in vectors],
        pieces(wq),
        pieces(wk),
        pieces(wv),
        pieces(wo),
        pieces(wu),
        pieces(wd),
    )


def results_kernel(
    outputs_in,
    down_in,
    up_in,
    proj_in,
    input_in,
    sums_in,
    outputs_ref,
    input_ref,
    query_ref,
    key_ref,
    value_ref,
    query_bias_ref,
    value_bias_ref,
    out_ref,
    out_bias_ref,
    gain1_ref,
    shift1_ref,
    up_ref,
    up_bias_ref,
    down_ref,
    down_bias_ref,
    gain2_ref,
    shift2_ref,
):
    t = lax.axis_index("tensor")
    width = query_ref.shape[1]
    outputs_ref[...] = outputs_in[...]
    input_ref[...] = input_in[...]
    down_ref[...] = down_in[...].astype(F32)
    up_ref[...] = up_in[...].astype(F32)
    for n, ref in enumerate((query_ref, key_ref, value_ref, out_ref)):
        ref[...] = proj_in[:, n * width : (n + 1) * width].astype(F32)
    rows = (gain2_ref, shift2_ref, down_bias_ref, gain1_ref, shift1_ref, out_bias_ref)
    for n, ref in enumerate(rows):
        ref[...] = sums_in[n : n + 1]
    up_bias_ref[...] = sums_in[pl.ds(6 + t, 1), :]
    proj = sums_in[pl.ds(10 + t, 1), :]
    query_bias_ref[...] = proj[:, :width]
    value_bias_ref[...] = proj[:, 2 * width : 3 * width]


def run_results(outputs, down, up, proj, input_grad, sums, width):
    rows, model = outputs.shape
    steps = 4
    tall = lambda count, cols=model: pl.BlockSpec((count // steps, cols), lambda i: (i, 0))
    row = lambda cols=model: pl.BlockSpec((1, cols), lambda i: (0, 0))
    out = lambda count, cols=model, dtype=F32: jax.ShapeDtypeStruct((count, cols), dtype)
    whole = pl.BlockSpec(sums.shape, lambda i: (0, 0))
    outs = [
        (out(rows, dtype=BF), tall(rows)),
        (out(rows), tall(rows)),
        *[(out(model, width), tall(model, width))] * 3,
        *[(out(1, width), row(width))] * 2,
        (out(width), pl.BlockSpec((width, model // steps), lambda i: (0, i))),
        *[(out(1), row())] * 3,
        (out(model), tall(model)),
        (out(1), row()),
        (out(model), tall(model)),
        *[(out(1), row())] * 3,
    ]
    return pl.pallas_call(
        results_kernel,
        grid=(steps,),
        in_specs=[tall(rows), tall(model), tall(model), tall(model), tall(rows), whole],
        out_specs=[spec for _, spec in outs],
        out_shape=[shape for shape, _ in outs],
        compiler_params=pltpu.CompilerParams(vmem_limit_bytes=VMEM_LIMIT),
        name="results",
    )(outputs, down, up, proj, input_grad, sums)


def on_device(
    inputs,
    cotangent,
    lengths,
    query_weight,
    key_weight,
    value_weight,
    query_bias,
    value_bias,
    out_weight,
    out_bias,
    norm1_gain,
    norm1_bias,
    up_weight,
    up_bias,
    down_weight,
    down_bias,
    norm2_gain,
    norm2_bias,
):
    model = inputs.shape[1]
    rows = cotangent.shape[0]
    width = out_weight.shape[0]
    results = run_layer(
        lengths,
        inputs,
        cotangent,
        (
            out_bias,
            norm1_gain,
            norm1_bias,
            down_bias,
            norm2_gain,
            norm2_bias,
            query_bias,
            value_bias,
            up_bias,
        ),
        query_weight,
        key_weight,
        value_weight,
        out_weight,
        up_weight,
        down_weight,
    )
    outputs, down_grad, up_grad, proj_grad, input_grad, sums = results[7:]
    grads = [g.reshape(model, model) for g in (down_grad, up_grad, proj_grad)]
    size = lax.axis_size("dp")
    if size > GROUP:
        grads = [g.astype(F32) for g in grads]
        groups = [list(range(first, size, GROUP)) for first in range(GROUP)]
        *grads, sums = lax.psum((*grads, sums), "dp", axis_index_groups=groups)
    done = run_results(outputs.reshape(rows, model), *grads, input_grad, sums, width)
    return tuple(v.reshape(-1) if v.shape[0] == 1 else v for v in done)


def solution(mesh):
    rows = P(("dp", "tensor"), None)
    by_col = P(None, "tensor")
    by_row = P("tensor", None)
    split = P("tensor")
    whole = P()
    return jax.shard_map(
        on_device,
        mesh=mesh,
        in_specs=(
            P("dp", None),
            rows,
            P("dp"),
            by_col,
            by_col,
            by_col,
            split,
            split,
            by_row,
            whole,
            whole,
            whole,
            by_col,
            split,
            by_row,
            whole,
            whole,
            whole,
        ),
        out_specs=(
            rows,
            rows,
            by_col,
            by_col,
            by_col,
            split,
            split,
            by_row,
            whole,
            whole,
            whole,
            by_col,
            split,
            by_row,
            whole,
            whole,
            whole,
        ),
        check_vma=False,
    )
```

```python
import functools

import jax
import jax.numpy as jnp
from jax import lax
from jax.experimental import pallas as pl
from jax.experimental.pallas import tpu as pltpu
from jax.sharding import PartitionSpec as P

HD = 64
LEN = 1024
PAIR = 2 * HD
GROUP = 8
F32 = jnp.float32
BF = jnp.bfloat16
NN = (((1,), (0,)), ((), ()))
NT = (((1,), (1,)), ((), ()))
TN = (((0,), (0,)), ((), ()))
MESH = pl.DeviceIdType.MESH
VMEM_LIMIT = 63 << 20


def product(left, right, dims=NN):
    return lax.dot_general(left, right, dims, preferred_element_type=F32)


def flip(index, bit):
    return index + bit * (1 - 2 * lax.rem(lax.div(index, bit), 2))


def mix(index, step):
    low = lax.rem(index + step, 2)
    high = lax.rem(lax.div(index, 2) + lax.div(step, 2), 2)
    return 2 * high + low


class Place:
    def __init__(self):
        self.dp = lax.axis_index("dp")
        self.t = lax.axis_index("tensor")
        self.e = lax.rem(self.dp, GROUP)
        self.core = lax.rem(self.e, 2)
        self.quad = lax.div(self.e, 2)
        self.to_core = (flip(self.dp, 1), self.t)
        self.to_x = (flip(self.dp, 2), self.t)
        self.to_y = (flip(self.dp, 4), self.t)
        self.quad_x = flip(self.quad, 1)
        self.quad_y = flip(self.quad, 2)
        self.quad_xy = flip(self.quad_x, 2)

    def to_z(self, step):
        return (self.dp, mix(self.t, jnp.int32(step)))

    def greet(self):
        barrier = pltpu.get_barrier_semaphore()
        peers = [self.to_core, self.to_x, self.to_y, self.to_z(1), self.to_z(2), self.to_z(3)]
        for peer in peers:
            pl.semaphore_signal(barrier, inc=1, device_id=peer, device_id_type=MESH)
        pl.semaphore_wait(barrier, len(peers))


def remote(src, dst, send, recv, index, device):
    return pltpu.make_async_remote_copy(
        src_ref=src,
        dst_ref=dst,
        send_sem=send.at[index],
        recv_sem=recv.at[index],
        device_id=device,
        device_id_type=MESH,
    )


class Spread:
    def __init__(self, place, full, sems, index, doubled=()):
        self.doubled = doubled
        self.p = place
        self.full = full
        self.sems = sems
        self.index = index

    def block(self, step):
        return mix(self.p.t, jnp.int32(step)) if step else self.p.t

    def slot(self, step):
        return self.index * 4 + step

    def x_copy(self, step, src=None):
        p = self.p
        ref = self.full.at[self.block(step), p.quad, p.core]
        if step in self.doubled:
            half = self.full.shape[3] // 2
            ref = ref.at[pl.ds(0, half)]
        return remote(ref if src is None else src, ref, self.sems[0], self.sems[1], self.slot(step), p.to_x)

    def y_copy(self, step, src=None):
        p = self.p
        ref = self.full.at[self.block(step), p.quad, p.core]
        if step in self.doubled:
            half = self.full.shape[3] // 2
            ref = ref.at[pl.ds(half, half)]
        return remote(ref if src is None else src, ref, self.sems[2], self.sems[3], self.slot(step), p.to_y)

    def half_copies(self, step):
        p = self.p
        half = self.full.shape[3] // 2
        low, high = (half, 0) if step in self.doubled else (0, half)
        first = self.full.at[self.block(step), p.quad_x, p.core, pl.ds(low, half)]
        second = self.full.at[self.block(step), p.quad_y, p.core, pl.ds(high, half)]
        return (
            remote(first, first, self.sems[4], self.sems[5], self.slot(step), p.to_y),
            remote(second, second, self.sems[6], self.sems[7], self.slot(step), p.to_x),
        )

    def core_copy(self, step):
        p = self.p
        ref = self.full.at[self.block(step), :, p.core]
        return remote(ref, ref, self.sems[8], self.sems[9], self.slot(step), p.to_core)

    def first(self, step, src=None):
        self.x_copy(step, src).start()
        self.y_copy(step, src).start()
        if step in self.doubled:
            for copy in self.half_copies(step):
                copy.start()

    def second(self, step):
        self.x_copy(step).wait_recv()
        self.y_copy(step).wait_recv()
        for copy in self.half_copies(step):
            copy.start()

    def third(self, step):
        if step in self.doubled:
            self.x_copy(step).wait_recv()
            self.y_copy(step).wait_recv()
        for copy in self.half_copies(step):
            copy.wait_recv()
        self.core_copy(step).start()

    def arrived(self, step):
        self.core_copy(step).wait_recv()

    def finish(self, step):
        self.x_copy(step).wait_send()
        self.y_copy(step).wait_send()
        for copy in self.half_copies(step):
            copy.wait_send()
        self.core_copy(step).wait_send()

    @staticmethod
    def scratch(count):
        return [pltpu.SemaphoreType.DMA((4 * count,))] * 10


def norm_center(values):
    center = values - jnp.mean(values, axis=-1, keepdims=True)
    inverse = lax.rsqrt(jnp.mean(center * center, axis=-1, keepdims=True) + 1e-05)
    return center * inverse, inverse


def norm_back(grad, normal, inverse, gain):
    scaled = grad * gain
    first_mean = jnp.mean(scaled, axis=-1, keepdims=True)
    second_mean = jnp.mean(scaled * normal, axis=-1, keepdims=True)
    return inverse * (scaled - first_mean - normal * second_mean)


class Reduce:
    def __init__(self, place, bufs, sems):
        self.p = place
        self.g, self.s, self.rc, self.ra, self.rb, self.zs, self.rz, self.own = bufs
        self.sems = sems

    @staticmethod
    def scratch(piece, cols, arrays):
        return [
            pltpu.VMEM((2, 4, 2, piece, cols), BF),
            pltpu.VMEM((3, 4, piece, cols), BF),
            pltpu.VMEM((2, 4, piece, cols), BF),
            pltpu.VMEM((3, 2, piece // 2, cols), BF),
            pltpu.VMEM((3, 2, piece, cols), BF),
            pltpu.VMEM((3, piece, cols), BF),
            pltpu.VMEM((arrays, 3, piece, cols), BF),
            pltpu.VMEM((arrays, piece, cols), BF),
        ]

    @staticmethod
    def semaphores(units):
        return [pltpu.SemaphoreType.DMA((units,))] * 12

    def core_copy(self, u):
        other = 1 - self.p.core
        return remote(
            self.g.at[lax.rem(u, 2), :, other],
            self.rc.at[lax.rem(u, 2)],
            self.sems[0],
            self.sems[1],
            u,
            self.p.to_core,
        )

    def corner_copies(self, u):
        p, slot = self.p, lax.rem(u, 3)
        half = self.ra.shape[2]
        return (
            remote(
                self.s.at[slot, p.quad_xy, pl.ds(0, half)],
                self.ra.at[slot, 0],
                self.sems[2],
                self.sems[3],
                u,
                p.to_y,
            ),
            remote(
                self.s.at[slot, p.quad_xy, pl.ds(half, half)],
                self.ra.at[slot, 1],
                self.sems[4],
                self.sems[5],
                u,
                p.to_x,
            ),
        )

    def side_copies(self, u):
        p, slot = self.p, lax.rem(u, 3)
        return (
            remote(
                self.s.at[slot, p.quad_x], self.rb.at[slot, 0], self.sems[6], self.sems[7], u, p.to_x
            ),
            remote(
                self.s.at[slot, p.quad_y], self.rb.at[slot, 1], self.sems[8], self.sems[9], u, p.to_y
            ),
        )

    def z_copy(self, u, array, step):
        return remote(
            self.zs.at[lax.rem(u, 3)],
            self.rz.at[array, step - 1],
            self.sems[10],
            self.sems[11],
            array * 4 + step,
            (self.p.dp, mix(self.p.t, step)),
        )

    def free_g(self, u):
        if not isinstance(u, int):
            pl.when(u >= 2)(lambda: self.core_copy(u - 2).wait_send())
        elif u >= 2:
            self.core_copy(jnp.int32(u - 2)).wait_send()

    def send(self, u):
        self.core_copy(u).start()

    def fold_core(self, u):
        slot = lax.rem(u, 3)

        def freed():
            for copy in self.side_copies(u - 3) + self.corner_copies(u - 3):
                copy.wait_send()

        pl.when(u >= 3)(freed)
        self.core_copy(u).wait_recv()
        mine = self.g[lax.rem(u, 2), :, self.p.core].astype(F32)
        self.s[slot] = (mine + self.rc[lax.rem(u, 2)].astype(F32)).astype(BF)
        for copy in self.corner_copies(u):
            copy.start()

    def fold_corner(self, u):
        p, slot = self.p, lax.rem(u, 3)
        half = self.ra.shape[2]
        for copy in self.corner_copies(u):
            copy.wait_recv()
        lower = self.s[slot, p.quad_x, :half].astype(F32) + self.ra[slot, 0].astype(F32)
        self.s[slot, p.quad_x, :half] = lower.astype(BF)
        upper = self.s[slot, p.quad_y, half:].astype(F32) + self.ra[slot, 1].astype(F32)
        self.s[slot, p.quad_y, half:] = upper.astype(BF)
        for copy in self.side_copies(u):
            copy.start()

    def fold_sides(self, u, array, step, before):
        p, slot = self.p, lax.rem(u, 3)
        for copy in self.side_copies(u):
            copy.wait_recv()
        total = (
            self.s[slot, p.quad].astype(F32)
            + self.rb[slot, 0].astype(F32)
            + self.rb[slot, 1].astype(F32)
        ).astype(BF)

        if before is not None:
            old_array, old_step, valid = before
            pl.when(valid)(lambda: self.z_copy(u - 3, old_array, old_step).wait_send())

        def store():
            self.own[array] = total

        def pass_on():
            self.zs[slot] = total
            self.z_copy(u, array, step).start()

        pl.when(step == 0)(store)
        pl.when(step != 0)(pass_on)

    def finish(self, array):
        total = self.own[array].astype(F32)
        for step in (1, 2, 3):
            self.z_copy(jnp.int32(0), jnp.int32(array), jnp.int32(step)).wait_recv()
            total = total + self.rz[array, step - 1].astype(F32)
        self.own[array] = total.astype(BF)


def layer_kernel(
    len_ref,
    x_hbm,
    cot_hbm,
    out_bias_ref,
    gain1_ref,
    shift1_ref,
    down_bias_ref,
    gain2_ref,
    shift2_ref,
    query_bias_ref,
    value_bias_ref,
    up_bias_ref,
    wq_hbm,
    wk_hbm,
    wv_hbm,
    wo_hbm,
    wu_hbm,
    wd_hbm,
    qkv_full,
    out_full,
    up_full,
    down_full,
    q_hbm,
    k_hbm,
    v_hbm,
    outputs_hbm,
    down_grad,
    up_grad,
    proj_grad,
    acc,
    sums_ref,
    x_seq,
    bias_s,
    bias_all,
    w_s,
    w_out,
    q_s,
    k_s,
    v_s,
    o_s,
    act_s,
    slope_s,
    wide,
    hidden_s,
    low_s,
    inverse_s,
    lse_s,
    d_att,
    kv_temp,
    rows_recv,
    small,
    small_recv,
    z_send,
    z_recv,
    bias_send,
    bias_recv,
    local,
    load,
    save,
    att_load,
    back_load,
    rows_send_sem,
    rows_recv_sem,
    small_ssem,
    small_rsem,
    *rest,
):
    p = Place()
    reduce = Reduce(p, rest[:8], rest[8:20])
    rows, model = acc.shape
    width = q_s.shape[2]
    half_index = lax.rem(p.t, 2)
    seq = lax.div(p.t, 2)
    own_at = pl.multiple_of(half_index * rows, rows)
    other_at = pl.multiple_of((1 - half_index) * rows, rows)
    own_rows, other_rows = pl.ds(own_at, rows), pl.ds(other_at, rows)
    fulls = [qkv_full, out_full, up_full, down_full]
    QKV, OUT, UP, DOWN = range(4)
    spreads = [
        Spread(p, full, rest[20:30], i, (1,) if i in (UP, DOWN) else ())
        for i, full in enumerate(fulls)
    ]
    qkv_cols = pl.ds(0, 3 * width)

    def on(step, at, *actions):
        @pl.when(step == at)
        def _():
            for action in actions:
                action()

    def begin(copies):
        for copy in copies:
            copy.start()

    def end(copies):
        for copy in copies:
            copy.wait()

    x_load = pltpu.make_async_copy(
        x_hbm.at[pl.ds(pl.multiple_of(seq * LEN, LEN), LEN)], x_seq, local.at[0]
    )
    own_loads = [
        pltpu.make_async_copy(w, w_s.at[2, :, :, :, pl.ds(i * width, width)], local.at[1 + i])
        for i, w in enumerate((wq_hbm, wk_hbm, wv_hbm))
    ]
    out_load = pltpu.make_async_copy(wo_hbm, w_out.at[0], local.at[4])
    up_load = pltpu.make_async_copy(wu_hbm, w_s.at[0], local.at[5])
    down_load = pltpu.make_async_copy(wd_hbm, w_s.at[0], local.at[6])
    cot_load = pltpu.make_async_copy(cot_hbm, low_s, local.at[7])
    qkv_save = pltpu.make_async_copy(w_s.at[2, :, :, :, qkv_cols], qkv_full.at[p.t], local.at[8])
    up_save = pltpu.make_async_copy(w_s.at[0], up_full.at[p.t], local.at[9])
    outputs_s = reduce.g.at[1, 0:2]
    outputs_save = pltpu.make_async_copy(outputs_s, outputs_hbm, local.at[10])
    begin(own_loads)
    x_load.start()
    out_load.start()
    up_load.start()
    cot_load.start()
    bias_s[...] = jnp.zeros(bias_s.shape, F32)
    bias_s[0:1, :width] = query_bias_ref[...]
    bias_s[0:1, width : 2 * width] = value_bias_ref[...]
    bias_s[1:2] = up_bias_ref[...]
    bias_all[p.t] = bias_s[...]
    p.greet()

    def z_copies(array, step):
        slot = array * 4 + step
        if array == QKV:
            return [
                remote(
                    w.at[p.quad, p.core],
                    qkv_full.at[p.t, p.quad, p.core, :, pl.ds(i * width, width)],
                    z_send,
                    z_recv,
                    slot if i == 0 else 16 + 4 * (i - 1) + step,
                    p.to_z(step),
                )
                for i, w in enumerate((wq_hbm, wk_hbm, wv_hbm))
            ]
        w = (None, wo_hbm, wu_hbm, wd_hbm)[array]
        place = fulls[array].at[p.t, p.quad, p.core]
        copies = [remote(w.at[p.quad, p.core], place, z_send, z_recv, slot, p.to_z(step))]
        if step in spreads[array].doubled:
            half = w.shape[2] // 2
            for n, quad in enumerate((p.quad_y, p.quad_x)):
                at = pl.ds(n * half, half)
                src = w.at[quad, p.core, at]
                dst = fulls[array].at[p.t, quad, p.core, at]
                extra = 24 + 2 * (array - UP) + n
                copies.append(remote(src, dst, z_send, z_recv, extra, p.to_z(step)))
        return copies

    def bias_copy(step):
        return remote(bias_s, bias_all.at[p.t], bias_send, bias_recv, step, p.to_z(step))

    for step in (1, 2, 3):
        bias_copy(step).start()
    for array in (QKV, OUT, UP, DOWN):
        for step in (1, 2, 3):
            begin(z_copies(array, step))

    def load_copy(array, step):
        if array == QKV:
            dst = w_s.at[2 + step % 2, :, :, :, qkv_cols]
        elif array == OUT:
            dst = w_out.at[step]
        else:
            dst = w_s.at[step]
        src = fulls[array].at[mix(p.t, jnp.int32(step))]
        return pltpu.make_async_copy(src, dst, load.at[array * 4 + step])

    def relay(plan):
        for array, legs in plan:
            spread = spreads[array]
            for leg in legs.split():
                kind, step = leg[0], int(leg[1])
                if kind == "f":
                    for copy in z_copies(array, step):
                        copy.wait_recv()
                    spread.first(step)
                elif kind == "s":
                    spread.second(step)
                elif kind == "t":
                    spread.third(step)
                else:
                    spread.arrived(step)
                    load_copy(array, step).start()

    def passed(step, place):
        plans = {
            (0, "end"): [
                (QKV, "f1 f2 s1 f3 s2"),
                (OUT, "f1"),
                (QKV, "t1"),
                (OUT, "f2 f3"),
                (QKV, "a1 s3"),
            ],
            (1, "mid"): [(QKV, "t2"), (OUT, "s1")],
            (1, "end"): [(OUT, "s2 s3"), (UP, "f1"), (QKV, "a2")],
            (2, "start"): [(QKV, "t3"), (OUT, "t1 t2")],
            (2, "mid"): [(OUT, "t3")],
            (2, "end"): [(QKV, "a3"), (OUT, "a1 a2 a3"), (UP, "f2")],
            (3, "start"): [(UP, "t1 f3")],
            (3, "end"): [(UP, "s2")],
        }
        for (at, where), plan in plans.items():
            if where == place:
                on(step, at, lambda plan=plan: relay(plan))

    def attend_saves(step):
        group, slot = mix(p.t, step), lax.rem(step, 2)
        pairs = ((q_s, q_hbm), (k_s, k_hbm), (v_s, v_hbm))
        return [
            pltpu.make_async_copy(vmem.at[slot], hbm.at[group], save.at[3 * step + i])
            for i, (vmem, hbm) in enumerate(pairs)
        ]

    def attend(step):
        group, slot = mix(p.t, step), lax.rem(step, 2)
        weights = w_s[2 + slot, :, :, :, qkv_cols].reshape(model, 3 * width)
        bias = bias_all[group, 0:1]
        queries = (product(x_seq[own_rows, :], weights[:, :width]) + bias[:, :width]).astype(BF)
        q_s[slot] = (queries.astype(F32) * HD ** (-0.5)).astype(BF)
        k_s[slot] = product(x_seq[...], weights[:, width : 2 * width]).astype(BF)
        v_s[slot] = (
            product(x_seq[...], weights[:, 2 * width :]) + bias[:, width : 2 * width]
        ).astype(BF)
        passed(step, "start")
        length = len_ref[seq]
        key_slot = lax.broadcasted_iota(jnp.int32, (LEN, rows), 0)
        lane = lax.broadcasted_iota(jnp.int32, (rows, PAIR), 1)
        for pair in range(width // PAIR):
            if pair == 1:
                passed(step, "mid")
            cols = slice(pair * PAIR, (pair + 1) * PAIR)
            keys, values, q_pair = k_s[slot, :, cols], v_s[slot, :, cols], q_s[slot, :, cols]
            parts = []
            for head in range(2):
                mine = jnp.where((lane >= HD) == (head == 1), q_pair, jnp.zeros_like(q_pair))
                scores = jnp.where(key_slot < length, product(keys, mine, NT), -1e30)
                top = jnp.max(scores, axis=0, keepdims=True)
                exponent = jnp.exp(scores - top)
                total = jnp.sum(exponent, axis=0, keepdims=True)
                mixed = product(values, exponent.astype(BF), TN)
                parts.append(mixed[head * HD : (head + 1) * HD] * (1.0 / total))
                lse_s[group, pl.ds(pair * 2 + head, 1), :] = top + jnp.log(total)
            o_s[step, :, cols] = jnp.concatenate(parts, axis=0).T.astype(BF)

    x_load.wait()
    end(own_loads)
    qkv_save.start()
    for step in (1, 2, 3):
        bias_copy(step).wait_recv()

    def attend_step(step, carry):
        for i in (1, 2, 3):
            on(step, i, load_copy(QKV, i).wait)
        pl.when(step >= 2)(lambda: end(attend_saves(step - 2)))
        attend(step)
        begin(attend_saves(step))
        on(step, 1, qkv_save.wait)
        passed(step, "end")
        return carry

    lax.fori_loop(0, 4, attend_step, 0)

    out_load.wait()
    for step in (1, 2, 3):
        load_copy(OUT, step).wait()
    acc[...] = x_seq[own_rows, :].astype(F32) + out_bias_ref[...]
    for step in range(4):
        acc[...] += product(o_s[step], w_out[step].reshape(width, model))
    normal1, inverse1 = norm_center(acc[...])
    wide[...] = normal1
    inverse_s[...] = jnp.broadcast_to(inverse1, inverse_s.shape)
    normed1 = normal1 * gain1_ref[...] + shift1_ref[...]
    hidden_s[...] = normed1.astype(BF)
    acc[...] = normed1 + down_bias_ref[...]
    relay([(UP, "a1")])

    def up_step(step, carry):
        on(step, 0, up_load.wait, up_save.start)
        for i in (1, 2, 3):
            on(step, i, load_copy(UP, i).wait)
        upper = product(hidden_s[...], w_s[step].reshape(model, model))
        upper = upper + bias_all[mix(p.t, step), 1:2]
        cdf = 0.5 * (1.0 + lax.erf(upper * 0.7071067811865476))
        act_s[step] = (upper * cdf).astype(BF)
        density = jnp.exp(-0.5 * upper * upper) * 0.3989422804014327
        slope_s[step] = (cdf + upper * density).astype(BF)
        on(step, 0, lambda: relay([(UP, "s3"), (DOWN, "f1")]))
        on(step, 1, up_save.wait, down_load.start)
        on(step, 1, lambda: relay([(UP, "t2"), (DOWN, "f2"), (UP, "t3"), (DOWN, "f3"), (UP, "a2")]))
        on(step, 2, lambda: relay([(UP, "a3"), (DOWN, "t1")]))
        on(step, 3, lambda: relay([(DOWN, "s2 a1")]))
        return carry

    lax.fori_loop(0, 4, up_step, 0)
    for step in (2, 3):
        end(attend_saves(jnp.int32(step)))

    def down_step(step, carry):
        on(step, 0, down_load.wait)
        for i in (1, 2, 3):
            on(step, i, load_copy(DOWN, i).wait)
        acc[...] += product(act_s[step], w_s[step].reshape(model, model))
        on(step, 0, lambda: relay([(DOWN, "s3 t2")]))
        on(step, 1, lambda: relay([(DOWN, "t3 a2")]))
        on(step, 2, lambda: relay([(DOWN, "a3")]))
        return carry

    lax.fori_loop(0, 4, down_step, 0)

    cot_load.wait()
    normal2, inverse2 = norm_center(acc[...])
    outputs = (normal2 * gain2_ref[...] + shift2_ref[...]).astype(BF)
    reduce.g[1, 0:2] = outputs.reshape(2, 2, rows // 4, model)
    outputs_save.start()
    slot_index = half_index * rows + lax.broadcasted_iota(jnp.int32, (rows, 1), 0)
    grad_out = jnp.where(slot_index < len_ref[seq], low_s[...].astype(F32), 0.0)
    d_second = norm_back(grad_out, normal2, inverse2, gain2_ref[...])
    acc[...] = d_second
    low_s[...] = d_second.astype(BF)
    small[0] = jnp.zeros(small.shape[1:], F32)
    small[0, 0:1] = jnp.sum(grad_out * normal2, axis=0, keepdims=True)
    small[0, 1:2] = jnp.sum(grad_out, axis=0, keepdims=True)
    small[0, 2:3] = jnp.sum(d_second, axis=0, keepdims=True)

    grads = (down_grad, up_grad, proj_grad)
    back_spreads = [Spread(p, grad, rest[30:40], i) for i, grad in enumerate(grads)]
    for spread in back_spreads:
        spread.block = lambda step: 0
    B_DOWN, B_UP, B_PROJ = range(3)

    def group_at(i):
        return mix(p.t, 3 - i)

    def att_loads(i):
        g, slot = group_at(i), lax.rem(i, 2)
        pairs = ((q_hbm, q_s), (k_hbm, k_s), (v_hbm, v_s))
        return [
            pltpu.make_async_copy(hbm.at[g], vmem.at[slot], att_load.at[4 * i + n])
            for n, (hbm, vmem) in enumerate(pairs)
        ]

    def proj_load(i):
        slot = lax.rem(i, 2)
        return pltpu.make_async_copy(
            qkv_full.at[group_at(i)], w_s.at[slot, :, :, :, qkv_cols], att_load.at[4 * i + 3]
        )

    def up_again(step):
        return pltpu.make_async_copy(up_full.at[mix(p.t, step)], w_s.at[step], back_load.at[step])

    begin(att_loads(jnp.int32(0)))

    def mlp_order(i):
        return 3 - 2 * lax.rem(i, 2) - lax.div(i, 2)

    def unit_of(u):
        if isinstance(u, int) and u >= 8:
            return jnp.int32(B_PROJ), jnp.int32(11 - u)
        u = jnp.int32(u)
        return lax.rem(u, 2), mlp_order(lax.div(u, 2))

    def fold_core(u):
        reduce.fold_core(jnp.int32(u))

    def fold_corner(u):
        reduce.fold_corner(jnp.int32(u))

    def fold_sides(u):
        array, step = unit_of(u)
        if isinstance(u, int):
            old_array, old_step = unit_of(max(u - 3, 0))
            valid = jnp.logical_and(u >= 3, old_step != 0)
            u = jnp.int32(u)
        else:
            old_array, old_step = unit_of(jnp.maximum(u - 3, 0))
            valid = jnp.logical_and(u >= 3, old_step != 0)
        reduce.fold_sides(u, array, step, (old_array, old_step, valid))

    def tick(u):
        pl.when(u >= 4)(lambda: fold_sides(u - 4))
        pl.when(u >= 1)(lambda: fold_core(u - 1))
        reduce.send(u)
        pl.when(u >= 2)(lambda: fold_corner(u - 2))

    def store_unit(slot, left, right):
        part = model // 4
        for quad in range(4):
            terms = product(left(slice(quad * part, (quad + 1) * part)), right, TN)
            reduce.g[slot, quad] = terms.astype(BF).reshape(2, part // 2, right.shape[1])

    def mlp_step(i, carry):
        step = mlp_order(i)
        u = 2 * i
        reduce.free_g(u)
        store_unit(0, lambda cols: act_s[step, :, cols], low_s[...])
        tick(u)
        d_act = product(low_s[...], w_s[step].reshape(model, model), NT)
        d_up = (d_act * slope_s[step].astype(F32)).astype(BF)
        slope_s[step] = d_up
        up_again(step).start()
        at = pl.ds(6 + mix(p.t, step), 1)
        small[0, at, :] = jnp.sum(d_up.astype(F32), axis=0, keepdims=True)
        reduce.free_g(u + 1)
        on(i, 0, outputs_save.wait)
        store_unit(1, lambda cols: hidden_s[:, cols], slope_s[step])
        tick(u + 1)
        up_again(step).wait()
        acc[...] += product(slope_s[step], w_s[step].reshape(model, model), NT)
        return carry

    lax.fori_loop(0, 4, mlp_step, 0)

    proj_load(jnp.int32(0)).start()
    normal1 = wide[...]
    small[0, 3:4] = jnp.sum(acc[...] * normal1, axis=0, keepdims=True)
    small[0, 4:5] = jnp.sum(acc[...], axis=0, keepdims=True)
    d_first = norm_back(acc[...], normal1, inverse_s[:, 0:1], gain1_ref[...])
    acc[...] = d_first
    low_s[...] = d_first.astype(BF)
    small[0, 5:6] = jnp.sum(d_first, axis=0, keepdims=True)
    d_own, d_other = act_s.at[0], act_s.at[1]

    def attend_back(i):
        slot = lax.rem(i, 2)
        g = group_at(i)
        step = mix(p.t, g)
        length = len_ref[seq]
        d_att[...] = product(low_s[...], w_out[step].reshape(width, model), NT).astype(BF)
        key_slot = lax.broadcasted_iota(jnp.int32, (LEN, rows), 0)
        lane = lax.broadcasted_iota(jnp.int32, (rows, PAIR), 1)
        for pair in range(width // PAIR):
            cols = slice(pair * PAIR, (pair + 1) * PAIR)
            keys, values, queries = k_s[slot, :, cols], v_s[slot, :, cols], q_s[slot, :, cols]
            d_out = d_att[:, cols]
            inner_all = (d_out.astype(F32) * o_s[step, :, cols].astype(F32)).T
            query_parts = []
            for head in range(2):
                mine = (lane >= HD) == (head == 1)
                own_q = jnp.where(mine, queries, jnp.zeros_like(queries))
                own_d = jnp.where(mine, d_out, jnp.zeros_like(d_out))
                inner = jnp.sum(inner_all[head * HD : (head + 1) * HD], axis=0, keepdims=True)
                scores = jnp.where(key_slot < length, product(keys, own_q, NT), -1e30)
                probs = jnp.exp(scores - lse_s[g, pl.ds(pair * 2 + head, 1), :])
                d_probs = product(values, own_d, NT)
                d_scores = (probs * (d_probs - inner) * HD ** (-0.5)).astype(BF)
                d_values = product(probs.astype(BF), own_d)
                d_keys = product(d_scores, own_q) * HD**0.5
                if head == 0:
                    kv_temp[0] = d_keys
                    kv_temp[1] = d_values
                else:
                    kv_temp[0] += d_keys
                    kv_temp[1] += d_values
                query_parts.append(product(keys, d_scores, TN)[head * HD : (head + 1) * HD])
            d_own[:, cols] = jnp.concatenate(query_parts, axis=0).T.astype(BF)
            for n in range(2):
                at = slice((n + 1) * width + pair * PAIR, (n + 1) * width + (pair + 1) * PAIR)
                d_own[:, at] = kv_temp[n, own_rows, :].astype(BF)
                d_other[:, at] = kv_temp[n, other_rows, :].astype(BF)

    def proj_unit(i, u):
        slot = lax.rem(i, 2)
        g = group_at(i)
        qkv, kv = slice(0, 3 * width), slice(width, 3 * width)
        at = pl.ds(10 + g, 1)
        small[0, at, qkv] = jnp.sum(d_own[:, qkv].astype(F32), axis=0, keepdims=True)
        small[0, at, kv] += jnp.sum(d_other[:, kv].astype(F32), axis=0, keepdims=True)
        reduce.core_copy(u - 2).wait_send()
        g_slot = lax.rem(u, 2)
        out_terms = product(o_s[mix(p.t, g)], low_s[...], TN).astype(BF)
        for quad in range(4):
            cols = slice(quad * width, (quad + 1) * width)
            block = (2, width // 2, width)
            x_own, x_other = x_seq[own_rows, cols], x_seq[other_rows, cols]
            queries = product(x_own, d_own[:, :width], TN)
            reduce.g[g_slot, quad, :, :, :width] = queries.astype(BF).reshape(block)
            both = product(x_own, d_own[:, kv], TN) + product(x_other, d_other[:, kv], TN)
            reduce.g[g_slot, quad, :, :, kv] = both.astype(BF).reshape(2, width // 2, 2 * width)
            reduce.g[g_slot, quad, :, :, 3 * width :] = out_terms[:, cols].reshape(block)
        reduce.send(u)
        proj_load(i).wait()
        weights = w_s[slot, :, :, :, qkv_cols].reshape(model, 3 * width)
        acc[...] += product(d_own[:, qkv], weights, NT)
        other = product(d_other[:, kv], weights[:, kv], NT)

        @pl.when(i == 0)
        def _():
            wide[...] = other

        @pl.when(i > 0)
        def _():
            wide[...] += other

    def own_save(array):
        place = grads[array].at[0, p.quad, p.core]
        return pltpu.make_async_copy(reduce.own.at[array], place, local.at[11 + array])

    def start_spread(array):
        reduce.finish(array)
        own_save(array).start()
        back_spreads[array].first(0, reduce.own.at[array])

    def end_spread(array):
        own_save(array).wait()
        back_spreads[array].third(0)

    def att_step(i, carry):
        end(att_loads(i))
        attend_back(i)

        def next_loads():
            begin(att_loads(i + 1))
            proj_load(i + 1).start()

        pl.when(i < 3)(next_loads)

        def passed_back(at):
            fold_sides(4 + at)
            fold_core(7 + at)
            fold_corner(6 + at)
            if at == 2:
                start_spread(B_DOWN)
            if at == 3:
                back_spreads[B_DOWN].second(0)
                start_spread(B_UP)

        for at in range(4):
            on(i, at, lambda at=at: passed_back(at))
        proj_unit(i, i + 8)
        return carry

    lax.fori_loop(0, 4, att_step, 0)
    rows_out = act_s.at[2]
    rows_out[...] = wide[...].astype(BF)

    def rows_copy(part):
        at = pl.ds(part * (rows // 4), rows // 4)
        return remote(
            rows_out.at[at], rows_recv.at[at], rows_send_sem, rows_recv_sem, part, p.to_z(1)
        )

    rows_copy(0).start()
    rows_copy(1).start()
    peers = [p.to_core, p.to_x, p.to_y, p.to_z(1), p.to_z(2)]

    def small_copy(n):
        return remote(small.at[n], small_recv.at[n], small_ssem, small_rsem, n, peers[n])

    def small_next(n):
        small_copy(n).wait_recv()
        small[n + 1] = small[n] + small_recv[n]
        if n < 4:
            small_copy(n + 1).start()

    small_copy(0).start()
    fold_sides(8)
    fold_core(11)
    fold_corner(10)
    end_spread(B_DOWN)
    back_spreads[B_UP].second(0)
    small_next(0)
    fold_sides(9)
    rows_copy(2).start()
    fold_corner(11)
    end_spread(B_UP)
    small_next(1)
    fold_sides(10)
    rows_copy(3).start()
    small_next(2)
    fold_sides(11)
    start_spread(B_PROJ)
    small_next(3)
    back_spreads[B_PROJ].second(0)
    small_next(4)
    end_spread(B_PROJ)
    sums_ref[...] = small[5]

    for step in (1, 2, 3):
        bias_copy(step).wait_send()
        for array in range(4):
            for copy in z_copies(array, step):
                copy.wait_send()
            spreads[array].finish(step)
    for part in range(4):
        rows_copy(part).wait()
    acc[...] += rows_recv[...].astype(F32)
    for u in (10, 11):
        reduce.core_copy(jnp.int32(u)).wait_send()
    for u in (9, 10, 11):
        for copy in reduce.side_copies(jnp.int32(u)) + reduce.corner_copies(jnp.int32(u)):
            copy.wait_send()
    for u in (9, 10):
        array, step = unit_of(u)
        reduce.z_copy(jnp.int32(u), array, step).wait_send()
    for n in range(5):
        small_copy(n).wait_send()
    for spread in back_spreads:
        spread.arrived(0)
        spread.finish(0)


def run_layer(lengths, x, cot, vectors, wq, wk, wv, wo, wu, wd):
    T = lax.axis_size("tensor")
    model = x.shape[1]
    rows = x.shape[0] // T
    width = wo.shape[0]
    piece = model // GROUP

    def pieces(w):
        return w.reshape(4, 2, w.shape[0] // GROUP, w.shape[1])

    def out(*shape, dtype=BF):
        return jax.ShapeDtypeStruct(shape, dtype)

    anyw = pl.BlockSpec(memory_space=pl.ANY)
    vmem = pl.BlockSpec(memory_space=pltpu.VMEM)
    smem = pl.BlockSpec(memory_space=pltpu.SMEM)
    dma = pltpu.SemaphoreType.DMA
    outs = [
        out(T, 4, 2, piece, 3 * width),
        out(T, 4, 2, width // GROUP, model),
        out(T, 4, 2, piece, model),
        out(T, 4, 2, piece, model),
        out(T, rows, width),
        out(T, LEN, width),
        out(T, LEN, width),
        out(2, 2, rows // 4, model),
        *[out(1, 4, 2, piece, model)] * 3,
        out(rows, model, dtype=F32),
        out(16, model, dtype=F32),
    ]
    return pl.pallas_call(
        layer_kernel,
        in_specs=[smem, anyw, anyw] + [vmem] * 9 + [anyw] * 6,
        out_specs=[anyw] * 11 + [vmem] * 2,
        out_shape=outs,
        scratch_shapes=[
            pltpu.VMEM((LEN, model), BF),
            pltpu.VMEM((8, model), F32),
            pltpu.VMEM((T, 8, model), F32),
            pltpu.VMEM((4, 4, 2, piece, model), BF),
            pltpu.VMEM((T, 4, 2, width // GROUP, model), BF),
            pltpu.VMEM((2, rows, width), BF),
            pltpu.VMEM((2, LEN, width), BF),
            pltpu.VMEM((2, LEN, width), BF),
            pltpu.VMEM((T, rows, width), BF),
            pltpu.VMEM((T, rows, model), BF),
            pltpu.VMEM((T, rows, model), BF),
            pltpu.VMEM((rows, model), F32),
            pltpu.VMEM((rows, model), BF),
            pltpu.VMEM((rows, model), BF),
            pltpu.VMEM((rows, 128), F32),
            pltpu.VMEM((T, 8, rows), F32),
            pltpu.VMEM((rows, width), BF),
            pltpu.VMEM((2, LEN, PAIR), F32),
            pltpu.VMEM((rows, model), BF),
            pltpu.VMEM((6, 16, model), F32),
            pltpu.VMEM((5, 16, model), F32),
            dma((28,)),
            dma((28,)),
            dma((4,)),
            dma((4,)),
            dma((14,)),
            dma((16,)),
            dma((12,)),
            dma((16,)),
            dma((4,)),
            dma((4,)),
            dma((4,)),
            dma((5,)),
            dma((5,)),
            *Reduce.scratch(piece, model, 3),
            *Reduce.semaphores(12),
            *Spread.scratch(4),
            *Spread.scratch(3),
        ],
        compiler_params=pltpu.CompilerParams(
            collective_id=0, has_side_effects=True, vmem_limit_bytes=VMEM_LIMIT
        ),
        cost_estimate=pl.CostEstimate(
            flops=100 * 10**9, bytes_accessed=120 << 20, transcendentals=24 << 20
        ),
        name="layer",
    )(
        lengths,
        x,
        cot,
        *[v.reshape(1, -1) for v in vectors],
        pieces(wq),
        pieces(wk),
        pieces(wv),
        pieces(wo),
        pieces(wu),
        pieces(wd),
    )


def results_kernel(
    outputs_in,
    down_in,
    up_in,
    proj_in,
    input_in,
    sums_in,
    outputs_ref,
    input_ref,
    query_ref,
    key_ref,
    value_ref,
    query_bias_ref,
    value_bias_ref,
    out_ref,
    out_bias_ref,
    gain1_ref,
    shift1_ref,
    up_ref,
    up_bias_ref,
    down_ref,
    down_bias_ref,
    gain2_ref,
    shift2_ref,
):
    t = lax.axis_index("tensor")
    width = query_ref.shape[1]
    outputs_ref[...] = outputs_in[...]
    input_ref[...] = input_in[...]
    down_ref[...] = down_in[...].astype(F32)
    up_ref[...] = up_in[...].astype(F32)
    for n, ref in enumerate((query_ref, key_ref, value_ref, out_ref)):
        ref[...] = proj_in[:, n * width : (n + 1) * width].astype(F32)
    rows = (gain2_ref, shift2_ref, down_bias_ref, gain1_ref, shift1_ref, out_bias_ref)
    for n, ref in enumerate(rows):
        ref[...] = sums_in[n : n + 1]
    up_bias_ref[...] = sums_in[pl.ds(6 + t, 1), :]
    proj = sums_in[pl.ds(10 + t, 1), :]
    query_bias_ref[...] = proj[:, :width]
    value_bias_ref[...] = proj[:, 2 * width : 3 * width]


def run_results(outputs, down, up, proj, input_grad, sums, width):
    rows, model = outputs.shape
    steps = 4
    tall = lambda count, cols=model: pl.BlockSpec((count // steps, cols), lambda i: (i, 0))
    row = lambda cols=model: pl.BlockSpec((1, cols), lambda i: (0, 0))
    out = lambda count, cols=model, dtype=F32: jax.ShapeDtypeStruct((count, cols), dtype)
    whole = pl.BlockSpec(sums.shape, lambda i: (0, 0))
    outs = [
        (out(rows, dtype=BF), tall(rows)),
        (out(rows), tall(rows)),
        *[(out(model, width), tall(model, width))] * 3,
        *[(out(1, width), row(width))] * 2,
        (out(width), pl.BlockSpec((width, model // steps), lambda i: (0, i))),
        *[(out(1), row())] * 3,
        (out(model), tall(model)),
        (out(1), row()),
        (out(model), tall(model)),
        *[(out(1), row())] * 3,
    ]
    return pl.pallas_call(
        results_kernel,
        grid=(steps,),
        in_specs=[tall(rows), tall(model), tall(model), tall(model), tall(rows), whole],
        out_specs=[spec for _, spec in outs],
        out_shape=[shape for shape, _ in outs],
        compiler_params=pltpu.CompilerParams(vmem_limit_bytes=VMEM_LIMIT),
        name="results",
    )(outputs, down, up, proj, input_grad, sums)


def on_device(
    inputs,
    cotangent,
    lengths,
    query_weight,
    key_weight,
    value_weight,
    query_bias,
    value_bias,
    out_weight,
    out_bias,
    norm1_gain,
    norm1_bias,
    up_weight,
    up_bias,
    down_weight,
    down_bias,
    norm2_gain,
    norm2_bias,
):
    model = inputs.shape[1]
    rows = cotangent.shape[0]
    width = out_weight.shape[0]
    results = run_layer(
        lengths,
        inputs,
        cotangent,
        (
            out_bias,
            norm1_gain,
            norm1_bias,
            down_bias,
            norm2_gain,
            norm2_bias,
            query_bias,
            value_bias,
            up_bias,
        ),
        query_weight,
        key_weight,
        value_weight,
        out_weight,
        up_weight,
        down_weight,
    )
    outputs, down_grad, up_grad, proj_grad, input_grad, sums = results[7:]
    grads = [g.reshape(model, model) for g in (down_grad, up_grad, proj_grad)]
    size = lax.axis_size("dp")
    if size > GROUP:
        grads = [g.astype(F32) for g in grads]
        groups = [list(range(first, size, GROUP)) for first in range(GROUP)]
        *grads, sums = lax.psum((*grads, sums), "dp", axis_index_groups=groups)
    done = run_results(outputs.reshape(rows, model), *grads, input_grad, sums, width)
    return tuple(v.reshape(-1) if v.shape[0] == 1 else v for v in done)


def solution(mesh):
    rows = P(("dp", "tensor"), None)
    by_col = P(None, "tensor")
    by_row = P("tensor", None)
    split = P("tensor")
    whole = P()
    return jax.shard_map(
        on_device,
        mesh=mesh,
        in_specs=(
            P("dp", None),
            rows,
            P("dp"),
            by_col,
            by_col,
            by_col,
            split,
            split,
            by_row,
            whole,
            whole,
            whole,
            by_col,
            split,
            by_row,
            whole,
            whole,
            whole,
        ),
        out_specs=(
            rows,
            rows,
            by_col,
            by_col,
            by_col,
            split,
            split,
            by_row,
            whole,
            whole,
            whole,
            by_col,
            split,
            by_row,
            whole,
            whole,
            whole,
        ),
        check_vma=False,
    )
```

```python
import functools

import jax
import jax.numpy as jnp
from jax import lax
from jax.experimental import pallas as pl
from jax.experimental.pallas import tpu as pltpu
from jax.sharding import PartitionSpec as P

HD = 64
LEN = 1024
PAIR = 2 * HD
GROUP = 8
F32 = jnp.float32
BF = jnp.bfloat16
NN = (((1,), (0,)), ((), ()))
NT = (((1,), (1,)), ((), ()))
TN = (((0,), (0,)), ((), ()))
MESH = pl.DeviceIdType.MESH
VMEM_LIMIT = 63 << 20


def product(left, right, dims=NN):
    return lax.dot_general(left, right, dims, preferred_element_type=F32)


def flip(index, bit):
    return index + bit * (1 - 2 * lax.rem(lax.div(index, bit), 2))


def mix(index, step):
    low = lax.rem(index + step, 2)
    high = lax.rem(lax.div(index, 2) + lax.div(step, 2), 2)
    return 2 * high + low


class Place:
    def __init__(self):
        self.dp = lax.axis_index("dp")
        self.t = lax.axis_index("tensor")
        self.e = lax.rem(self.dp, GROUP)
        self.core = lax.rem(self.e, 2)
        self.quad = lax.div(self.e, 2)
        self.to_core = (flip(self.dp, 1), self.t)
        self.to_x = (flip(self.dp, 2), self.t)
        self.to_y = (flip(self.dp, 4), self.t)
        self.quad_x = flip(self.quad, 1)
        self.quad_y = flip(self.quad, 2)
        self.quad_xy = flip(self.quad_x, 2)

    def to_z(self, step):
        return (self.dp, mix(self.t, jnp.int32(step)))

    def greet(self):
        barrier = pltpu.get_barrier_semaphore()
        peers = [self.to_core, self.to_x, self.to_y, self.to_z(1), self.to_z(2), self.to_z(3)]
        for peer in peers:
            pl.semaphore_signal(barrier, inc=1, device_id=peer, device_id_type=MESH)
        pl.semaphore_wait(barrier, len(peers))


def remote(src, dst, send, recv, index, device):
    return pltpu.make_async_remote_copy(
        src_ref=src,
        dst_ref=dst,
        send_sem=send.at[index],
        recv_sem=recv.at[index],
        device_id=device,
        device_id_type=MESH,
    )


class Spread:
    def __init__(self, place, full, sems, index, doubled=()):
        self.doubled = doubled
        self.p = place
        self.full = full
        self.sems = sems
        self.index = index

    def block(self, step):
        return mix(self.p.t, jnp.int32(step)) if step else self.p.t

    def slot(self, step):
        return self.index * 4 + step

    def x_copy(self, step, src=None):
        p = self.p
        ref = self.full.at[self.block(step), p.quad, p.core]
        if step in self.doubled:
            half = self.full.shape[3] // 2
            ref = ref.at[pl.ds(0, half)]
        return remote(ref if src is None else src, ref, self.sems[0], self.sems[1], self.slot(step), p.to_x)

    def y_copy(self, step, src=None):
        p = self.p
        ref = self.full.at[self.block(step), p.quad, p.core]
        if step in self.doubled:
            half = self.full.shape[3] // 2
            ref = ref.at[pl.ds(half, half)]
        return remote(ref if src is None else src, ref, self.sems[2], self.sems[3], self.slot(step), p.to_y)

    def half_copies(self, step):
        p = self.p
        half = self.full.shape[3] // 2
        low, high = (half, 0) if step in self.doubled else (0, half)
        first = self.full.at[self.block(step), p.quad_x, p.core, pl.ds(low, half)]
        second = self.full.at[self.block(step), p.quad_y, p.core, pl.ds(high, half)]
        return (
            remote(first, first, self.sems[4], self.sems[5], self.slot(step), p.to_y),
            remote(second, second, self.sems[6], self.sems[7], self.slot(step), p.to_x),
        )

    def core_copy(self, step):
        p = self.p
        ref = self.full.at[self.block(step), :, p.core]
        return remote(ref, ref, self.sems[8], self.sems[9], self.slot(step), p.to_core)

    def first(self, step, src=None):
        self.x_copy(step, src).start()
        self.y_copy(step, src).start()
        if step in self.doubled:
            for copy in self.half_copies(step):
                copy.start()

    def second(self, step):
        self.x_copy(step).wait_recv()
        self.y_copy(step).wait_recv()
        for copy in self.half_copies(step):
            copy.start()

    def third(self, step):
        if step in self.doubled:
            self.x_copy(step).wait_recv()
            self.y_copy(step).wait_recv()
        for copy in self.half_copies(step):
            copy.wait_recv()
        self.core_copy(step).start()

    def arrived(self, step):
        self.core_copy(step).wait_recv()

    def finish(self, step):
        self.x_copy(step).wait_send()
        self.y_copy(step).wait_send()
        for copy in self.half_copies(step):
            copy.wait_send()
        self.core_copy(step).wait_send()

    @staticmethod
    def scratch(count):
        return [pltpu.SemaphoreType.DMA((4 * count,))] * 10


def norm_center(values):
    center = values - jnp.mean(values, axis=-1, keepdims=True)
    inverse = lax.rsqrt(jnp.mean(center * center, axis=-1, keepdims=True) + 1e-05)
    return center * inverse, inverse


def norm_back(grad, normal, inverse, gain):
    scaled = grad * gain
    first_mean = jnp.mean(scaled, axis=-1, keepdims=True)
    second_mean = jnp.mean(scaled * normal, axis=-1, keepdims=True)
    return inverse * (scaled - first_mean - normal * second_mean)


class Reduce:
    def __init__(self, place, bufs, sems):
        self.p = place
        self.g, self.s, self.rc, self.ra, self.rb, self.zs, self.rz, self.own = bufs
        self.sems = sems

    @staticmethod
    def scratch(piece, cols, arrays):
        return [
            pltpu.VMEM((2, 4, 2, piece, cols), BF),
            pltpu.VMEM((3, 4, piece, cols), BF),
            pltpu.VMEM((2, 4, piece, cols), BF),
            pltpu.VMEM((3, 2, piece // 2, cols), BF),
            pltpu.VMEM((3, 2, piece, cols), BF),
            pltpu.VMEM((3, piece, cols), BF),
            pltpu.VMEM((arrays, 3, piece, cols), BF),
            pltpu.VMEM((arrays, piece, cols), BF),
        ]

    @staticmethod
    def semaphores(units):
        return [pltpu.SemaphoreType.DMA((units,))] * 12

    def core_copy(self, u):
        other = 1 - self.p.core
        return remote(
            self.g.at[lax.rem(u, 2), :, other],
            self.rc.at[lax.rem(u, 2)],
            self.sems[0],
            self.sems[1],
            u,
            self.p.to_core,
        )

    def corner_copies(self, u):
        p, slot = self.p, lax.rem(u, 3)
        half = self.ra.shape[2]
        return (
            remote(
                self.s.at[slot, p.quad_xy, pl.ds(0, half)],
                self.ra.at[slot, 0],
                self.sems[2],
                self.sems[3],
                u,
                p.to_y,
            ),
            remote(
                self.s.at[slot, p.quad_xy, pl.ds(half, half)],
                self.ra.at[slot, 1],
                self.sems[4],
                self.sems[5],
                u,
                p.to_x,
            ),
        )

    def side_copies(self, u):
        p, slot = self.p, lax.rem(u, 3)
        return (
            remote(
                self.s.at[slot, p.quad_x], self.rb.at[slot, 0], self.sems[6], self.sems[7], u, p.to_x
            ),
            remote(
                self.s.at[slot, p.quad_y], self.rb.at[slot, 1], self.sems[8], self.sems[9], u, p.to_y
            ),
        )

    def z_copy(self, u, array, step):
        return remote(
            self.zs.at[lax.rem(u, 3)],
            self.rz.at[array, step - 1],
            self.sems[10],
            self.sems[11],
            array * 4 + step,
            (self.p.dp, mix(self.p.t, step)),
        )

    def free_g(self, u):
        if not isinstance(u, int):
            pl.when(u >= 2)(lambda: self.core_copy(u - 2).wait_send())
        elif u >= 2:
            self.core_copy(jnp.int32(u - 2)).wait_send()

    def send(self, u):
        self.core_copy(u).start()

    def fold_core(self, u):
        slot = lax.rem(u, 3)

        def freed():
            for copy in self.side_copies(u - 3) + self.corner_copies(u - 3):
                copy.wait_send()

        pl.when(u >= 3)(freed)
        self.core_copy(u).wait_recv()
        mine = self.g[lax.rem(u, 2), :, self.p.core].astype(F32)
        self.s[slot] = (mine + self.rc[lax.rem(u, 2)].astype(F32)).astype(BF)
        for copy in self.corner_copies(u):
            copy.start()

    def fold_corner(self, u):
        p, slot = self.p, lax.rem(u, 3)
        half = self.ra.shape[2]
        for copy in self.corner_copies(u):
            copy.wait_recv()
        lower = self.s[slot, p.quad_x, :half].astype(F32) + self.ra[slot, 0].astype(F32)
        self.s[slot, p.quad_x, :half] = lower.astype(BF)
        upper = self.s[slot, p.quad_y, half:].astype(F32) + self.ra[slot, 1].astype(F32)
        self.s[slot, p.quad_y, half:] = upper.astype(BF)
        for copy in self.side_copies(u):
            copy.start()

    def fold_sides(self, u, array, step, before):
        p, slot = self.p, lax.rem(u, 3)
        for copy in self.side_copies(u):
            copy.wait_recv()
        total = (
            self.s[slot, p.quad].astype(F32)
            + self.rb[slot, 0].astype(F32)
            + self.rb[slot, 1].astype(F32)
        ).astype(BF)

        if before is not None:
            old_array, old_step, valid = before
            pl.when(valid)(lambda: self.z_copy(u - 3, old_array, old_step).wait_send())

        def store():
            self.own[array] = total

        def pass_on():
            self.zs[slot] = total
            self.z_copy(u, array, step).start()

        pl.when(step == 0)(store)
        pl.when(step != 0)(pass_on)

    def finish(self, array):
        total = self.own[array].astype(F32)
        for step in (1, 2, 3):
            self.z_copy(jnp.int32(0), jnp.int32(array), jnp.int32(step)).wait_recv()
            total = total + self.rz[array, step - 1].astype(F32)
        self.own[array] = total.astype(BF)


def layer_kernel(
    len_ref,
    x_hbm,
    cot_hbm,
    out_bias_ref,
    gain1_ref,
    shift1_ref,
    down_bias_ref,
    gain2_ref,
    shift2_ref,
    query_bias_ref,
    value_bias_ref,
    up_bias_ref,
    wq_hbm,
    wk_hbm,
    wv_hbm,
    wo_hbm,
    wu_hbm,
    wd_hbm,
    qkv_full,
    out_full,
    up_full,
    down_full,
    q_hbm,
    k_hbm,
    v_hbm,
    outputs_hbm,
    down_grad,
    up_grad,
    proj_grad,
    acc,
    sums_ref,
    x_seq,
    bias_s,
    bias_all,
    w_s,
    w_out,
    q_s,
    k_s,
    v_s,
    o_s,
    act_s,
    slope_s,
    wide,
    hidden_s,
    low_s,
    inverse_s,
    lse_s,
    d_att,
    kv_temp,
    rows_recv,
    small,
    small_recv,
    z_send,
    z_recv,
    bias_send,
    bias_recv,
    local,
    load,
    save,
    att_load,
    back_load,
    rows_send_sem,
    rows_recv_sem,
    small_ssem,
    small_rsem,
    *rest,
):
    p = Place()
    reduce = Reduce(p, rest[:8], rest[8:20])
    rows, model = acc.shape
    width = q_s.shape[2]
    half_index = lax.rem(p.t, 2)
    seq = lax.div(p.t, 2)
    own_at = pl.multiple_of(half_index * rows, rows)
    other_at = pl.multiple_of((1 - half_index) * rows, rows)
    own_rows, other_rows = pl.ds(own_at, rows), pl.ds(other_at, rows)
    fulls = [qkv_full, out_full, up_full, down_full]
    QKV, OUT, UP, DOWN = range(4)
    spreads = [
        Spread(p, full, rest[20:30], i, (1,) if i in (UP, DOWN) else ())
        for i, full in enumerate(fulls)
    ]
    qkv_cols = pl.ds(0, 3 * width)

    def on(step, at, *actions):
        @pl.when(step == at)
        def _():
            for action in actions:
                action()

    def begin(copies):
        for copy in copies:
            copy.start()

    def end(copies):
        for copy in copies:
            copy.wait()

    x_load = pltpu.make_async_copy(
        x_hbm.at[pl.ds(pl.multiple_of(seq * LEN, LEN), LEN)], x_seq, local.at[0]
    )
    own_loads = [
        pltpu.make_async_copy(w, w_s.at[2, :, :, :, pl.ds(i * width, width)], local.at[1 + i])
        for i, w in enumerate((wq_hbm, wk_hbm, wv_hbm))
    ]
    out_load = pltpu.make_async_copy(wo_hbm, w_out.at[0], local.at[4])
    up_load = pltpu.make_async_copy(wu_hbm, w_s.at[0], local.at[5])
    down_load = pltpu.make_async_copy(wd_hbm, w_s.at[0], local.at[6])
    cot_load = pltpu.make_async_copy(cot_hbm, low_s, local.at[7])
    qkv_save = pltpu.make_async_copy(w_s.at[2, :, :, :, qkv_cols], qkv_full.at[p.t], local.at[8])
    up_save = pltpu.make_async_copy(w_s.at[0], up_full.at[p.t], local.at[9])
    outputs_s = reduce.g.at[1, 0:2]
    outputs_save = pltpu.make_async_copy(outputs_s, outputs_hbm, local.at[10])
    begin(own_loads)
    x_load.start()
    out_load.start()
    up_load.start()
    cot_load.start()
    bias_s[...] = jnp.zeros(bias_s.shape, F32)
    bias_s[0:1, :width] = query_bias_ref[...]
    bias_s[0:1, width : 2 * width] = value_bias_ref[...]
    bias_s[1:2] = up_bias_ref[...]
    bias_all[p.t] = bias_s[...]
    p.greet()

    def z_copies(array, step):
        slot = array * 4 + step
        if array == QKV:
            return [
                remote(
                    w.at[p.quad, p.core],
                    qkv_full.at[p.t, p.quad, p.core, :, pl.ds(i * width, width)],
                    z_send,
                    z_recv,
                    slot if i == 0 else 16 + 4 * (i - 1) + step,
                    p.to_z(step),
                )
                for i, w in enumerate((wq_hbm, wk_hbm, wv_hbm))
            ]
        w = (None, wo_hbm, wu_hbm, wd_hbm)[array]
        place = fulls[array].at[p.t, p.quad, p.core]
        copies = [remote(w.at[p.quad, p.core], place, z_send, z_recv, slot, p.to_z(step))]
        if step in spreads[array].doubled:
            half = w.shape[2] // 2
            for n, quad in enumerate((p.quad_y, p.quad_x)):
                at = pl.ds(n * half, half)
                src = w.at[quad, p.core, at]
                dst = fulls[array].at[p.t, quad, p.core, at]
                extra = 24 + 2 * (array - UP) + n
                copies.append(remote(src, dst, z_send, z_recv, extra, p.to_z(step)))
        return copies

    def bias_copy(step):
        return remote(bias_s, bias_all.at[p.t], bias_send, bias_recv, step, p.to_z(step))

    for step in (1, 2, 3):
        bias_copy(step).start()
    for array in (QKV, OUT, UP, DOWN):
        for step in (1, 2, 3):
            begin(z_copies(array, step))

    def load_copy(array, step):
        if array == QKV:
            dst = w_s.at[2 + step % 2, :, :, :, qkv_cols]
        elif array == OUT:
            dst = w_out.at[step]
        else:
            dst = w_s.at[step]
        src = fulls[array].at[mix(p.t, jnp.int32(step))]
        return pltpu.make_async_copy(src, dst, load.at[array * 4 + step])

    def relay(plan):
        for array, legs in plan:
            spread = spreads[array]
            for leg in legs.split():
                kind, step = leg[0], int(leg[1])
                if kind == "f":
                    for copy in z_copies(array, step):
                        copy.wait_recv()
                    spread.first(step)
                elif kind == "s":
                    spread.second(step)
                elif kind == "t":
                    spread.third(step)
                else:
                    spread.arrived(step)
                    load_copy(array, step).start()

    def passed(step, place):
        plans = {
            (0, "end"): [
                (QKV, "f1 f2 s1 f3 s2"),
                (OUT, "f1"),
                (QKV, "t1"),
                (OUT, "f2 f3"),
                (QKV, "a1 s3"),
            ],
            (1, "mid"): [(QKV, "t2"), (OUT, "s1")],
            (1, "end"): [(OUT, "s2 s3"), (UP, "f1"), (QKV, "a2")],
            (2, "start"): [(QKV, "t3"), (OUT, "t1 t2")],
            (2, "mid"): [(OUT, "t3")],
            (2, "end"): [(QKV, "a3"), (OUT, "a1 a2 a3"), (UP, "f2")],
            (3, "start"): [(UP, "t1 f3")],
            (3, "end"): [(UP, "s2")],
        }
        for (at, where), plan in plans.items():
            if where == place:
                on(step, at, lambda plan=plan: relay(plan))

    def attend_saves(step):
        group, slot = mix(p.t, step), lax.rem(step, 2)
        pairs = ((q_s, q_hbm), (k_s, k_hbm), (v_s, v_hbm))
        return [
            pltpu.make_async_copy(vmem.at[slot], hbm.at[group], save.at[3 * step + i])
            for i, (vmem, hbm) in enumerate(pairs)
        ]

    def attend(step):
        group, slot = mix(p.t, step), lax.rem(step, 2)
        weights = w_s[2 + slot, :, :, :, qkv_cols].reshape(model, 3 * width)
        bias = bias_all[group, 0:1]
        queries = (product(x_seq[own_rows, :], weights[:, :width]) + bias[:, :width]).astype(BF)
        q_s[slot] = (queries.astype(F32) * HD ** (-0.5)).astype(BF)
        k_s[slot] = product(x_seq[...], weights[:, width : 2 * width]).astype(BF)
        v_s[slot] = (
            product(x_seq[...], weights[:, 2 * width :]) + bias[:, width : 2 * width]
        ).astype(BF)
        passed(step, "start")
        length = len_ref[seq]
        key_slot = lax.broadcasted_iota(jnp.int32, (LEN, rows), 0)
        lane = lax.broadcasted_iota(jnp.int32, (rows, PAIR), 1)
        for pair in range(width // PAIR):
            if pair == 1:
                passed(step, "mid")
            cols = slice(pair * PAIR, (pair + 1) * PAIR)
            keys, values, q_pair = k_s[slot, :, cols], v_s[slot, :, cols], q_s[slot, :, cols]
            parts = []
            for head in range(2):
                mine = jnp.where((lane >= HD) == (head == 1), q_pair, jnp.zeros_like(q_pair))
                scores = jnp.where(key_slot < length, product(keys, mine, NT), -1e30)
                top = jnp.max(scores, axis=0, keepdims=True)
                exponent = jnp.exp(scores - top)
                total = jnp.sum(exponent, axis=0, keepdims=True)
                mixed = product(values, exponent.astype(BF), TN)
                parts.append(mixed[head * HD : (head + 1) * HD] * (1.0 / total))
                lse_s[group, pl.ds(pair * 2 + head, 1), :] = top + jnp.log(total)
            o_s[step, :, cols] = jnp.concatenate(parts, axis=0).T.astype(BF)

    x_load.wait()
    end(own_loads)
    qkv_save.start()
    for step in (1, 2, 3):
        bias_copy(step).wait_recv()

    def attend_step(step, carry):
        for i in (1, 2, 3):
            on(step, i, load_copy(QKV, i).wait)
        pl.when(step >= 2)(lambda: end(attend_saves(step - 2)))
        attend(step)
        begin(attend_saves(step))
        on(step, 1, qkv_save.wait)
        passed(step, "end")
        return carry

    lax.fori_loop(0, 4, attend_step, 0)

    out_load.wait()
    for step in (1, 2, 3):
        load_copy(OUT, step).wait()
    acc[...] = x_seq[own_rows, :].astype(F32) + out_bias_ref[...]
    for step in range(4):
        acc[...] += product(o_s[step], w_out[step].reshape(width, model))
    normal1, inverse1 = norm_center(acc[...])
    wide[...] = normal1
    inverse_s[...] = jnp.broadcast_to(inverse1, inverse_s.shape)
    normed1 = normal1 * gain1_ref[...] + shift1_ref[...]
    hidden_s[...] = normed1.astype(BF)
    acc[...] = normed1 + down_bias_ref[...]
    relay([(UP, "a1")])

    def up_step(step, carry):
        on(step, 0, up_load.wait, up_save.start)
        for i in (1, 2, 3):
            on(step, i, load_copy(UP, i).wait)
        upper = product(hidden_s[...], w_s[step].reshape(model, model))
        upper = upper + bias_all[mix(p.t, step), 1:2]
        cdf = 0.5 * (1.0 + lax.erf(upper * 0.7071067811865476))
        act_s[step] = (upper * cdf).astype(BF)
        density = jnp.exp(-0.5 * upper * upper) * 0.3989422804014327
        slope_s[step] = (cdf + upper * density).astype(BF)
        on(step, 0, lambda: relay([(UP, "s3"), (DOWN, "f1")]))
        on(step, 1, up_save.wait, down_load.start)
        on(step, 1, lambda: relay([(UP, "t2"), (DOWN, "f2"), (UP, "t3"), (DOWN, "f3"), (UP, "a2")]))
        on(step, 2, lambda: relay([(UP, "a3"), (DOWN, "t1")]))
        on(step, 3, lambda: relay([(DOWN, "s2 a1")]))
        return carry

    lax.fori_loop(0, 4, up_step, 0)
    for step in (2, 3):
        end(attend_saves(jnp.int32(step)))

    def down_step(step, carry):
        on(step, 0, down_load.wait)
        for i in (1, 2, 3):
            on(step, i, load_copy(DOWN, i).wait)
        acc[...] += product(act_s[step], w_s[step].reshape(model, model))
        on(step, 0, lambda: relay([(DOWN, "s3 t2")]))
        on(step, 1, lambda: relay([(DOWN, "t3 a2")]))
        on(step, 2, lambda: relay([(DOWN, "a3")]))
        return carry

    lax.fori_loop(0, 4, down_step, 0)

    cot_load.wait()
    normal2, inverse2 = norm_center(acc[...])
    outputs = (normal2 * gain2_ref[...] + shift2_ref[...]).astype(BF)
    reduce.g[1, 0:2] = outputs.reshape(2, 2, rows // 4, model)
    outputs_save.start()
    slot_index = half_index * rows + lax.broadcasted_iota(jnp.int32, (rows, 1), 0)
    grad_out = jnp.where(slot_index < len_ref[seq], low_s[...].astype(F32), 0.0)
    d_second = norm_back(grad_out, normal2, inverse2, gain2_ref[...])
    acc[...] = d_second
    low_s[...] = d_second.astype(BF)
    small[0] = jnp.zeros(small.shape[1:], F32)
    small[0, 0:1] = jnp.sum(grad_out * normal2, axis=0, keepdims=True)
    small[0, 1:2] = jnp.sum(grad_out, axis=0, keepdims=True)
    small[0, 2:3] = jnp.sum(d_second, axis=0, keepdims=True)

    grads = (down_grad, up_grad, proj_grad)
    back_spreads = [Spread(p, grad, rest[30:40], i) for i, grad in enumerate(grads)]
    for spread in back_spreads:
        spread.block = lambda step: 0
    B_DOWN, B_UP, B_PROJ = range(3)

    def group_at(i):
        return mix(p.t, 3 - i)

    def att_loads(i):
        g, slot = group_at(i), lax.rem(i, 2)
        pairs = ((q_hbm, q_s), (k_hbm, k_s), (v_hbm, v_s))
        return [
            pltpu.make_async_copy(hbm.at[g], vmem.at[slot], att_load.at[4 * i + n])
            for n, (hbm, vmem) in enumerate(pairs)
        ]

    def proj_load(i):
        slot = lax.rem(i, 2)
        return pltpu.make_async_copy(
            qkv_full.at[group_at(i)], w_s.at[slot, :, :, :, qkv_cols], att_load.at[4 * i + 3]
        )

    def up_again(step):
        return pltpu.make_async_copy(up_full.at[mix(p.t, step)], w_s.at[step], back_load.at[step])

    begin(att_loads(jnp.int32(0)))

    def mlp_order(i):
        return 3 - 2 * lax.rem(i, 2) - lax.div(i, 2)

    def unit_of(u):
        if isinstance(u, int) and u >= 8:
            return jnp.int32(B_PROJ), jnp.int32(11 - u)
        u = jnp.int32(u)
        return lax.rem(u, 2), mlp_order(lax.div(u, 2))

    def fold_core(u):
        reduce.fold_core(jnp.int32(u))

    def fold_corner(u):
        reduce.fold_corner(jnp.int32(u))

    def fold_sides(u):
        array, step = unit_of(u)
        if isinstance(u, int):
            old_array, old_step = unit_of(max(u - 3, 0))
            valid = jnp.logical_and(u >= 3, old_step != 0)
            u = jnp.int32(u)
        else:
            old_array, old_step = unit_of(jnp.maximum(u - 3, 0))
            valid = jnp.logical_and(u >= 3, old_step != 0)
        reduce.fold_sides(u, array, step, (old_array, old_step, valid))

    def tick(u):
        pl.when(u >= 4)(lambda: fold_sides(u - 4))
        pl.when(u >= 1)(lambda: fold_core(u - 1))
        reduce.send(u)
        pl.when(u >= 2)(lambda: fold_corner(u - 2))

    def store_unit(slot, left, right):
        part = model // 4
        for quad in range(4):
            terms = product(left(slice(quad * part, (quad + 1) * part)), right, TN)
            reduce.g[slot, quad] = terms.astype(BF).reshape(2, part // 2, right.shape[1])

    def mlp_step(i, carry):
        step = mlp_order(i)
        u = 2 * i
        reduce.free_g(u)
        store_unit(0, lambda cols: act_s[step, :, cols], low_s[...])
        tick(u)
        d_act = product(low_s[...], w_s[step].reshape(model, model), NT)
        d_up = (d_act * slope_s[step].astype(F32)).astype(BF)
        slope_s[step] = d_up
        up_again(step).start()
        at = pl.ds(6 + mix(p.t, step), 1)
        small[0, at, :] = jnp.sum(d_up.astype(F32), axis=0, keepdims=True)
        reduce.free_g(u + 1)
        on(i, 0, outputs_save.wait)
        store_unit(1, lambda cols: hidden_s[:, cols], slope_s[step])
        tick(u + 1)
        up_again(step).wait()
        acc[...] += product(slope_s[step], w_s[step].reshape(model, model), NT)
        return carry

    lax.fori_loop(0, 4, mlp_step, 0)

    proj_load(jnp.int32(0)).start()
    normal1 = wide[...]
    small[0, 3:4] = jnp.sum(acc[...] * normal1, axis=0, keepdims=True)
    small[0, 4:5] = jnp.sum(acc[...], axis=0, keepdims=True)
    d_first = norm_back(acc[...], normal1, inverse_s[:, 0:1], gain1_ref[...])
    acc[...] = d_first
    low_s[...] = d_first.astype(BF)
    small[0, 5:6] = jnp.sum(d_first, axis=0, keepdims=True)
    d_own, d_other = act_s.at[0], act_s.at[1]

    def attend_back(i):
        slot = lax.rem(i, 2)
        g = group_at(i)
        step = mix(p.t, g)
        length = len_ref[seq]
        d_att[...] = product(low_s[...], w_out[step].reshape(width, model), NT).astype(BF)
        key_slot = lax.broadcasted_iota(jnp.int32, (LEN, rows), 0)
        lane = lax.broadcasted_iota(jnp.int32, (rows, PAIR), 1)
        for pair in range(width // PAIR):
            cols = slice(pair * PAIR, (pair + 1) * PAIR)
            keys, values, queries = k_s[slot, :, cols], v_s[slot, :, cols], q_s[slot, :, cols]
            d_out = d_att[:, cols]
            inner_all = (d_out.astype(F32) * o_s[step, :, cols].astype(F32)).T
            query_parts = []
            for head in range(2):
                mine = (lane >= HD) == (head == 1)
                own_q = jnp.where(mine, queries, jnp.zeros_like(queries))
                own_d = jnp.where(mine, d_out, jnp.zeros_like(d_out))
                inner = jnp.sum(inner_all[head * HD : (head + 1) * HD], axis=0, keepdims=True)
                scores = jnp.where(key_slot < length, product(keys, own_q, NT), -1e30)
                probs = jnp.exp(scores - lse_s[g, pl.ds(pair * 2 + head, 1), :])
                d_probs = product(values, own_d, NT)
                d_scores = (probs * (d_probs - inner) * HD ** (-0.5)).astype(BF)
                d_values = product(probs.astype(BF), own_d)
                d_keys = product(d_scores, own_q) * HD**0.5
                if head == 0:
                    kv_temp[0] = d_keys
                    kv_temp[1] = d_values
                else:
                    kv_temp[0] += d_keys
                    kv_temp[1] += d_values
                query_parts.append(product(keys, d_scores, TN)[head * HD : (head + 1) * HD])
            d_own[:, cols] = jnp.concatenate(query_parts, axis=0).T.astype(BF)
            for n in range(2):
                at = slice((n + 1) * width + pair * PAIR, (n + 1) * width + (pair + 1) * PAIR)
                d_own[:, at] = kv_temp[n, own_rows, :].astype(BF)
                d_other[:, at] = kv_temp[n, other_rows, :].astype(BF)

    def proj_unit(i, u):
        slot = lax.rem(i, 2)
        g = group_at(i)
        qkv, kv = slice(0, 3 * width), slice(width, 3 * width)
        at = pl.ds(10 + g, 1)
        small[0, at, qkv] = jnp.sum(d_own[:, qkv].astype(F32), axis=0, keepdims=True)
        small[0, at, kv] += jnp.sum(d_other[:, kv].astype(F32), axis=0, keepdims=True)
        reduce.core_copy(u - 2).wait_send()
        g_slot = lax.rem(u, 2)
        out_terms = product(o_s[mix(p.t, g)], low_s[...], TN).astype(BF)
        for quad in range(4):
            cols = slice(quad * width, (quad + 1) * width)
            block = (2, width // 2, width)
            x_own, x_other = x_seq[own_rows, cols], x_seq[other_rows, cols]
            queries = product(x_own, d_own[:, :width], TN)
            reduce.g[g_slot, quad, :, :, :width] = queries.astype(BF).reshape(block)
            both = product(x_own, d_own[:, kv], TN) + product(x_other, d_other[:, kv], TN)
            reduce.g[g_slot, quad, :, :, kv] = both.astype(BF).reshape(2, width // 2, 2 * width)
            reduce.g[g_slot, quad, :, :, 3 * width :] = out_terms[:, cols].reshape(block)
        reduce.send(u)
        proj_load(i).wait()
        weights = w_s[slot, :, :, :, qkv_cols].reshape(model, 3 * width)
        acc[...] += product(d_own[:, qkv], weights, NT)
        other = product(d_other[:, kv], weights[:, kv], NT)

        @pl.when(i == 0)
        def _():
            wide[...] = other

        @pl.when(i > 0)
        def _():
            wide[...] += other

    def own_save(array):
        place = grads[array].at[0, p.quad, p.core]
        return pltpu.make_async_copy(reduce.own.at[array], place, local.at[11 + array])

    def start_spread(array):
        reduce.finish(array)
        own_save(array).start()
        back_spreads[array].first(0, reduce.own.at[array])

    def end_spread(array):
        own_save(array).wait()
        back_spreads[array].third(0)

    def att_step(i, carry):
        end(att_loads(i))
        attend_back(i)

        def next_loads():
            begin(att_loads(i + 1))
            proj_load(i + 1).start()

        pl.when(i < 3)(next_loads)

        def passed_back(at):
            fold_sides(4 + at)
            fold_core(7 + at)
            fold_corner(6 + at)
            if at == 3:
                start_spread(B_DOWN)

        for at in range(4):
            on(i, at, lambda at=at: passed_back(at))
        proj_unit(i, i + 8)
        return carry

    lax.fori_loop(0, 4, att_step, 0)
    rows_out = act_s.at[2]
    rows_out[...] = wide[...].astype(BF)

    def rows_copy(part):
        at = pl.ds(part * (rows // 4), rows // 4)
        return remote(
            rows_out.at[at], rows_recv.at[at], rows_send_sem, rows_recv_sem, part, p.to_z(1)
        )

    rows_copy(0).start()
    rows_copy(1).start()
    peers = [p.to_core, p.to_x, p.to_y, p.to_z(1), p.to_z(2)]

    def small_copy(n):
        return remote(small.at[n], small_recv.at[n], small_ssem, small_rsem, n, peers[n])

    def small_next(n):
        small_copy(n).wait_recv()
        small[n + 1] = small[n] + small_recv[n]
        if n < 4:
            small_copy(n + 1).start()

    small_copy(0).start()
    fold_sides(8)
    fold_core(11)
    fold_corner(10)
    back_spreads[B_DOWN].second(0)
    start_spread(B_UP)
    small_next(0)
    fold_sides(9)
    rows_copy(2).start()
    fold_corner(11)
    end_spread(B_DOWN)
    back_spreads[B_UP].second(0)
    small_next(1)
    fold_sides(10)
    rows_copy(3).start()
    small_next(2)
    fold_sides(11)
    start_spread(B_PROJ)
    end_spread(B_UP)
    small_next(3)
    back_spreads[B_PROJ].second(0)
    small_next(4)
    end_spread(B_PROJ)
    sums_ref[...] = small[5]

    for step in (1, 2, 3):
        bias_copy(step).wait_send()
        for array in range(4):
            for copy in z_copies(array, step):
                copy.wait_send()
            spreads[array].finish(step)
    for part in range(4):
        rows_copy(part).wait()
    acc[...] += rows_recv[...].astype(F32)
    for u in (10, 11):
        reduce.core_copy(jnp.int32(u)).wait_send()
    for u in (9, 10, 11):
        for copy in reduce.side_copies(jnp.int32(u)) + reduce.corner_copies(jnp.int32(u)):
            copy.wait_send()
    for u in (9, 10):
        array, step = unit_of(u)
        reduce.z_copy(jnp.int32(u), array, step).wait_send()
    for n in range(5):
        small_copy(n).wait_send()
    for spread in back_spreads:
        spread.arrived(0)
        spread.finish(0)


def run_layer(lengths, x, cot, vectors, wq, wk, wv, wo, wu, wd):
    T = lax.axis_size("tensor")
    model = x.shape[1]
    rows = x.shape[0] // T
    width = wo.shape[0]
    piece = model // GROUP

    def pieces(w):
        return w.reshape(4, 2, w.shape[0] // GROUP, w.shape[1])

    def out(*shape, dtype=BF):
        return jax.ShapeDtypeStruct(shape, dtype)

    anyw = pl.BlockSpec(memory_space=pl.ANY)
    vmem = pl.BlockSpec(memory_space=pltpu.VMEM)
    smem = pl.BlockSpec(memory_space=pltpu.SMEM)
    dma = pltpu.SemaphoreType.DMA
    outs = [
        out(T, 4, 2, piece, 3 * width),
        out(T, 4, 2, width // GROUP, model),
        out(T, 4, 2, piece, model),
        out(T, 4, 2, piece, model),
        out(T, rows, width),
        out(T, LEN, width),
        out(T, LEN, width),
        out(2, 2, rows // 4, model),
        *[out(1, 4, 2, piece, model)] * 3,
        out(rows, model, dtype=F32),
        out(16, model, dtype=F32),
    ]
    return pl.pallas_call(
        layer_kernel,
        in_specs=[smem, anyw, anyw] + [vmem] * 9 + [anyw] * 6,
        out_specs=[anyw] * 11 + [vmem] * 2,
        out_shape=outs,
        scratch_shapes=[
            pltpu.VMEM((LEN, model), BF),
            pltpu.VMEM((8, model), F32),
            pltpu.VMEM((T, 8, model), F32),
            pltpu.VMEM((4, 4, 2, piece, model), BF),
            pltpu.VMEM((T, 4, 2, width // GROUP, model), BF),
            pltpu.VMEM((2, rows, width), BF),
            pltpu.VMEM((2, LEN, width), BF),
            pltpu.VMEM((2, LEN, width), BF),
            pltpu.VMEM((T, rows, width), BF),
            pltpu.VMEM((T, rows, model), BF),
            pltpu.VMEM((T, rows, model), BF),
            pltpu.VMEM((rows, model), F32),
            pltpu.VMEM((rows, model), BF),
            pltpu.VMEM((rows, model), BF),
            pltpu.VMEM((rows, 128), F32),
            pltpu.VMEM((T, 8, rows), F32),
            pltpu.VMEM((rows, width), BF),
            pltpu.VMEM((2, LEN, PAIR), F32),
            pltpu.VMEM((rows, model), BF),
            pltpu.VMEM((6, 16, model), F32),
            pltpu.VMEM((5, 16, model), F32),
            dma((28,)),
            dma((28,)),
            dma((4,)),
            dma((4,)),
            dma((14,)),
            dma((16,)),
            dma((12,)),
            dma((16,)),
            dma((4,)),
            dma((4,)),
            dma((4,)),
            dma((5,)),
            dma((5,)),
            *Reduce.scratch(piece, model, 3),
            *Reduce.semaphores(12),
            *Spread.scratch(4),
            *Spread.scratch(3),
        ],
        compiler_params=pltpu.CompilerParams(
            collective_id=0, has_side_effects=True, vmem_limit_bytes=VMEM_LIMIT
        ),
        cost_estimate=pl.CostEstimate(
            flops=100 * 10**9, bytes_accessed=120 << 20, transcendentals=24 << 20
        ),
        name="layer",
    )(
        lengths,
        x,
        cot,
        *[v.reshape(1, -1) for v in vectors],
        pieces(wq),
        pieces(wk),
        pieces(wv),
        pieces(wo),
        pieces(wu),
        pieces(wd),
    )


def results_kernel(
    outputs_in,
    down_in,
    up_in,
    proj_in,
    input_in,
    sums_in,
    outputs_ref,
    input_ref,
    query_ref,
    key_ref,
    value_ref,
    query_bias_ref,
    value_bias_ref,
    out_ref,
    out_bias_ref,
    gain1_ref,
    shift1_ref,
    up_ref,
    up_bias_ref,
    down_ref,
    down_bias_ref,
    gain2_ref,
    shift2_ref,
):
    t = lax.axis_index("tensor")
    width = query_ref.shape[1]
    outputs_ref[...] = outputs_in[...]
    input_ref[...] = input_in[...]
    down_ref[...] = down_in[...].astype(F32)
    up_ref[...] = up_in[...].astype(F32)
    for n, ref in enumerate((query_ref, key_ref, value_ref, out_ref)):
        ref[...] = proj_in[:, n * width : (n + 1) * width].astype(F32)
    rows = (gain2_ref, shift2_ref, down_bias_ref, gain1_ref, shift1_ref, out_bias_ref)
    for n, ref in enumerate(rows):
        ref[...] = sums_in[n : n + 1]
    up_bias_ref[...] = sums_in[pl.ds(6 + t, 1), :]
    proj = sums_in[pl.ds(10 + t, 1), :]
    query_bias_ref[...] = proj[:, :width]
    value_bias_ref[...] = proj[:, 2 * width : 3 * width]


def run_results(outputs, down, up, proj, input_grad, sums, width):
    rows, model = outputs.shape
    steps = 4
    tall = lambda count, cols=model: pl.BlockSpec((count // steps, cols), lambda i: (i, 0))
    row = lambda cols=model: pl.BlockSpec((1, cols), lambda i: (0, 0))
    out = lambda count, cols=model, dtype=F32: jax.ShapeDtypeStruct((count, cols), dtype)
    whole = pl.BlockSpec(sums.shape, lambda i: (0, 0))
    outs = [
        (out(rows, dtype=BF), tall(rows)),
        (out(rows), tall(rows)),
        *[(out(model, width), tall(model, width))] * 3,
        *[(out(1, width), row(width))] * 2,
        (out(width), pl.BlockSpec((width, model // steps), lambda i: (0, i))),
        *[(out(1), row())] * 3,
        (out(model), tall(model)),
        (out(1), row()),
        (out(model), tall(model)),
        *[(out(1), row())] * 3,
    ]
    return pl.pallas_call(
        results_kernel,
        grid=(steps,),
        in_specs=[tall(rows), tall(model), tall(model), tall(model), tall(rows), whole],
        out_specs=[spec for _, spec in outs],
        out_shape=[shape for shape, _ in outs],
        compiler_params=pltpu.CompilerParams(vmem_limit_bytes=VMEM_LIMIT),
        name="results",
    )(outputs, down, up, proj, input_grad, sums)


def on_device(
    inputs,
    cotangent,
    lengths,
    query_weight,
    key_weight,
    value_weight,
    query_bias,
    value_bias,
    out_weight,
    out_bias,
    norm1_gain,
    norm1_bias,
    up_weight,
    up_bias,
    down_weight,
    down_bias,
    norm2_gain,
    norm2_bias,
):
    model = inputs.shape[1]
    rows = cotangent.shape[0]
    width = out_weight.shape[0]
    results = run_layer(
        lengths,
        inputs,
        cotangent,
        (
            out_bias,
            norm1_gain,
            norm1_bias,
            down_bias,
            norm2_gain,
            norm2_bias,
            query_bias,
            value_bias,
            up_bias,
        ),
        query_weight,
        key_weight,
        value_weight,
        out_weight,
        up_weight,
        down_weight,
    )
    outputs, down_grad, up_grad, proj_grad, input_grad, sums = results[7:]
    grads = [g.reshape(model, model) for g in (down_grad, up_grad, proj_grad)]
    size = lax.axis_size("dp")
    if size > GROUP:
        grads = [g.astype(F32) for g in grads]
        groups = [list(range(first, size, GROUP)) for first in range(GROUP)]
        *grads, sums = lax.psum((*grads, sums), "dp", axis_index_groups=groups)
    done = run_results(outputs.reshape(rows, model), *grads, input_grad, sums, width)
    return tuple(v.reshape(-1) if v.shape[0] == 1 else v for v in done)


def solution(mesh):
    rows = P(("dp", "tensor"), None)
    by_col = P(None, "tensor")
    by_row = P("tensor", None)
    split = P("tensor")
    whole = P()
    return jax.shard_map(
        on_device,
        mesh=mesh,
        in_specs=(
            P("dp", None),
            rows,
            P("dp"),
            by_col,
            by_col,
            by_col,
            split,
            split,
            by_row,
            whole,
            whole,
            whole,
            by_col,
            split,
            by_row,
            whole,
            whole,
            whole,
        ),
        out_specs=(
            rows,
            rows,
            by_col,
            by_col,
            by_col,
            split,
            split,
            by_row,
            whole,
            whole,
            whole,
            by_col,
            split,
            by_row,
            whole,
            whole,
            whole,
        ),
        check_vma=False,
    )
```
